256 devices in a mesh: inst: 32 (over y, x, z_lo), tp: 8 (over z_hi, core).
Axes of the slice: x: 4, y: 4, z: 8 (z_hi: 4, z_lo: 2; z = z_hi * 2 + z_lo), core: 2. Of those that a mesh axis runs over, the one named last changes fastest.
Arguments:
- pool: bfloat16 [1536, 2, 128, 1024], P('inst', None, None, 'tp'), may hold values from -8 to 8
- page_table: int32 [1024, 2], P('inst'), may hold values from 0 to 47, as said below
- lengths: int32 [1024], P('inst'), may hold values from 1 to 253
- targets: int32 [1024], P('inst'), may hold values from 0 to 31, as said below
- migrating: int32 [1024], P('inst'), may hold values 0 or 1
- queries_src: bfloat16 [1024, 2, 4096], P('inst', None, 'tp'), may hold values from -6 to 6
- new_rows: bfloat16 [1024, 2, 2, 1024], P('inst', None, None, 'tp'), may hold values from -6 to 6
- queries_dst: bfloat16 [1024, 4096], P('inst', 'tp'), may hold values from -6 to 6
- rows_dst: bfloat16 [1024, 2, 1024], P('inst', None, 'tp'), may hold values from -6 to 6
- w_out: bfloat16 [4096, 4096], P('tp'), may hold values from -1 to 1
Outputs:
- src_out: bfloat16 [1024, 2, 4096], P('inst')
- dest_cache: bfloat16 [1024, 2, 2, 128, 1024], P('inst', None, None, None, 'tp')
- dst_out: bfloat16 [1024, 4096], P('inst')
The draws below stay inside these ranges and needn't reach their ends.
Inputs may be any that keep to these rules, and one draw needn't show every extreme that they name: `page_table`: the first ceil(lengths / 128) entries of a request name pages of its instance's pool that no other request names; the pages of an instance's 32 requests fill its 48 pool pages exactly; later entries are valid page numbers. `targets`: every destination is named by exactly 1 of the 32 requests of each source instance.
All inputs are finite; a program needn't handle non-finite values. No bound on the sum of `migrating` on one device may be relied on, other than what follows from the above.
Results may differ from the reference program's by a relative error of at most 0.0058.
Values may be sent and summed in bfloat16 or wider, within the bound.
A program may use at most 128 MiB of HBM per device.

```python
import math
from functools import reduce
import jax
import jax.numpy as jnp
from jax import lax

D = 4096
HD = 128
KVH = 8
G = 4
PAGE = 128
PMAX = 2
R = 32
PAIR = 1
NPAGE = 48
REQS = 1024
QW = 4096
KW = 1024
N_INST = 32


def request_layout(key):
    base = jax.random.fold_in(key, 101)
    streams = jax.random.split(base, 4)
    half = R // 2
    first = jax.random.randint(streams[0], (N_INST, half), PMAX - 1, PMAX + 1)
    first = first.at[:, 0].set(PMAX)
    counts = jnp.concatenate([first, 2 * PMAX - 1 - first], axis=1)
    tail = jax.random.randint(streams[1], (N_INST, R), 1, PAGE + 1)
    tail = jnp.where(counts == PMAX, jnp.minimum(tail, PAGE - 3), tail)
    tail = tail.at[:, 0].set(PAGE - 3)
    spans = (counts - 1) * PAGE + tail
    shuffle = jax.vmap(lambda piece: jax.random.permutation(piece, R))(jax.random.split(streams[2], N_INST))
    counts = jnp.take_along_axis(counts, shuffle, axis=1)
    spans = jnp.take_along_axis(spans, shuffle, axis=1)
    frames = jax.vmap(lambda piece: jax.random.permutation(piece, NPAGE))(jax.random.split(streams[3], N_INST))
    offsets = jnp.cumsum(counts, axis=1) - counts
    index = (offsets[:, :, None] + jnp.arange(PMAX)[None, None, :]) % NPAGE
    table = jnp.take_along_axis(frames, index.reshape(N_INST, R * PMAX), axis=1)
    return (spans.reshape(N_INST * R).astype(jnp.int32), table.reshape(N_INST * R, PMAX).astype(jnp.int32))


def draw_lengths(key, part):
    return request_layout(key)[0]


def draw_page_table(key, part):
    return request_layout(key)[1]


def draw_targets(key, part):
    key = jax.random.fold_in(key, 7)
    shuffle = jax.vmap(lambda piece: jax.random.permutation(piece, R))(jax.random.split(key, N_INST))
    return (shuffle // PAIR).reshape(N_INST * R).astype(jnp.int32)


def draw_pool(key, part):
    key = jax.random.fold_in(key, 3)
    shape = (N_INST * NPAGE, 2, PAGE, KVH * HD)
    cells = jnp.clip(jax.random.normal(key, shape, jnp.float32), -6.0, 6.0)
    return cells.astype(jnp.bfloat16)


def draw_queries_src(key, part):
    key = jax.random.fold_in(key, 5)
    count = N_INST * R
    cells = jnp.clip(jax.random.normal(key, (count, 2, KVH, G, HD), jnp.float32), -6.0, 6.0)
    return cells.reshape(count, 2, KVH * G * HD).astype(jnp.bfloat16)


def draw_queries_dst(key, part):
    key = jax.random.fold_in(key, 9)
    count = N_INST * R
    cells = jnp.clip(jax.random.normal(key, (count, 1, KVH, G, HD), jnp.float32), -6.0, 6.0)
    return cells.reshape(count, KVH * G * HD).astype(jnp.bfloat16)


def touch_ends(result, key, least, high):
    extent = result.shape
    index_at = [jax.random.randint(jax.random.fold_in(key, axis), (), 0, extent[axis]) for axis in range(len(extent))]
    result = result.at[tuple(index_at)].set(least)
    longest = extent.index(max(extent))
    index_at[longest] = (index_at[longest] + 1) % extent[longest]
    return result.at[tuple(index_at)].set(high)


def shard_levels(own_key, shape, cuts, smallest, largest):
    factor_of, own = 1.0, jax.random.fold_in(own_key, 6)
    for axis_at, shards_of in cuts:
        draws = jnp.exp(jax.random.uniform(jax.random.fold_in(own, axis_at), (shards_of,), jnp.float32, smallest / len(cuts), largest / len(cuts)))
        factor_of = factor_of * jnp.repeat(draws, shape[axis_at] // shards_of).reshape([-1 if axis == axis_at else 1 for axis in range(len(shape))])
    return factor_of


def scatter_about(rng, dims, scale, reach, cuts=(), kind=jnp.bfloat16):
    level = shard_levels(rng, dims, cuts, -0.22, 0.18) if cuts else 1.0
    entries = jax.random.normal(rng, dims, jnp.float32) * scale * level
    return jnp.minimum(jnp.maximum(entries, -reach), reach).astype(kind)


def setup_inputs(seed: int = 0) -> dict:
    splits = jax.random.split(jax.random.key(seed), 11)
    return {
        "pool": draw_pool(jax.random.fold_in(splits[10], 71), 0),
        "page_table": draw_page_table(jax.random.fold_in(splits[10], 71), 0),
        "lengths": draw_lengths(jax.random.fold_in(splits[10], 71), 0),
        "targets": draw_targets(jax.random.fold_in(splits[10], 71), 0),
        "migrating": touch_ends((jax.random.randint(splits[4], (REQS,), 0, 8) < 7).astype(jnp.int32), jax.random.fold_in(splits[4], 1), 0, 1),
        "queries_src": draw_queries_src(jax.random.fold_in(splits[10], 71), 0),
        "new_rows": scatter_about(splits[6], (REQS, 2, 2, KW), 1.0, 6.0, ((0, 32), (3, 8))),
        "queries_dst": draw_queries_dst(jax.random.fold_in(splits[10], 71), 0),
        "rows_dst": scatter_about(splits[8], (REQS, 2, KW), 1.0, 6.0, ((0, 32), (2, 8))),
        "w_out": scatter_about(splits[9], (QW, D), (KVH * G) ** -0.5, 1.0, ((0, 8),)),
    }


masked_score = -1e+30

def attend(query_heads, blocks):
    scale = 1.0 / math.sqrt(query_heads.shape[-1])
    wide_query = query_heads.astype(jnp.float32)
    scored = []
    for block_keys, block_values, block_keep in blocks:
        raw_scores = jnp.einsum('bthge,bshe->bthgs', wide_query, block_keys.astype(jnp.float32)) * scale
        scored.append(jnp.where(block_keep[:, :, None, None, :], raw_scores, masked_score))
    highest = reduce(jnp.maximum, [lax.optimization_barrier(jnp.max(entry, axis=-1, keepdims=True)) for entry in scored])
    powers = [jnp.exp(entry - highest) for entry in scored]
    totals = reduce(jnp.add, [lax.optimization_barrier(jnp.sum(entry, axis=-1, keepdims=True)) for entry in powers])
    mixed = jnp.zeros(query_heads.shape, jnp.float32)
    for weight_block, block in zip(powers, blocks):
        weights = (weight_block / totals).astype(jnp.bfloat16)
        mixed = mixed + jnp.einsum('bthgs,bshe->bthge', weights.astype(jnp.float32), block[1].astype(jnp.float32))
    return mixed.astype(jnp.bfloat16)

def reference(pool, page_table, lengths, targets, migrating, queries_src, new_rows, queries_dst, rows_dst, w_out):
    span = PMAX * PAGE
    kv_width = KVH * HD
    position = jnp.arange(span, dtype=jnp.int32)
    page_grid = jnp.arange(PMAX, dtype=jnp.int32)[:, None] * PAGE + jnp.arange(PAGE, dtype=jnp.int32)[None, :]
    ordinal = jnp.arange(R, dtype=jnp.int32)
    pools = pool.reshape(N_INST, NPAGE, 2, PAGE, kv_width)
    fresh_keep = (jnp.arange(2)[None, :] <= jnp.arange(2)[:, None])[None]
    zero_value = jnp.zeros((), jnp.bfloat16)

    def source_side(source):
        start = source * R
        table = lax.dynamic_slice_in_dim(page_table, start, R, 0).astype(jnp.int32)
        local_len = lax.dynamic_slice_in_dim(lengths, start, R, 0)
        local_target = lax.dynamic_slice_in_dim(targets, start, R, 0)
        local_flag = lax.dynamic_slice_in_dim(migrating, start, R, 0)
        local_query = lax.dynamic_slice_in_dim(queries_src, start, R, 0)
        local_rows = lax.dynamic_slice_in_dim(new_rows, start, R, 0)
        view = pools[source][table]
        old_keys = view[:, :, 0].reshape(R, span, KVH, HD)
        old_values = view[:, :, 1].reshape(R, span, KVH, HD)
        keep_old = (position[None, :] < local_len[:, None])[:, None, :]
        fresh_keys = local_rows[:, :, 0].reshape(R, 2, KVH, HD)
        fresh_values = local_rows[:, :, 1].reshape(R, 2, KVH, HD)
        query_heads = local_query.reshape(R, 2, KVH, G, HD)
        attended = attend(query_heads, [(old_keys, old_values, keep_old), (fresh_keys, fresh_values, fresh_keep)])
        out_rows = jnp.dot(attended.reshape(R * 2, KVH * G * HD), w_out, preferred_element_type=jnp.float32)
        out_rows = out_rows.astype(jnp.bfloat16).reshape(R, 2, D)
        same_target = local_target[:, None] == local_target[None, :]
        rank_of = lax.optimization_barrier(jnp.sum((same_target & (ordinal[None, :] < ordinal[:, None])).astype(jnp.int32), axis=1)).astype(jnp.int32)
        slot_of = (local_target * PAIR + rank_of).astype(jnp.int32)
        inverse = lax.optimization_barrier(jnp.sum(jnp.where(slot_of[:, None] == ordinal[None, :], ordinal[:, None], 0), axis=0)).astype(jnp.int32)
        moving = local_flag == 1
        held = moving[:, None, None] & (page_grid[None] < local_len[:, None, None])
        outgoing = jnp.where(held[:, :, None, :, None], view, zero_value)[inverse]
        fresh_out = jnp.where(moving[:, None, None, None], local_rows, zero_value)[inverse]
        return (out_rows, outgoing, fresh_out, local_len[inverse], local_flag[inverse])
    src_rows, sent, fresh_sent, len_sent, flag_sent = lax.map(source_side, jnp.arange(N_INST, dtype=jnp.int32))
    sent = sent.reshape(N_INST, N_INST, PAIR, PMAX, 2, PAGE, kv_width)
    fresh_sent = fresh_sent.reshape(N_INST, N_INST, PAIR, 2, 2, kv_width)
    len_sent = len_sent.reshape(N_INST, N_INST, PAIR)
    flag_sent = flag_sent.reshape(N_INST, N_INST, PAIR)

    def dest_side(dest):
        arrived = lax.dynamic_index_in_dim(sent, dest, 1, keepdims=False).reshape(R, PMAX, 2, PAGE, kv_width)
        fresh_in = lax.dynamic_index_in_dim(fresh_sent, dest, 1, keepdims=False).reshape(R, 2, 2, kv_width)
        len_in = lax.dynamic_index_in_dim(len_sent, dest, 1, keepdims=False).reshape(R)
        flag_in = lax.dynamic_index_in_dim(flag_sent, dest, 1, keepdims=False).reshape(R)
        own_rows = lax.dynamic_slice_in_dim(rows_dst, dest * R, R, 0)
        own_query = lax.dynamic_slice_in_dim(queries_dst, dest * R, R, 0)
        own_rows = jnp.where((flag_in == 1)[:, None, None], own_rows, zero_value)
        offset = (page_grid[None] - len_in[:, None, None])[:, :, None, :, None]
        filled = jnp.where(offset == 0, fresh_in[:, 0][:, None, :, None, :], arrived)
        filled = jnp.where(offset == 1, fresh_in[:, 1][:, None, :, None, :], filled)
        filled = jnp.where(offset == 2, own_rows[:, None, :, None, :], filled)
        dst_keys = filled[:, :, 0].reshape(R, span, KVH, HD)
        dst_values = filled[:, :, 1].reshape(R, span, KVH, HD)
        keep_new = (position[None, :] < (len_in + 3)[:, None])[:, None, :]
        query_heads = own_query.reshape(R, 1, KVH, G, HD)
        attended = attend(query_heads, [(dst_keys, dst_values, keep_new)])
        attended = jnp.where((flag_in == 1)[:, None, None, None, None], attended, zero_value)
        out_rows = jnp.dot(attended.reshape(R, KVH * G * HD), w_out, preferred_element_type=jnp.float32)
        return (filled, out_rows.astype(jnp.bfloat16))
    dest_cache, dst_rows = lax.map(dest_side, jnp.arange(N_INST, dtype=jnp.int32))
    src_out = src_rows.reshape(N_INST * R, 2, D)
    dest_cache = dest_cache.reshape(N_INST * R, PMAX, 2, PAGE, kv_width)
    dst_out = dst_rows.reshape(N_INST * R, D)
    return (src_out, dest_cache, dst_out)
```

```python
import functools
import math

import jax
import jax.numpy as jnp
from jax import lax
from jax.experimental import pallas as pl
from jax.experimental.pallas import tpu as pltpu
from jax.sharding import PartitionSpec as P

MESH = pl.DeviceIdType.MESH
BF16 = jnp.bfloat16
F32 = jnp.float32
NEG = -1e30
HEAD = 128
PAGE = 128
GROUPS = 4
MIX = 11


def xor(a, b, bits):
    total = 0
    for bit in range(bits):
        weight = 2**bit
        u, v = (a // weight) % 2, (b // weight) % 2
        total = total + (u + v - 2 * u * v) * weight
    return total


def order(k, n):
    if n != 32:
        return (k * MIX) % n
    late = k // 16
    spot = (k - 16 * late) % 8
    turn = (k - 16 * late) // 8
    hop0 = (k % 3 + 1) // 2
    hop1 = 1 - (spot % 3 + 1) // 2
    hop = (1 - late) * hop0 + late * hop1
    cross0 = k - k // 3 - 1
    cross1 = 10 + 3 * turn + spot // 3
    plane0 = k // 3
    plane1 = 6 + 5 * turn + spot - spot // 3 - 1
    count = hop * ((1 - late) * cross0 + late * cross1)
    count = count + (1 - hop) * ((1 - late) * plane0 + late * plane1)
    return ((count * MIX) % 16) * 2 + hop


def kernel(
    n,
    tp_size,
    lens,
    tgts,
    mig,
    table,
    qsrc,
    fresh,
    qdst,
    rdst,
    pool_hbm,
    w_hbm,
    s_full,
    cache_out,
    d_full,
    pool,
    w,
    send,
    arr,
    qs,
    qd,
    att_s,
    att_d,
    s_half,
    s_half_in,
    s_pair,
    s_rs,
    s_rs_in,
    d_half,
    d_half_in,
    d_pair,
    d_rs,
    d_rs_in,
    load_sem,
    send_sem,
    recv_sem,
    half_sem,
    rs_sem,
    ag_sem,
    fwd_sem,
):
    me = lax.axis_index("inst")
    tp = lax.axis_index("tp")
    core = tp % 2
    hi = tp // 2
    his = tp_size // 2
    mate = tp + 1 - 2 * core
    bits = n.bit_length() - 1
    scale = 1.0 / math.sqrt(HEAD)
    cols = w.shape[1] // tp_size

    def peer_hi(step):
        return ((hi + step) % his) * 2 + core

    def partner(k):
        return xor(me, order(k, n), bits)

    barrier = pltpu.get_barrier_semaphore()

    def greet(k, _):
        pl.semaphore_signal(
            barrier, inc=1, device_id=(xor(me, k, bits), tp), device_id_type=MESH
        )
        return 0

    lax.fori_loop(1, n, greet, 0)
    pl.semaphore_signal(barrier, inc=1, device_id=(me, mate), device_id_type=MESH)
    for step in range(1, his):
        pl.semaphore_signal(barrier, inc=1, device_id=(me, peer_hi(step)), device_id_type=MESH)

    load_pool = pltpu.make_async_copy(pool_hbm, pool, load_sem.at[0])
    load_w = pltpu.make_async_copy(w_hbm, w, load_sem.at[1])
    load_pool.start()
    load_w.start()

    row = lax.broadcasted_iota(jnp.int32, (PAGE, HEAD), 0).astype(F32).astype(BF16)
    last = row == jnp.asarray(PAGE - 1, BF16)
    zero = jnp.zeros((PAGE, HEAD), BF16)

    def splat(value):
        return jnp.full((1, HEAD), value, F32)

    def move(k):
        peer = partner(k)
        return pltpu.make_async_remote_copy(
            src_ref=send.at[peer],
            dst_ref=arr.at[me],
            send_sem=send_sem.at[k],
            recv_sem=recv_sem.at[k],
            device_id=(peer, tp),
            device_id_type=MESH,
        )

    def arrive(k):
        peer = partner(k)
        return pltpu.make_async_remote_copy(
            src_ref=send.at[peer],
            dst_ref=arr.at[peer],
            send_sem=send_sem.at[k],
            recv_sem=recv_sem.at[k],
            device_id=(peer, tp),
            device_id_type=MESH,
        )

    def pack(k, ref):
        slot = partner(k)
        request = jnp.int32(0)
        for j in range(n):
            request = jnp.where(tgts[j] == slot, j, request)
        length = lens[request].astype(F32)
        flag = mig[request].astype(F32)
        rows_new = fresh[request].astype(F32)
        for p in range(2):
            at = splat(length - p * PAGE).astype(BF16)
            next_at = splat(length - p * PAGE + 1.0).astype(BF16)
            keep = row < at
            first = row == at
            second = row == next_at
            for c in range(2):
                page = pool[table[p, request], c]
                new0 = rows_new[0, c : c + 1].astype(BF16)
                new1 = rows_new[1, c : c + 1].astype(BF16)
                block = jnp.where(keep, page, zero)
                block = jnp.where(first, new0, block)
                block = jnp.where(second, new1, block)
                if p == 1:
                    note = splat(length if c == 0 else flag).astype(BF16)
                    block = jnp.where(last, note, block)
                ref[slot, p, c] = block

    load_pool.wait()
    pl.semaphore_wait(barrier, n - 1 + his)

    def send_step(k, _):
        pack(k, send)
        move(k).start()
        return 0

    batch = min(4, n)
    ahead = min(4 * batch, n)
    lax.fori_loop(1, ahead, send_step, 0)
    pack(0, send)
    arr[me] = send[me]

    def pack_step(k, _):
        pack(k, send)
        return 0

    lax.fori_loop(ahead, n, pack_step, 0)

    q_wide = qsrc[...].astype(F32)
    for g in range(GROUPS):
        lanes = slice(g * HEAD, (g + 1) * HEAD)
        for t in range(2):
            qs[:, 2 * g + t, :] = q_wide[:, t, lanes]
        qd[:, g, :] = qdst[:, lanes].astype(F32)

    def dot_t(a, b):
        return lax.dot_general(a, b, (((1,), (1,)), ((), ())), preferred_element_type=F32)

    def dot(a, b):
        return jnp.dot(a, b, preferred_element_type=F32)

    def soft(s0, s1):
        top = jnp.maximum(
            jnp.max(s0, axis=1, keepdims=True), jnp.max(s1, axis=1, keepdims=True)
        )
        e0, e1 = jnp.exp(s0 - top), jnp.exp(s1 - top)
        total = jnp.sum(e0, axis=1, keepdims=True) + jnp.sum(e1, axis=1, keepdims=True)
        return (e0 / total).astype(BF16), (e1 / total).astype(BF16)

    wide = min(8, n)
    lane8 = lax.broadcasted_iota(jnp.int32, (8, HEAD), 1)
    step8 = lax.broadcasted_iota(jnp.int32, (8, HEAD), 0) % 2

    def src_step(b, _):
        parts0, parts1 = [], []
        for i in range(wide):
            request = b * wide + i
            slot = tgts[request]
            query = qs[request].astype(BF16)
            bound = lens[request] + 1 + step8
            s0 = dot_t(query, send[slot, 0, 0]) * scale
            s1 = dot_t(query, send[slot, 1, 0]) * scale
            parts0.append(jnp.where(lane8 < bound, s0, NEG))
            parts1.append(jnp.where(lane8 + PAGE < bound, s1, NEG))
        w0, w1 = soft(jnp.concatenate(parts0, axis=0), jnp.concatenate(parts1, axis=0))
        for i in range(wide):
            request = b * wide + i
            slot = tgts[request]
            rows = slice(8 * i, 8 * i + 8)
            value1 = jnp.where(last, zero, send[slot, 1, 1])
            mixed = dot(w0[rows], send[slot, 0, 1]) + dot(w1[rows], value1)
            for g in range(GROUPS):
                att_s[g, pl.ds(2 * request, 2), :] = mixed[2 * g : 2 * g + 2]
        return 0

    lax.fori_loop(0, n // wide, src_step, 0)

    def remote(src, dst, sems, index, target):
        return pltpu.make_async_remote_copy(
            src_ref=src,
            dst_ref=dst,
            send_sem=sems.at[2 * index],
            recv_sem=sems.at[2 * index + 1],
            device_id=(me, target),
            device_id_type=MESH,
        )

    def block_cols(index):
        return pl.ds(pl.multiple_of(index * cols, cols), cols)

    def tail(part, att, half, half_in, pair, rs, rs_in, full):
        a = jnp.concatenate([att[g].astype(BF16) for g in range(GROUPS)], axis=1)

        def part_full(index):
            where = block_cols(index)
            return full.at[(slice(None),) * (len(full.shape) - 1) + (where,)]

        swap = remote(half, half_in, half_sem, part, mate)
        scatter = [
            remote(rs.at[step], rs_in.at[step], rs_sem, part * his + step, peer_hi(step))
            for step in range(1, his)
        ]
        mine = part_full(tp)
        gather = [
            remote(mine, mine, ag_sem, part * his + step, peer_hi(step))
            for step in range(1, his)
        ]
        landed = [
            remote(
                mine,
                part_full(((hi + his - step) % his) * 2 + core),
                ag_sem,
                part * his + step,
                peer_hi(step),
            )
            for step in range(1, his)
        ]
        forward = []
        received = []
        for step in range(his):
            owner = ((hi + his - step) % his) * 2
            have, want = part_full(owner + core), part_full(owner + 1 - core)
            forward.append(remote(have, have, fwd_sem, part * his + step, mate))
            received.append(remote(have, want, fwd_sem, part * his + step, mate))

        def one():
            for step in range(his):
                z = (hi + step) % his
                half[step] = dot(a, w[:, block_cols(z * 2 + 1 - core)]).astype(BF16)
            swap.start()
            for step in range(his):
                z = (hi + step) % his
                pair[step] = dot(a, w[:, block_cols(z * 2 + core)])

        def two():
            swap.wait()
            for step in range(1, his):
                rs[step] = (pair[step] + half_in[step].astype(F32)).astype(BF16)
                scatter[step - 1].start()
            pair[0] = pair[0] + half_in[0].astype(F32)

        def three():
            for copy in scatter:
                copy.wait()
            total = pair[0]
            for step in range(1, his):
                total = total + rs_in[step].astype(F32)
            if len(full.shape) == 3:
                total = total.reshape(full.shape[:2] + (cols,))
            mine[...] = total.astype(BF16)
            for copy in gather:
                copy.start()
            forward[0].start()

        def four():
            for step in range(1, his):
                landed[step - 1].wait_recv()
                forward[step].start()
            for step in range(his):
                received[step].wait_recv()

        def five():
            for copy in gather:
                copy.wait_send()
            for copy in forward:
                copy.wait_send()

        return one, two, three, four, five

    load_w.wait()
    src_tail = tail(0, att_s, s_half, s_half_in, s_pair, s_rs, s_rs_in, s_full)
    src_tail[0]()

    lane4 = lax.broadcasted_iota(jnp.int32, (GROUPS, HEAD), 1).astype(F32)

    def dst_step(b, _):
        slots, parts0, parts1, values = [], [], [], []
        for i in range(batch):
            k = b * batch + i

            @pl.when(k > 0)
            def _():
                move(k).wait_send()

            @pl.when(k + ahead < n)
            def _():
                move(k + ahead).start()

        for i in range(batch):
            k = b * batch + i
            slot = partner(k)
            slots.append(slot)

            @pl.when(k > 0)
            def _():
                arrive(k).wait_recv()

            length = arr[slot, 1, 0][PAGE - 1 :].astype(F32)
            flag = arr[slot, 1, 1][PAGE - 1 :].astype(F32)
            moved = jnp.broadcast_to(flag, (PAGE, HEAD)).astype(BF16) == jnp.asarray(1.0, BF16)
            own = rdst[slot].astype(F32)
            kept = []
            for p in range(2):
                at = (length + (2.0 - p * PAGE)).astype(BF16)
                hit = row == at
                for c in range(2):
                    block = arr[slot, p, c]
                    if p == 1:
                        block = jnp.where(last, zero, block)
                    block = jnp.where(hit, own[c : c + 1].astype(BF16), block)
                    block = jnp.where(moved, block, zero)
                    cache_out[slot, p, c] = block
                    kept.append(block)
            query = qd[slot].astype(BF16)
            bound = length + 3.0
            s0 = dot_t(query, kept[0]) * scale
            s1 = dot_t(query, kept[2]) * scale
            parts0.append(jnp.where(lane4 < bound, s0, NEG))
            parts1.append(jnp.where(lane4 + float(PAGE) < bound, s1, NEG))
            values.append((kept[1], kept[3]))
        for i in range(batch):
            w0, w1 = soft(parts0[i], parts1[i])
            mixed = dot(w0, values[i][0]) + dot(w1, values[i][1])
            for g in range(GROUPS):
                att_d[g, pl.ds(slots[i], 1), :] = mixed[g : g + 1]
        return 0

    steps = n // batch
    marks = [0, steps // 4, 3 * steps // 4, steps]
    lax.fori_loop(marks[0], marks[1], dst_step, 0)
    src_tail[1]()
    lax.fori_loop(marks[1], marks[2], dst_step, 0)
    src_tail[2]()
    lax.fori_loop(marks[2], marks[3], dst_step, 0)

    dst_tail = tail(1, att_d, d_half, d_half_in, d_pair, d_rs, d_rs_in, d_full)
    dst_tail[0]()
    src_tail[3]()
    for stage in dst_tail[1:]:
        stage()
    src_tail[4]()


def place(*refs):
    sem = refs[-1]
    half = len(refs) // 2
    copies = [
        pltpu.make_async_copy(src, dst, sem.at[i])
        for i, (src, dst) in enumerate(zip(refs[:half], refs[half:-1]))
    ]
    for copy in copies:
        copy.start()
    for copy in copies:
        copy.wait()


def shards(
    pool,
    page_table,
    lengths,
    targets,
    migrating,
    queries_src,
    new_rows,
    queries_dst,
    rows_dst,
    w_out,
):
    n = lax.axis_size("inst")
    tp_size = lax.axis_size("tp")
    his = tp_size // 2
    requests = queries_src.shape[0]
    width = w_out.shape[1]
    cols = width // tp_size
    smem = pl.BlockSpec(memory_space=pltpu.SMEM)
    vmem = pl.BlockSpec(memory_space=pltpu.VMEM)
    hbm = pl.BlockSpec(memory_space=pl.ANY)
    cache = (requests, 2, 2, PAGE, HEAD)

    def sums(rows):
        return [
            pltpu.VMEM((his, rows, cols), BF16),
            pltpu.VMEM((his, rows, cols), BF16),
            pltpu.VMEM((his, rows, cols), F32),
            pltpu.VMEM((his, rows, cols), BF16),
            pltpu.VMEM((his, rows, cols), BF16),
        ]

    dma = pltpu.SemaphoreType.DMA
    in_hbm = functools.partial(pltpu.with_memory_space_constraint, memory_space=pltpu.HBM)
    results = pl.pallas_call(
        functools.partial(kernel, n, tp_size),
        out_shape=(
            pltpu.VMEM((requests, 2, width), BF16),
            pltpu.VMEM(cache, BF16),
            pltpu.VMEM((requests, width), BF16),
        ),
        in_specs=[smem] * 4 + [vmem] * 4 + [hbm] * 2,
        out_specs=(vmem, vmem, vmem),
        scratch_shapes=[
            pltpu.VMEM(pool.shape, BF16),
            pltpu.VMEM(w_out.shape, BF16),
            pltpu.VMEM(cache, BF16),
            pltpu.VMEM(cache, BF16),
            pltpu.VMEM((requests, 2 * GROUPS, HEAD), F32),
            pltpu.VMEM((requests, GROUPS, HEAD), F32),
            pltpu.VMEM((GROUPS, 2 * requests, HEAD), F32),
            pltpu.VMEM((GROUPS, requests, HEAD), F32),
        ]
        + sums(2 * requests)
        + sums(requests)
        + [
            dma((2,)),
            dma((n,)),
            dma((n,)),
            dma((4,)),
            dma((4 * his,)),
            dma((4 * his,)),
            dma((4 * his,)),
        ],
        compiler_params=pltpu.CompilerParams(
            collective_id=0, has_side_effects=True, vmem_limit_bytes=28 * 1024 * 1024
        ),
        name="migrate",
    )(
        *map(
            in_hbm,
            (
                lengths,
                targets,
                migrating,
                page_table.T,
                queries_src,
                new_rows,
                queries_dst,
                rows_dst,
                pool,
                w_out,
            ),
        )
    )
    return pl.pallas_call(
        place,
        out_shape=tuple(pltpu.HBM(x.shape, x.dtype) for x in results),
        in_specs=[vmem] * 3,
        out_specs=(hbm,) * 3,
        scratch_shapes=[dma((3,))],
        compiler_params=pltpu.CompilerParams(vmem_limit_bytes=8 * 1024 * 1024),
        name="place",
    )(*(pltpu.with_memory_space_constraint(x, pltpu.VMEM) for x in results))


def solution(mesh):
    return jax.shard_map(
        shards,
        mesh=mesh,
        in_specs=(
            P("inst", None, None, "tp"),
            P("inst", None),
            P("inst"),
            P("inst"),
            P("inst"),
            P("inst", None, "tp"),
            P("inst", None, None, "tp"),
            P("inst", "tp"),
            P("inst", None, "tp"),
            P("tp", None),
        ),
        out_specs=(P("inst", None, None), P("inst", None, None, None, "tp"), P("inst", None)),
        check_vma=False,
    )
```

```python
import functools
import math

import jax
import jax.numpy as jnp
from jax import lax
from jax.experimental import pallas as pl
from jax.experimental.pallas import tpu as pltpu
from jax.sharding import PartitionSpec as P

MESH = pl.DeviceIdType.MESH
BF16 = jnp.bfloat16
F32 = jnp.float32
NEG = -1e30
HEAD = 128
PAGE = 128
GROUPS = 4
MIX = 11


def xor(a, b, bits):
    total = 0
    for bit in range(bits):
        weight = 2**bit
        u, v = (a // weight) % 2, (b // weight) % 2
        total = total + (u + v - 2 * u * v) * weight
    return total


def order(k, n):
    if n != 32:
        return (k * MIX) % n
    late = k // 16
    spot = (k - 16 * late) % 8
    turn = (k - 16 * late) // 8
    hop0 = (k % 3 + 1) // 2
    hop1 = 1 - (spot % 3 + 1) // 2
    hop = (1 - late) * hop0 + late * hop1
    cross0 = k - k // 3 - 1
    cross1 = 10 + 3 * turn + spot // 3
    plane0 = k // 3
    plane1 = 6 + 5 * turn + spot - spot // 3 - 1
    count = hop * ((1 - late) * cross0 + late * cross1)
    count = count + (1 - hop) * ((1 - late) * plane0 + late * plane1)
    return ((count * MIX) % 16) * 2 + hop


def kernel(
    n,
    tp_size,
    lens,
    tgts,
    mig,
    table,
    qsrc,
    fresh,
    qdst,
    rdst,
    pool_hbm,
    w_hbm,
    s_full,
    cache_out,
    d_full,
    pool,
    w,
    send,
    arr,
    qs,
    qd,
    att_s,
    att_d,
    s_half,
    s_half_in,
    s_pair,
    s_cross,
    s_cross_in,
    s_rs,
    s_rs_in,
    d_half,
    d_half_in,
    d_pair,
    d_rs,
    d_rs_in,
    load_sem,
    send_sem,
    recv_sem,
    half_sem,
    rs_sem,
    ag_sem,
    fwd_sem,
):
    me = lax.axis_index("inst")
    tp = lax.axis_index("tp")
    core = tp % 2
    hi = tp // 2
    his = tp_size // 2
    mate = tp + 1 - 2 * core
    bits = n.bit_length() - 1
    scale = 1.0 / math.sqrt(HEAD)
    cols = w.shape[1] // tp_size

    def peer_hi(step):
        return ((hi + step) % his) * 2 + core

    def partner(k):
        return xor(me, order(k, n), bits)

    load_pool = pltpu.make_async_copy(pool_hbm, pool, load_sem.at[0])
    load_w = pltpu.make_async_copy(w_hbm, w, load_sem.at[1])
    load_pool.start()
    barrier = pltpu.get_barrier_semaphore()

    def greet(k, _):
        pl.semaphore_signal(
            barrier, inc=1, device_id=(xor(me, k, bits), tp), device_id_type=MESH
        )
        return 0

    lax.fori_loop(1, n, greet, 0)
    pl.semaphore_signal(barrier, inc=1, device_id=(me, mate), device_id_type=MESH)
    for step in range(1, his):
        pl.semaphore_signal(barrier, inc=1, device_id=(me, peer_hi(step)), device_id_type=MESH)

    row = lax.broadcasted_iota(jnp.int32, (PAGE, HEAD), 0).astype(F32).astype(BF16)
    last = row == jnp.asarray(PAGE - 1, BF16)
    zero = jnp.zeros((PAGE, HEAD), BF16)

    def splat(value):
        return jnp.full((1, HEAD), value, F32)

    def move(k):
        peer = partner(k)
        return pltpu.make_async_remote_copy(
            src_ref=send.at[peer],
            dst_ref=arr.at[me],
            send_sem=send_sem.at[k],
            recv_sem=recv_sem.at[k],
            device_id=(peer, tp),
            device_id_type=MESH,
        )

    def arrive(k):
        peer = partner(k)
        return pltpu.make_async_remote_copy(
            src_ref=send.at[peer],
            dst_ref=arr.at[peer],
            send_sem=send_sem.at[k],
            recv_sem=recv_sem.at[k],
            device_id=(peer, tp),
            device_id_type=MESH,
        )

    def pack(k, ref):
        slot = partner(k)
        request = jnp.int32(0)
        for j in range(n):
            request = jnp.where(tgts[j] == slot, j, request)
        length = lens[request].astype(F32)
        flag = mig[request].astype(F32)
        rows_new = fresh[request].astype(F32)
        for p in range(2):
            at = splat(length - p * PAGE).astype(BF16)
            next_at = splat(length - p * PAGE + 1.0).astype(BF16)
            keep = row < at
            first = row == at
            second = row == next_at
            for c in range(2):
                page = pool[table[p, request], c]
                new0 = rows_new[0, c : c + 1].astype(BF16)
                new1 = rows_new[1, c : c + 1].astype(BF16)
                block = jnp.where(keep, page, zero)
                block = jnp.where(first, new0, block)
                block = jnp.where(second, new1, block)
                if p == 1:
                    note = splat(length if c == 0 else flag).astype(BF16)
                    block = jnp.where(last, note, block)
                ref[slot, p, c] = block

    q_wide = qsrc[...].astype(F32)
    for g in range(GROUPS):
        lanes = slice(g * HEAD, (g + 1) * HEAD)
        for t in range(2):
            qs[:, 2 * g + t, :] = q_wide[:, t, lanes]
        qd[:, g, :] = qdst[:, lanes].astype(F32)

    load_pool.wait()
    pl.semaphore_wait(barrier, n - 1 + his)
    load_w.start()

    def send_step(k, _):
        pack(k, send)
        move(k).start()
        return 0

    batch = min(4, n)
    lax.fori_loop(1, n, send_step, 0)
    pack(0, send)
    arr[me] = send[me]

    def dot_t(a, b):
        return lax.dot_general(a, b, (((1,), (1,)), ((), ())), preferred_element_type=F32)

    def dot(a, b):
        return jnp.dot(a, b, preferred_element_type=F32)

    def soft(s0, s1):
        top = jnp.maximum(
            jnp.max(s0, axis=1, keepdims=True), jnp.max(s1, axis=1, keepdims=True)
        )
        e0, e1 = jnp.exp(s0 - top), jnp.exp(s1 - top)
        total = jnp.sum(e0, axis=1, keepdims=True) + jnp.sum(e1, axis=1, keepdims=True)
        return (e0 / total).astype(BF16), (e1 / total).astype(BF16)

    wide = min(8, n)
    lane8 = lax.broadcasted_iota(jnp.int32, (8, HEAD), 1)
    step8 = lax.broadcasted_iota(jnp.int32, (8, HEAD), 0) % 2

    def src_step(b, _):
        parts0, parts1 = [], []
        for i in range(wide):
            request = b * wide + i
            slot = tgts[request]
            query = qs[request].astype(BF16)
            bound = lens[request] + 1 + step8
            s0 = dot_t(query, send[slot, 0, 0]) * scale
            s1 = dot_t(query, send[slot, 1, 0]) * scale
            parts0.append(jnp.where(lane8 < bound, s0, NEG))
            parts1.append(jnp.where(lane8 + PAGE < bound, s1, NEG))
        w0, w1 = soft(jnp.concatenate(parts0, axis=0), jnp.concatenate(parts1, axis=0))
        for i in range(wide):
            request = b * wide + i
            slot = tgts[request]
            rows = slice(8 * i, 8 * i + 8)
            value1 = jnp.where(last, zero, send[slot, 1, 1])
            mixed = dot(w0[rows], send[slot, 0, 1]) + dot(w1[rows], value1)
            for g in range(GROUPS):
                att_s[g, pl.ds(2 * request, 2), :] = mixed[2 * g : 2 * g + 2]
        return 0

    lax.fori_loop(0, n // wide, src_step, 0)

    def remote(src, dst, sems, index, target):
        return pltpu.make_async_remote_copy(
            src_ref=src,
            dst_ref=dst,
            send_sem=sems.at[2 * index],
            recv_sem=sems.at[2 * index + 1],
            device_id=(me, target),
            device_id_type=MESH,
        )

    def block_cols(index):
        return pl.ds(pl.multiple_of(index * cols, cols), cols)

    def ring_tail(att, half, half_in, pair, cross, cross_in, rs, rs_in, full):
        a = jnp.concatenate([att[g].astype(BF16) for g in range(GROUPS)], axis=1)
        part = cols // 2
        up, down = peer_hi(1), peer_hi(his - 1)

        def spot(step, side=None):
            start = (((hi + step) % his) * 2 + core) * cols
            if side is None:
                return full.at[:, :, pl.ds(pl.multiple_of(start, cols), cols)]
            return full.at[:, :, pl.ds(pl.multiple_of(start + side * part, part), part)]

        def mates(step):
            start = (((hi + step) % his) * 2 + 1 - core) * cols
            return full.at[:, :, pl.ds(pl.multiple_of(start, cols), cols)]

        swap = remote(half, half_in, half_sem, 0, mate)
        over = [
            remote(cross.at[0], cross_in.at[0], rs_sem, 0, up),
            remote(cross.at[1], cross_in.at[1], rs_sem, 1, down),
        ]
        near = [
            remote(rs.at[0], rs_in.at[0], rs_sem, 2, up),
            remote(rs.at[1], rs_in.at[1], rs_sem, 3, down),
        ]
        give = [remote(spot(0), spot(0), ag_sem, i, to) for i, to in enumerate((up, down))]
        take = [
            remote(spot(0), spot(step), ag_sem, i, to)
            for i, (step, to) in enumerate(((his - 1, up), (1, down)))
        ]
        pass_on = [
            remote(spot(step, side), spot(step, side), ag_sem, 2 + side, to)
            for side, (step, to) in enumerate(((his - 1, up), (1, down)))
        ]
        last_in = [
            remote(spot(0, side), spot(2, side), ag_sem, 2 + side, to)
            for side, to in enumerate((up, down))
        ]
        forward = [remote(spot(step), spot(step), fwd_sem, step, mate) for step in range(his)]
        received = [remote(spot(step), mates(step), fwd_sem, step, mate) for step in range(his)]

        def project():
            for step in range(his):
                z = (hi + step) % his
                half[step] = dot(a, w[:, block_cols(z * 2 + 1 - core)]).astype(BF16)
            swap.start()
            for step in range(his):
                z = (hi + step) % his
                pair[step] = dot(a, w[:, block_cols(z * 2 + core)])

        def far():
            swap.wait()
            for step in range(his):
                pair[step] = pair[step] + half_in[step].astype(F32)
            cross[0] = pair[2, :, :part].astype(BF16)
            cross[1] = pair[2, :, part:].astype(BF16)
            for copy in over:
                copy.start()

        def close():
            for copy in over:
                copy.wait()
            rs[0, :, :part] = (pair[1, :, :part] + cross_in[0].astype(F32)).astype(BF16)
            rs[0, :, part:] = pair[1, :, part:].astype(BF16)
            rs[1, :, :part] = pair[his - 1, :, :part].astype(BF16)
            rs[1, :, part:] = (pair[his - 1, :, part:] + cross_in[1].astype(F32)).astype(BF16)
            for copy in near:
                copy.start()

        def total():
            for copy in near:
                copy.wait()
            sums = pair[0] + rs_in[0].astype(F32) + rs_in[1].astype(F32)
            spot(0)[...] = sums.reshape(full.shape[:2] + (cols,)).astype(BF16)
            for copy in give:
                copy.start()
            forward[0].start()

        def relay():
            for side, step in enumerate((his - 1, 1)):
                take[side].wait_recv()
                pass_on[side].start()
                forward[step].start()

        def end():
            for copy in last_in:
                copy.wait_recv()
            forward[2].start()
            for copy in received:
                copy.wait_recv()
            for copy in give + pass_on + forward:
                copy.wait_send()

        return project, far, close, total, relay, end

    def tail(part, att, half, half_in, pair, rs, rs_in, full):
        a = jnp.concatenate([att[g].astype(BF16) for g in range(GROUPS)], axis=1)

        def part_full(index):
            where = block_cols(index)
            return full.at[:, where]

        swap = remote(half, half_in, half_sem, part, mate)
        scatter = [
            remote(rs.at[step], rs_in.at[step], rs_sem, part * his + step, peer_hi(step))
            for step in range(1, his)
        ]
        mine = part_full(tp)
        gather = [
            remote(mine, mine, ag_sem, part * his + step, peer_hi(step))
            for step in range(1, his)
        ]
        landed = [
            remote(
                mine,
                part_full(((hi + his - step) % his) * 2 + core),
                ag_sem,
                part * his + step,
                peer_hi(step),
            )
            for step in range(1, his)
        ]
        forward = []
        received = []
        for step in range(his):
            owner = ((hi + his - step) % his) * 2
            have, want = part_full(owner + core), part_full(owner + 1 - core)
            forward.append(remote(have, have, fwd_sem, part * his + step, mate))
            received.append(remote(have, want, fwd_sem, part * his + step, mate))

        def one():
            for step in range(his):
                z = (hi + step) % his
                half[step] = dot(a, w[:, block_cols(z * 2 + 1 - core)]).astype(BF16)
            swap.start()
            for step in range(his):
                z = (hi + step) % his
                pair[step] = dot(a, w[:, block_cols(z * 2 + core)])

        def two():
            swap.wait()
            for step in range(1, his):
                rs[step] = (pair[step] + half_in[step].astype(F32)).astype(BF16)
                scatter[step - 1].start()
            pair[0] = pair[0] + half_in[0].astype(F32)

        def three():
            for copy in scatter:
                copy.wait()
            total = pair[0]
            for step in range(1, his):
                total = total + rs_in[step].astype(F32)
            mine[...] = total.astype(BF16)
            for copy in gather:
                copy.start()
            forward[0].start()

        def four():
            for step in range(1, his):
                landed[step - 1].wait_recv()
                forward[step].start()
            for step in range(his):
                received[step].wait_recv()

        def five():
            for copy in gather:
                copy.wait_send()
            for copy in forward:
                copy.wait_send()

        return one, two, three, four, five

    load_w.wait()
    project, far, close, total_up, relay, end = ring_tail(
        att_s, s_half, s_half_in, s_pair, s_cross, s_cross_in, s_rs, s_rs_in, s_full
    )
    project()

    lane4 = lax.broadcasted_iota(jnp.int32, (GROUPS, HEAD), 1).astype(F32)

    def dst_step(b, _):
        slots, parts0, parts1, values = [], [], [], []
        for i in range(batch):
            k = b * batch + i

            @pl.when(k > 0)
            def _():
                move(k).wait_send()

        for i in range(batch):
            k = b * batch + i
            slot = partner(k)
            slots.append(slot)

            @pl.when(k > 0)
            def _():
                arrive(k).wait_recv()

            length = arr[slot, 1, 0][PAGE - 1 :].astype(F32)
            flag = arr[slot, 1, 1][PAGE - 1 :].astype(F32)
            moved = jnp.broadcast_to(flag, (PAGE, HEAD)).astype(BF16) == jnp.asarray(1.0, BF16)
            own = rdst[slot].astype(F32)
            kept = []
            for p in range(2):
                at = (length + (2.0 - p * PAGE)).astype(BF16)
                hit = row == at
                for c in range(2):
                    block = arr[slot, p, c]
                    if p == 1:
                        block = jnp.where(last, zero, block)
                    block = jnp.where(hit, own[c : c + 1].astype(BF16), block)
                    block = jnp.where(moved, block, zero)
                    cache_out[slot, p, c] = block
                    kept.append(block)
            query = qd[slot].astype(BF16)
            bound = length + 3.0
            s0 = dot_t(query, kept[0]) * scale
            s1 = dot_t(query, kept[2]) * scale
            parts0.append(jnp.where(lane4 < bound, s0, NEG))
            parts1.append(jnp.where(lane4 + float(PAGE) < bound, s1, NEG))
            values.append((kept[1], kept[3]))
        for i in range(batch):
            w0, w1 = soft(parts0[i], parts1[i])
            mixed = dot(w0, values[i][0]) + dot(w1, values[i][1])
            for g in range(GROUPS):
                att_d[g, pl.ds(slots[i], 1), :] = mixed[g : g + 1]
        return 0

    steps = n // batch
    marks = [steps * j // 8 for j in (0, 2, 4, 6, 8)]
    lax.fori_loop(marks[0], marks[1], dst_step, 0)
    far()
    lax.fori_loop(marks[1], marks[2], dst_step, 0)
    close()
    lax.fori_loop(marks[2], marks[3], dst_step, 0)
    total_up()
    lax.fori_loop(marks[3], marks[4], dst_step, 0)

    dst_tail = tail(1, att_d, d_half, d_half_in, d_pair, d_rs, d_rs_in, d_full)
    dst_tail[0]()
    relay()
    for stage in dst_tail[1:]:
        stage()
    end()


def place(*refs):
    sem = refs[-1]
    half = len(refs) // 2
    copies = [
        pltpu.make_async_copy(src, dst, sem.at[i])
        for i, (src, dst) in enumerate(zip(refs[:half], refs[half:-1]))
    ]
    for copy in copies:
        copy.start()
    for copy in copies:
        copy.wait()


def shards(
    pool,
    page_table,
    lengths,
    targets,
    migrating,
    queries_src,
    new_rows,
    queries_dst,
    rows_dst,
    w_out,
):
    n = lax.axis_size("inst")
    tp_size = lax.axis_size("tp")
    his = tp_size // 2
    requests = queries_src.shape[0]
    width = w_out.shape[1]
    cols = width // tp_size
    smem = pl.BlockSpec(memory_space=pltpu.SMEM)
    vmem = pl.BlockSpec(memory_space=pltpu.VMEM)
    hbm = pl.BlockSpec(memory_space=pl.ANY)
    cache = (requests, 2, 2, PAGE, HEAD)

    def sums(rows, sent):
        return [
            pltpu.VMEM((his, rows, cols), BF16),
            pltpu.VMEM((his, rows, cols), BF16),
            pltpu.VMEM((his, rows, cols), F32),
        ] + [pltpu.VMEM((parts, rows, width), BF16) for parts, width in sent]

    dma = pltpu.SemaphoreType.DMA
    in_hbm = functools.partial(pltpu.with_memory_space_constraint, memory_space=pltpu.HBM)
    results = pl.pallas_call(
        functools.partial(kernel, n, tp_size),
        out_shape=(
            pltpu.VMEM((requests, 2, width), BF16),
            pltpu.VMEM(cache, BF16),
            pltpu.VMEM((requests, width), BF16),
        ),
        in_specs=[smem] * 4 + [vmem] * 4 + [hbm] * 2,
        out_specs=(vmem, vmem, vmem),
        scratch_shapes=[
            pltpu.VMEM(pool.shape, BF16),
            pltpu.VMEM(w_out.shape, BF16),
            pltpu.VMEM(cache, BF16),
            pltpu.VMEM(cache, BF16),
            pltpu.VMEM((requests, 2 * GROUPS, HEAD), F32),
            pltpu.VMEM((requests, GROUPS, HEAD), F32),
            pltpu.VMEM((GROUPS, 2 * requests, HEAD), F32),
            pltpu.VMEM((GROUPS, requests, HEAD), F32),
        ]
        + sums(2 * requests, [(2, cols // 2)] * 2 + [(2, cols)] * 2)
        + sums(requests, [(his, cols)] * 2)
        + [
            dma((2,)),
            dma((n,)),
            dma((n,)),
            dma((4,)),
            dma((4 * his,)),
            dma((4 * his,)),
            dma((4 * his,)),
        ],
        compiler_params=pltpu.CompilerParams(
            collective_id=0, has_side_effects=True, vmem_limit_bytes=28 * 1024 * 1024
        ),
        name="migrate",
    )(
        *map(
            in_hbm,
            (
                lengths,
                targets,
                migrating,
                page_table.T,
                queries_src,
                new_rows,
                queries_dst,
                rows_dst,
                pool,
                w_out,
            ),
        )
    )
    return pl.pallas_call(
        place,
        out_shape=tuple(pltpu.HBM(x.shape, x.dtype) for x in results),
        in_specs=[vmem] * 3,
        out_specs=(hbm,) * 3,
        scratch_shapes=[dma((3,))],
        compiler_params=pltpu.CompilerParams(vmem_limit_bytes=8 * 1024 * 1024),
        name="place",
    )(*(pltpu.with_memory_space_constraint(x, pltpu.VMEM) for x in results))


def solution(mesh):
    return jax.shard_map(
        shards,
        mesh=mesh,
        in_specs=(
            P("inst", None, None, "tp"),
            P("inst", None),
            P("inst"),
            P("inst"),
            P("inst"),
            P("inst", None, "tp"),
            P("inst", None, None, "tp"),
            P("inst", "tp"),
            P("inst", None, "tp"),
            P("tp", None),
        ),
        out_specs=(P("inst", None, None), P("inst", None, None, None, "tp"), P("inst", None)),
        check_vma=False,
    )
```

```python
import functools
import math

import jax
import jax.numpy as jnp
from jax import lax
from jax.experimental import pallas as pl
from jax.experimental.pallas import tpu as pltpu
from jax.sharding import PartitionSpec as P

MESH = pl.DeviceIdType.MESH
BF16 = jnp.bfloat16
F32 = jnp.float32
NEG = -1e30
HEAD = 128
PAGE = 128
GROUPS = 4
MIX = 19
FIRST = 13
TURN = 5


def shift(a, b, n, sign):
    if n != 32:
        return (a + n + sign * b) % n
    y = (a // 8 + 4 + sign * (b // 8)) % 4
    x = ((a // 2) % 4 + 4 + sign * ((b // 2) % 4)) % 4
    return y * 8 + x * 2 + (a + b) % 2


def kernel(
    n,
    tp_size,
    lens,
    tgts,
    mig,
    table,
    qsrc,
    fresh,
    qdst,
    rdst,
    pool_hbm,
    w_hbm,
    s_full,
    cache_out,
    d_out,
    pool,
    w,
    send,
    arr,
    qs,
    qd,
    att_s,
    att_d,
    s_half,
    s_half_in,
    s_pair,
    s_rs,
    s_rs_in,
    e_half,
    e_half_in,
    e_pair,
    e_rs,
    e_rs_in,
    d_half,
    d_half_in,
    d_pair,
    d_rs,
    d_rs_in,
    d_rows,
    load_sem,
    send_sem,
    recv_sem,
    half_sem,
    rs_sem,
    ag_sem,
    fwd_sem,
):
    me = lax.axis_index("inst")
    tp = lax.axis_index("tp")
    core = tp % 2
    hi = tp // 2
    his = tp_size // 2
    mate = tp + 1 - 2 * core
    scale = 1.0 / math.sqrt(HEAD)
    cols = w.shape[1] // tp_size

    def peer_hi(step):
        return ((hi + step) % his) * 2 + core

    def item(k):
        half = n // 2
        return (k // half) * half + (k % half + TURN * core) % half

    def offset_of(index):
        return (index * MIX + FIRST) % n

    def offset(k):
        return offset_of(item(k))

    def target(k):
        return shift(me, offset(k), n, 1)

    def origin(k):
        return shift(me, offset(k), n, -1)

    load_pool = pltpu.make_async_copy(pool_hbm, pool, load_sem.at[0])
    load_w = pltpu.make_async_copy(w_hbm, w, load_sem.at[1])
    load_pool.start()
    barrier = pltpu.get_barrier_semaphore()

    def greet(k, _):
        pl.semaphore_signal(
            barrier, inc=1, device_id=((me + k) % n, tp), device_id_type=MESH
        )
        return 0

    lax.fori_loop(1, n, greet, 0)
    pl.semaphore_signal(barrier, inc=1, device_id=(me, mate), device_id_type=MESH)
    for step in range(1, his):
        pl.semaphore_signal(barrier, inc=1, device_id=(me, peer_hi(step)), device_id_type=MESH)

    row = lax.broadcasted_iota(jnp.int32, (PAGE, HEAD), 0).astype(F32).astype(BF16)
    last = row == jnp.asarray(PAGE - 1, BF16)
    zero = jnp.zeros((PAGE, HEAD), BF16)

    def splat(value):
        return jnp.full((1, HEAD), value, F32)

    def move(k):
        peer = target(k)
        return pltpu.make_async_remote_copy(
            src_ref=send.at[peer],
            dst_ref=arr.at[me],
            send_sem=send_sem.at[k],
            recv_sem=recv_sem.at[k],
            device_id=(peer, tp),
            device_id_type=MESH,
        )

    def arrive(k):
        peer = origin(k)
        return pltpu.make_async_remote_copy(
            src_ref=send.at[peer],
            dst_ref=arr.at[peer],
            send_sem=send_sem.at[k],
            recv_sem=recv_sem.at[k],
            device_id=(peer, tp),
            device_id_type=MESH,
        )

    def pack(k, ref):
        slot = target(k)
        request = jnp.int32(0)
        for j in range(n):
            request = jnp.where(tgts[j] == slot, j, request)
        length = lens[request].astype(F32)
        flag = mig[request].astype(F32)
        rows_new = fresh[request].astype(F32)
        for p in range(2):
            at = splat(length - p * PAGE).astype(BF16)
            next_at = splat(length - p * PAGE + 1.0).astype(BF16)
            keep = row < at
            first = row == at
            second = row == next_at
            for c in range(2):
                page = pool[table[p, request], c]
                new0 = rows_new[0, c : c + 1].astype(BF16)
                new1 = rows_new[1, c : c + 1].astype(BF16)
                block = jnp.where(keep, page, zero)
                block = jnp.where(first, new0, block)
                block = jnp.where(second, new1, block)
                if p == 1:
                    note = splat(length if c == 0 else flag).astype(BF16)
                    block = jnp.where(last, note, block)
                ref[slot, p, c] = block

    q_wide = qsrc[...].astype(F32)
    for g in range(GROUPS):
        lanes = slice(g * HEAD, (g + 1) * HEAD)
        for t in range(2):
            qs[:, 2 * g + t, :] = q_wide[:, t, lanes]
        qd[:, g, :] = qdst[:, lanes].astype(F32)

    load_pool.wait()
    pl.semaphore_wait(barrier, n - 1 + his)
    load_w.start()

    def go(k):
        @pl.when(offset(k) != 0)
        def _():
            move(k).start()

    def send_step(k, _):
        pack(k, send)
        go(k)
        return 0

    batch = min(4, n)
    ahead = min(8, n // 2)

    def tick(j):
        @pl.when(offset(j) != 0)
        def _():
            move(j).wait_send()

        go(j + ahead)

    lax.fori_loop(0, ahead, send_step, 0)

    def pack_step(k, _):
        pack(k, send)

        @pl.when(k % 4 == 3)
        def _():
            tick((k - ahead) // 4)

        return 0

    lax.fori_loop(ahead, n, pack_step, 0)
    arr[me] = send[me]

    def dot_t(a, b):
        return lax.dot_general(a, b, (((1,), (1,)), ((), ())), preferred_element_type=F32)

    def dot(a, b):
        return jnp.dot(a, b, preferred_element_type=F32)

    def soft(s0, s1):
        top = jnp.maximum(
            jnp.max(s0, axis=1, keepdims=True), jnp.max(s1, axis=1, keepdims=True)
        )
        e0, e1 = jnp.exp(s0 - top), jnp.exp(s1 - top)
        total = jnp.sum(e0, axis=1, keepdims=True) + jnp.sum(e1, axis=1, keepdims=True)
        return (e0 / total).astype(BF16), (e1 / total).astype(BF16)

    wide = min(8, n)
    lane8 = lax.broadcasted_iota(jnp.int32, (8, HEAD), 1)
    step8 = lax.broadcasted_iota(jnp.int32, (8, HEAD), 0) % 2

    def src_step(b, _):
        parts0, parts1 = [], []
        tick((n - ahead) // 4 + b)
        for i in range(wide):
            request = b * wide + i
            slot = tgts[request]
            query = qs[request].astype(BF16)
            bound = lens[request] + 1 + step8
            s0 = dot_t(query, send[slot, 0, 0]) * scale
            s1 = dot_t(query, send[slot, 1, 0]) * scale
            parts0.append(jnp.where(lane8 < bound, s0, NEG))
            parts1.append(jnp.where(lane8 + PAGE < bound, s1, NEG))
        w0, w1 = soft(jnp.concatenate(parts0, axis=0), jnp.concatenate(parts1, axis=0))
        for i in range(wide):
            request = b * wide + i
            slot = tgts[request]
            rows = slice(8 * i, 8 * i + 8)
            value1 = jnp.where(last, zero, send[slot, 1, 1])
            mixed = dot(w0[rows], send[slot, 0, 1]) + dot(w1[rows], value1)
            for g in range(GROUPS):
                att_s[g, pl.ds(2 * request, 2), :] = mixed[2 * g : 2 * g + 2]
        return 0

    lax.fori_loop(0, n // wide, src_step, 0)

    def remote(src, dst, sems, index, target):
        return pltpu.make_async_remote_copy(
            src_ref=src,
            dst_ref=dst,
            send_sem=sems.at[2 * index],
            recv_sem=sems.at[2 * index + 1],
            device_id=(me, target),
            device_id_type=MESH,
        )

    def block_cols(index):
        return pl.ds(pl.multiple_of(index * cols, cols), cols)

    def tail(part, att, rows, half, half_in, pair, rs, rs_in, full):
        a = jnp.concatenate([att[g, rows].astype(BF16) for g in range(GROUPS)], axis=1)

        def part_full(index):
            where = block_cols(index)
            if len(full.shape) == 2:
                return full.at[rows, where]
            return full.at[:, :, where]

        swap = remote(half, half_in, half_sem, part, mate)
        scatter = [
            remote(rs.at[step], rs_in.at[step], rs_sem, part * his + step, peer_hi(step))
            for step in range(1, his)
        ]
        mine = part_full(tp)
        gather = [
            remote(mine, mine, ag_sem, part * his + step, peer_hi(step))
            for step in range(1, his)
        ]
        landed = [
            remote(
                mine,
                part_full(((hi + his - step) % his) * 2 + core),
                ag_sem,
                part * his + step,
                peer_hi(step),
            )
            for step in range(1, his)
        ]
        forward = []
        received = []
        for step in range(his):
            owner = ((hi + his - step) % his) * 2
            have, want = part_full(owner + core), part_full(owner + 1 - core)
            forward.append(remote(have, have, fwd_sem, part * his + step, mate))
            received.append(remote(have, want, fwd_sem, part * his + step, mate))

        def one():
            for step in range(his):
                z = (hi + step) % his
                half[step] = dot(a, w[:, block_cols(z * 2 + 1 - core)]).astype(BF16)
            swap.start()
            for step in range(his):
                z = (hi + step) % his
                pair[step] = dot(a, w[:, block_cols(z * 2 + core)])

        def two():
            swap.wait()
            for step in range(1, his):
                rs[step] = (pair[step] + half_in[step].astype(F32)).astype(BF16)
                scatter[step - 1].start()
            pair[0] = pair[0] + half_in[0].astype(F32)

        def three():
            for copy in scatter:
                copy.wait()
            total = pair[0]
            for step in range(1, his):
                total = total + rs_in[step].astype(F32)
            if len(full.shape) == 3:
                total = total.reshape(full.shape[:2] + (cols,))
            mine[...] = total.astype(BF16)
            for copy in gather:
                copy.start()
            forward[0].start()

        def four():
            for step in range(1, his):
                landed[step - 1].wait_recv()
                forward[step].start()
            for step in range(his):
                received[step].wait_recv()

        def five():
            for copy in gather:
                copy.wait_send()
            for copy in forward:
                copy.wait_send()

        return one, two, three, four, five

    ticked = (n - ahead) // 4 + n // wide
    load_w.wait()
    src_tail = tail(0, att_s, slice(None), s_half, s_half_in, s_pair, s_rs, s_rs_in, s_full)
    src_tail[0]()

    lane4 = lax.broadcasted_iota(jnp.int32, (GROUPS, HEAD), 1).astype(F32)

    def dst_step(b, _):
        slots, parts0, parts1, values = [], [], [], []
        for i in range(2):
            j = ticked + 2 * b + i

            @pl.when(j + ahead < n)
            def _():
                tick(j)

        for i in range(batch):
            k = b * batch + i

            @pl.when(offset(k) != 0)
            def _():
                arrive(k).wait_recv()

        for i in range(batch):
            k = b * batch + i
            slot = origin(k)
            slots.append(slot)
            length = arr[slot, 1, 0][PAGE - 1 :].astype(F32)
            flag = arr[slot, 1, 1][PAGE - 1 :].astype(F32)
            moved = jnp.broadcast_to(flag, (PAGE, HEAD)).astype(BF16) == jnp.asarray(1.0, BF16)
            own = rdst[slot].astype(F32)
            kept = []
            for p in range(2):
                at = (length + (2.0 - p * PAGE)).astype(BF16)
                hit = row == at
                for c in range(2):
                    block = arr[slot, p, c]
                    if p == 1:
                        block = jnp.where(last, zero, block)
                    block = jnp.where(hit, own[c : c + 1].astype(BF16), block)
                    block = jnp.where(moved, block, zero)
                    cache_out[slot, p, c] = block
                    kept.append(block)
            query = qd[slot].astype(BF16)
            bound = length + 3.0
            s0 = dot_t(query, kept[0]) * scale
            s1 = dot_t(query, kept[2]) * scale
            parts0.append(jnp.where(lane4 < bound, s0, NEG))
            parts1.append(jnp.where(lane4 + float(PAGE) < bound, s1, NEG))
            values.append((kept[1], kept[3]))
        for i in range(batch):
            w0, w1 = soft(parts0[i], parts1[i])
            mixed = dot(w0, values[i][0]) + dot(w1, values[i][1])
            for g in range(GROUPS):
                att_d[g, pl.ds(item(b * batch + i), 1), :] = mixed[g : g + 1]
        return 0

    steps = n // batch
    marks = [steps * j // 8 for j in (0, 1, 3, 4, 6, 8)]
    lax.fori_loop(marks[0], marks[1], dst_step, 0)
    src_tail[1]()
    lax.fori_loop(marks[1], marks[2], dst_step, 0)
    src_tail[2]()
    lax.fori_loop(marks[2], marks[3], dst_step, 0)
    early = tail(1, att_d, slice(0, n // 2), e_half, e_half_in, e_pair, e_rs, e_rs_in, d_rows)
    early[0]()
    early[1]()
    lax.fori_loop(marks[3], marks[4], dst_step, 0)
    src_tail[3]()
    early[2]()
    lax.fori_loop(marks[4], marks[5], dst_step, 0)

    late = tail(2, att_d, slice(n // 2, n), d_half, d_half_in, d_pair, d_rs, d_rs_in, d_rows)
    late[0]()
    early[3]()
    for stage in late[1:4]:
        stage()

    lane = lax.broadcasted_iota(jnp.int32, (n, HEAD), 1)
    owner = jnp.full((n, HEAD), -1, jnp.int32)
    for k in range(n):
        owner = jnp.where(lane == k, shift(me, offset_of(k), n, -1), owner)
    place_row = lax.broadcasted_iota(jnp.int32, (n, HEAD), 0) == owner
    spread = jnp.where(place_row, 1.0, 0.0).astype(BF16)[:, :n]
    for index in range(tp_size):
        where = slice(index * cols, (index + 1) * cols)
        d_out[:, where] = dot(spread, d_rows[:, where]).astype(BF16)

    def drain(k, _):
        @pl.when(offset(k) != 0)
        def _():
            move(k).wait_send()

        return 0

    lax.fori_loop(n - ahead, n, drain, 0)
    src_tail[4]()
    early[4]()
    late[4]()


def place(*refs):
    sem = refs[-1]
    half = len(refs) // 2
    copies = [
        pltpu.make_async_copy(src, dst, sem.at[i])
        for i, (src, dst) in enumerate(zip(refs[:half], refs[half:-1]))
    ]
    for copy in copies:
        copy.start()
    for copy in copies:
        copy.wait()


def shards(
    pool,
    page_table,
    lengths,
    targets,
    migrating,
    queries_src,
    new_rows,
    queries_dst,
    rows_dst,
    w_out,
):
    n = lax.axis_size("inst")
    tp_size = lax.axis_size("tp")
    his = tp_size // 2
    requests = queries_src.shape[0]
    width = w_out.shape[1]
    cols = width // tp_size
    smem = pl.BlockSpec(memory_space=pltpu.SMEM)
    vmem = pl.BlockSpec(memory_space=pltpu.VMEM)
    hbm = pl.BlockSpec(memory_space=pl.ANY)
    cache = (requests, 2, 2, PAGE, HEAD)

    def sums(rows):
        return [
            pltpu.VMEM((his, rows, cols), BF16),
            pltpu.VMEM((his, rows, cols), BF16),
            pltpu.VMEM((his, rows, cols), F32),
            pltpu.VMEM((his, rows, cols), BF16),
            pltpu.VMEM((his, rows, cols), BF16),
        ]

    dma = pltpu.SemaphoreType.DMA
    in_hbm = functools.partial(pltpu.with_memory_space_constraint, memory_space=pltpu.HBM)
    results = pl.pallas_call(
        functools.partial(kernel, n, tp_size),
        out_shape=(
            pltpu.VMEM((requests, 2, width), BF16),
            pltpu.VMEM(cache, BF16),
            pltpu.VMEM((requests, width), BF16),
        ),
        in_specs=[smem] * 4 + [vmem] * 4 + [hbm] * 2,
        out_specs=(vmem, vmem, vmem),
        scratch_shapes=[
            pltpu.VMEM(pool.shape, BF16),
            pltpu.VMEM(w_out.shape, BF16),
            pltpu.VMEM(cache, BF16),
            pltpu.VMEM(cache, BF16),
            pltpu.VMEM((requests, 2 * GROUPS, HEAD), F32),
            pltpu.VMEM((requests, GROUPS, HEAD), F32),
            pltpu.VMEM((GROUPS, 2 * requests, HEAD), F32),
            pltpu.VMEM((GROUPS, requests, HEAD), F32),
        ]
        + sums(2 * requests)
        + sums(requests // 2)
        + sums(requests // 2)
        + [pltpu.VMEM((requests, width), BF16)]
        + [
            dma((2,)),
            dma((n,)),
            dma((n,)),
            dma((6,)),
            dma((6 * his,)),
            dma((6 * his,)),
            dma((6 * his,)),
        ],
        compiler_params=pltpu.CompilerParams(
            collective_id=0, has_side_effects=True, vmem_limit_bytes=28 * 1024 * 1024
        ),
        name="migrate",
    )(
        *map(
            in_hbm,
            (
                lengths,
                targets,
                migrating,
                page_table.T,
                queries_src,
                new_rows,
                queries_dst,
                rows_dst,
                pool,
                w_out,
            ),
        )
    )
    return pl.pallas_call(
        place,
        out_shape=tuple(pltpu.HBM(x.shape, x.dtype) for x in results),
        in_specs=[vmem] * 3,
        out_specs=(hbm,) * 3,
        scratch_shapes=[dma((3,))],
        compiler_params=pltpu.CompilerParams(vmem_limit_bytes=8 * 1024 * 1024),
        name="place",
    )(*(pltpu.with_memory_space_constraint(x, pltpu.VMEM) for x in results))


def solution(mesh):
    return jax.shard_map(
        shards,
        mesh=mesh,
        in_specs=(
            P("inst", None, None, "tp"),
            P("inst", None),
            P("inst"),
            P("inst"),
            P("inst"),
            P("inst", None, "tp"),
            P("inst", None, None, "tp"),
            P("inst", "tp"),
            P("inst", None, "tp"),
            P("tp", None),
        ),
        out_specs=(P("inst", None, None), P("inst", None, None, None, "tp"), P("inst", None)),
        check_vma=False,
    )
```

```python
import functools
import math

import jax
import jax.numpy as jnp
from jax import lax
from jax.experimental import pallas as pl
from jax.experimental.pallas import tpu as pltpu
from jax.sharding import PartitionSpec as P

MESH = pl.DeviceIdType.MESH
BF16 = jnp.bfloat16
F32 = jnp.float32
NEG = -1e30
HEAD = 128
PAGE = 128
GROUPS = 4
TILE = 16
PIECES = 8
MIX = 11


def xor(a, b, bits):
    total = 0
    for bit in range(bits):
        weight = 2**bit
        u, v = (a // weight) % 2, (b // weight) % 2
        total = total + (u + v - 2 * u * v) * weight
    return total


def order(k, n):
    if n != 32:
        return (k * MIX) % n
    late = k // 16
    spot = (k - 16 * late) % 8
    turn = (k - 16 * late) // 8
    hop0 = (k % 3 + 1) // 2
    hop1 = 1 - (spot % 3 + 1) // 2
    hop = (1 - late) * hop0 + late * hop1
    cross0 = k - k // 3 - 1
    cross1 = 10 + 3 * turn + spot // 3
    plane0 = k // 3
    plane1 = 6 + 5 * turn + spot - spot // 3 - 1
    count = hop * ((1 - late) * cross0 + late * cross1)
    count = count + (1 - hop) * ((1 - late) * plane0 + late * plane1)
    return ((count * MIX) % 16) * 2 + hop


def kernel(
    n,
    tp_size,
    lens,
    tgts,
    mig,
    table,
    qsrc,
    fresh,
    qdst,
    rdst,
    pool_hbm,
    w_hbm,
    s_full,
    cache_out,
    d_full,
    pool,
    w,
    send,
    arr,
    qs,
    qd,
    att_s,
    att_d,
    s_half,
    s_half_in,
    s_pair,
    s_cross,
    s_cross_in,
    s_rs,
    s_rs_in,
    d_half,
    d_half_in,
    d_pair,
    d_rs,
    d_rs_in,
    load_sem,
    send_sem,
    recv_sem,
    half_sem,
    rs_sem,
    ag_sem,
    fwd_sem,
):
    me = lax.axis_index("inst")
    tp = lax.axis_index("tp")
    core = tp % 2
    hi = tp // 2
    his = tp_size // 2
    mate = tp + 1 - 2 * core
    bits = n.bit_length() - 1
    scale = 1.0 / math.sqrt(HEAD)
    cols = w.shape[1] // tp_size

    def peer_hi(step):
        return ((hi + step) % his) * 2 + core

    def partner(k):
        return xor(me, order(k, n), bits)

    load_pool = pltpu.make_async_copy(pool_hbm, pool, load_sem.at[0])
    load_w = pltpu.make_async_copy(w_hbm, w, load_sem.at[1])
    load_pool.start()
    barrier = pltpu.get_barrier_semaphore()

    def greet(k, _):
        pl.semaphore_signal(
            barrier, inc=1, device_id=(xor(me, k, bits), tp), device_id_type=MESH
        )
        return 0

    lax.fori_loop(1, n, greet, 0)
    pl.semaphore_signal(barrier, inc=1, device_id=(me, mate), device_id_type=MESH)
    for step in range(1, his):
        pl.semaphore_signal(barrier, inc=1, device_id=(me, peer_hi(step)), device_id_type=MESH)

    row = lax.broadcasted_iota(jnp.int32, (PAGE, HEAD), 0).astype(F32).astype(BF16)
    last = row == jnp.asarray(PAGE - 1, BF16)
    zero = jnp.zeros((PAGE, HEAD), BF16)
    tile_row = lax.broadcasted_iota(jnp.int32, (TILE, HEAD), 0).astype(F32)

    def move(k):
        peer = partner(k)
        return pltpu.make_async_remote_copy(
            src_ref=send.at[peer],
            dst_ref=arr.at[me],
            send_sem=send_sem.at[k],
            recv_sem=recv_sem.at[k],
            device_id=(peer, tp),
            device_id_type=MESH,
        )

    def arrive(k):
        peer = partner(k)
        return pltpu.make_async_remote_copy(
            src_ref=send.at[peer],
            dst_ref=arr.at[peer],
            send_sem=send_sem.at[k],
            recv_sem=recv_sem.at[k],
            device_id=(peer, tp),
            device_id_type=MESH,
        )

    def pack(k, ref):
        slot = partner(k)
        request = jnp.int32(0)
        for j in range(n):
            request = jnp.where(tgts[j] == slot, j, request)
        length = lens[request].astype(F32)
        flag = mig[request].astype(F32)
        rows_new = fresh[request].astype(F32)
        for c in range(2):
            ref[slot, 0, c] = pool[table[0, request], c]
            page = pool[table[1, request], c]
            ref[slot, 1, c, : PAGE - TILE] = page[: PAGE - TILE]
            end = jnp.where(tile_row == TILE - 3.0, rows_new[0, c : c + 1], page[PAGE - TILE :].astype(F32))
            end = jnp.where(tile_row == TILE - 2.0, rows_new[1, c : c + 1], end)
            end = jnp.where(tile_row == TILE - 1.0, length if c == 0 else flag, end)
            ref[slot, 1, c, PAGE - TILE :] = end.astype(BF16)

    q_wide = qsrc[...].astype(F32)
    for g in range(GROUPS):
        lanes = slice(g * HEAD, (g + 1) * HEAD)
        for t in range(2):
            qs[:, 2 * g + t, :] = q_wide[:, t, lanes]
        qd[:, g, :] = qdst[:, lanes].astype(F32)

    load_pool.wait()
    pl.semaphore_wait(barrier, n - 1 + his)
    load_w.start()

    def send_step(k, _):
        pack(k, send)
        move(k).start()
        return 0

    batch = min(4, n)
    ahead = min(4 * batch, n)
    lax.fori_loop(1, ahead, send_step, 0)
    pack(0, send)
    arr[me] = send[me]

    def pack_step(k, _):
        pack(k, send)
        return 0

    lax.fori_loop(ahead, n, pack_step, 0)

    def dot_t(a, b):
        return lax.dot_general(a, b, (((1,), (1,)), ((), ())), preferred_element_type=F32)

    def dot(a, b):
        return jnp.dot(a, b, preferred_element_type=F32)

    def soft(s0, s1):
        top = jnp.maximum(
            jnp.max(s0, axis=1, keepdims=True), jnp.max(s1, axis=1, keepdims=True)
        )
        e0, e1 = jnp.exp(s0 - top), jnp.exp(s1 - top)
        total = jnp.sum(e0, axis=1, keepdims=True) + jnp.sum(e1, axis=1, keepdims=True)
        return (e0 / total).astype(BF16), (e1 / total).astype(BF16)

    wide = min(8, n)
    lane8 = lax.broadcasted_iota(jnp.int32, (8, HEAD), 1)
    step8 = lax.broadcasted_iota(jnp.int32, (8, HEAD), 0) % 2
    fresh8 = (lane8 == PAGE - 3) | ((lane8 == PAGE - 2) & (step8 == 1))

    def src_step(b, _):
        parts0, parts1 = [], []
        for i in range(wide):
            request = b * wide + i
            slot = tgts[request]
            query = qs[request].astype(BF16)
            bound = lens[request]
            s0 = dot_t(query, send[slot, 0, 0]) * scale
            s1 = dot_t(query, send[slot, 1, 0]) * scale
            parts0.append(jnp.where(lane8 < bound, s0, NEG))
            parts1.append(jnp.where((lane8 + PAGE < bound) | fresh8, s1, NEG))
        w0, w1 = soft(jnp.concatenate(parts0, axis=0), jnp.concatenate(parts1, axis=0))
        for i in range(wide):
            request = b * wide + i
            slot = tgts[request]
            rows = slice(8 * i, 8 * i + 8)
            mixed = dot(w0[rows], send[slot, 0, 1]) + dot(w1[rows], send[slot, 1, 1])
            for g in range(GROUPS):
                att_s[g, pl.ds(2 * request, 2), :] = mixed[2 * g : 2 * g + 2]
        return 0

    lax.fori_loop(0, n // wide, src_step, 0)

    def remote(src, dst, sems, index, target):
        return pltpu.make_async_remote_copy(
            src_ref=src,
            dst_ref=dst,
            send_sem=sems.at[2 * index],
            recv_sem=sems.at[2 * index + 1],
            device_id=(me, target),
            device_id_type=MESH,
        )

    def block_cols(index):
        return pl.ds(pl.multiple_of(index * cols, cols), cols)

    def ring_tail(att, half, half_in, pair, cross, cross_in, rs, rs_in, full):
        a = jnp.concatenate([att[g].astype(BF16) for g in range(GROUPS)], axis=1)
        part = cols // 2
        up, down = peer_hi(1), peer_hi(his - 1)

        def spot(step, side=None):
            start = (((hi + step) % his) * 2 + core) * cols
            if side is None:
                return full.at[:, :, pl.ds(pl.multiple_of(start, cols), cols)]
            return full.at[:, :, pl.ds(pl.multiple_of(start + side * part, part), part)]

        def mates(step):
            start = (((hi + step) % his) * 2 + 1 - core) * cols
            return full.at[:, :, pl.ds(pl.multiple_of(start, cols), cols)]

        swap = remote(half, half_in, half_sem, 0, mate)
        over = [
            remote(cross.at[0], cross_in.at[0], rs_sem, 0, up),
            remote(cross.at[1], cross_in.at[1], rs_sem, 1, down),
        ]
        near = [
            remote(rs.at[0], rs_in.at[0], rs_sem, 2, up),
            remote(rs.at[1], rs_in.at[1], rs_sem, 3, down),
        ]
        give = [remote(spot(0), spot(0), ag_sem, i, to) for i, to in enumerate((up, down))]
        take = [
            remote(spot(0), spot(step), ag_sem, i, to)
            for i, (step, to) in enumerate(((his - 1, up), (1, down)))
        ]
        pass_on = [
            remote(spot(step, side), spot(step, side), ag_sem, 2 + side, to)
            for side, (step, to) in enumerate(((his - 1, up), (1, down)))
        ]
        last_in = [
            remote(spot(0, side), spot(2, side), ag_sem, 2 + side, to)
            for side, to in enumerate((up, down))
        ]
        forward = [remote(spot(step), spot(step), fwd_sem, step, mate) for step in range(his)]
        received = [remote(spot(step), mates(step), fwd_sem, step, mate) for step in range(his)]

        def project():
            for step in range(his):
                z = (hi + step) % his
                half[step] = dot(a, w[:, block_cols(z * 2 + 1 - core)]).astype(BF16)
            swap.start()
            for step in range(his):
                z = (hi + step) % his
                pair[step] = dot(a, w[:, block_cols(z * 2 + core)])

        def far():
            swap.wait()
            for step in range(his):
                pair[step] = pair[step] + half_in[step].astype(F32)
            cross[0] = pair[2, :, :part].astype(BF16)
            cross[1] = pair[2, :, part:].astype(BF16)
            for copy in over:
                copy.start()

        def close():
            for copy in over:
                copy.wait()
            rs[0, :, :part] = (pair[1, :, :part] + cross_in[0].astype(F32)).astype(BF16)
            rs[0, :, part:] = pair[1, :, part:].astype(BF16)
            rs[1, :, :part] = pair[his - 1, :, :part].astype(BF16)
            rs[1, :, part:] = (pair[his - 1, :, part:] + cross_in[1].astype(F32)).astype(BF16)
            for copy in near:
                copy.start()

        def total():
            for copy in near:
                copy.wait()
            sums = pair[0] + rs_in[0].astype(F32) + rs_in[1].astype(F32)
            spot(0)[...] = sums.reshape(full.shape[:2] + (cols,)).astype(BF16)
            for copy in give:
                copy.start()
            forward[0].start()

        def relay():
            for side, step in enumerate((his - 1, 1)):
                take[side].wait_recv()
                pass_on[side].start()
                forward[step].start()

        def end():
            for copy in last_in:
                copy.wait_recv()
            forward[2].start()
            for copy in received:
                copy.wait_recv()
            for copy in give + pass_on + forward:
                copy.wait_send()

        return project, far, close, total, relay, end

    def tail(part, att, half, half_in, pair, rs, rs_in, full):
        a = jnp.concatenate([att[g].astype(BF16) for g in range(GROUPS)], axis=1)

        def part_full(index):
            where = block_cols(index)
            return full.at[:, where]

        swap = remote(half, half_in, half_sem, part, mate)
        scatter = [
            remote(rs.at[step], rs_in.at[step], rs_sem, part * his + step, peer_hi(step))
            for step in range(1, his)
        ]
        mine = part_full(tp)
        gather = [
            remote(mine, mine, ag_sem, part * his + step, peer_hi(step))
            for step in range(1, his)
        ]
        landed = [
            remote(
                mine,
                part_full(((hi + his - step) % his) * 2 + core),
                ag_sem,
                part * his + step,
                peer_hi(step),
            )
            for step in range(1, his)
        ]
        forward = []
        received = []
        for step in range(his):
            owner = ((hi + his - step) % his) * 2
            have, want = part_full(owner + core), part_full(owner + 1 - core)
            forward.append(remote(have, have, fwd_sem, part * his + step, mate))
            received.append(remote(have, want, fwd_sem, part * his + step, mate))

        def one():
            for step in range(his):
                z = (hi + step) % his
                half[step] = dot(a, w[:, block_cols(z * 2 + 1 - core)]).astype(BF16)
            swap.start()
            for step in range(his):
                z = (hi + step) % his
                pair[step] = dot(a, w[:, block_cols(z * 2 + core)])

        def two():
            swap.wait()
            for step in range(1, his):
                rs[step] = (pair[step] + half_in[step].astype(F32)).astype(BF16)
                scatter[step - 1].start()
            pair[0] = pair[0] + half_in[0].astype(F32)

        def three():
            for copy in scatter:
                copy.wait()
            total = pair[0]
            for step in range(1, his):
                total = total + rs_in[step].astype(F32)
            mine[...] = total.astype(BF16)
            for copy in gather:
                copy.start()
            forward[0].start()

        def four():
            for step in range(1, his):
                landed[step - 1].wait_recv()
                forward[step].start()
            for step in range(his):
                received[step].wait_recv()

        def five():
            for copy in gather:
                copy.wait_send()
            for copy in forward:
                copy.wait_send()

        return one, two, three, four, five

    load_w.wait()
    project, far, close, total_up, relay, end = ring_tail(
        att_s, s_half, s_half_in, s_pair, s_cross, s_cross_in, s_rs, s_rs_in, s_full
    )
    project()

    lane4 = lax.broadcasted_iota(jnp.int32, (GROUPS, HEAD), 1).astype(F32)

    def state(slot):
        length = arr[slot, 1, 0, PAGE - TILE :].astype(F32)[TILE - 1 :]
        flag = arr[slot, 1, 1, PAGE - TILE :].astype(F32)[TILE - 1 :]
        return length, flag == 1.0

    def dst_step(b, _):
        slots, parts0, parts1, values = [], [], [], []
        for i in range(batch):
            k = b * batch + i

            @pl.when(k > 0)
            def _():
                move(k).wait_send()

            @pl.when(k + ahead < n)
            def _():
                move(k + ahead).start()

        for i in range(batch):
            k = b * batch + i

            @pl.when(k > 0)
            def _():
                arrive(k).wait_recv()

        for i in range(batch):
            slot = partner(b * batch + i)
            slots.append(slot)
            length, moved = state(slot)
            own = rdst[slot].astype(F32)
            key1 = jnp.where(last, own[0:1].astype(BF16), arr[slot, 1, 0])
            value1 = jnp.where(last, own[1:2].astype(BF16), arr[slot, 1, 1])
            query = qd[slot].astype(BF16)
            s0 = dot_t(query, arr[slot, 0, 0]) * scale
            s1 = dot_t(query, key1) * scale
            parts0.append(jnp.where(lane4 < length, s0, NEG))
            keep1 = (lane4 + float(PAGE) < length) | (lane4 >= PAGE - 3.0)
            parts1.append(jnp.where(keep1, s1, NEG))
            values.append((arr[slot, 0, 1], value1, moved))
        for i in range(batch):
            w0, w1 = soft(parts0[i], parts1[i])
            mixed = dot(w0, values[i][0]) + dot(w1, values[i][1])
            mixed = jnp.where(values[i][2], mixed, 0.0)
            for g in range(GROUPS):
                att_d[g, pl.ds(slots[i], 1), :] = mixed[g : g + 1]
        return 0

    def fill_step(b, _):
        for i in range(batch):
            slot = partner(b * batch + i)
            length, moved = state(slot)
            length = jnp.where(moved, length, -512.0)
            own = rdst[slot].astype(F32)
            rows_in = [arr[slot, 1, c, PAGE - TILE :].astype(F32) for c in range(2)]
            for p in range(2):
                at = [(length + (j - p * PAGE)).astype(BF16) for j in range(3)]
                keep = row < at[0]
                hits = [row == spot for spot in at]
                for c in range(2):
                    rows_put = [
                        rows_in[c][TILE - 3 : TILE - 2],
                        rows_in[c][TILE - 2 : TILE - 1],
                        own[c : c + 1],
                    ]
                    block = jnp.where(keep, arr[slot, p, c], zero)
                    for hit, put in zip(hits, rows_put):
                        block = jnp.where(hit, put.astype(BF16), block)
                    cache_out[slot, p, c] = block
        return 0

    def both(b, _):
        dst_step(b, 0)
        return fill_step(b, 0)

    steps = n // batch
    marks = [steps * j // 8 for j in (0, 1, 3, 5, 6, 7, 8)]
    lax.fori_loop(marks[0], marks[1], both, 0)
    far()
    lax.fori_loop(marks[1], marks[2], both, 0)
    close()
    lax.fori_loop(marks[2], marks[3], both, 0)
    total_up()
    lax.fori_loop(marks[3], marks[4], both, 0)
    lax.fori_loop(marks[4], marks[6], dst_step, 0)

    dst_tail = tail(1, att_d, d_half, d_half_in, d_pair, d_rs, d_rs_in, d_full)
    dst_tail[0]()
    relay()
    dst_tail[1]()
    lax.fori_loop(marks[4], marks[5], fill_step, 0)
    dst_tail[2]()
    lax.fori_loop(marks[5], marks[6], fill_step, 0)
    dst_tail[3]()
    end()
    dst_tail[4]()


def place(src_in, cache_in, dst_in, src_hbm, cache_hbm, dst_hbm, sem):
    size = cache_in.shape[0] // PIECES
    copies = [
        pltpu.make_async_copy(
            cache_in.at[i * size : (i + 1) * size],
            cache_hbm.at[i * size : (i + 1) * size],
            sem.at[i],
        )
        for i in range(PIECES)
    ]
    copies.append(pltpu.make_async_copy(src_in, src_hbm, sem.at[PIECES]))
    copies.append(pltpu.make_async_copy(dst_in, dst_hbm, sem.at[PIECES + 1]))
    for copy in copies:
        copy.start()
    for copy in copies:
        copy.wait()


def shards(
    pool,
    page_table,
    lengths,
    targets,
    migrating,
    queries_src,
    new_rows,
    queries_dst,
    rows_dst,
    w_out,
):
    n = lax.axis_size("inst")
    tp_size = lax.axis_size("tp")
    his = tp_size // 2
    requests = queries_src.shape[0]
    width = w_out.shape[1]
    cols = width // tp_size
    smem = pl.BlockSpec(memory_space=pltpu.SMEM)
    vmem = pl.BlockSpec(memory_space=pltpu.VMEM)
    hbm = pl.BlockSpec(memory_space=pl.ANY)
    cache = (requests, 2, 2, PAGE, HEAD)

    def sums(rows, sent):
        return [
            pltpu.VMEM((his, rows, cols), BF16),
            pltpu.VMEM((his, rows, cols), BF16),
            pltpu.VMEM((his, rows, cols), F32),
        ] + [pltpu.VMEM((parts, rows, width), BF16) for parts, width in sent]

    dma = pltpu.SemaphoreType.DMA
    in_hbm = functools.partial(pltpu.with_memory_space_constraint, memory_space=pltpu.HBM)
    results = pl.pallas_call(
        functools.partial(kernel, n, tp_size),
        out_shape=(
            pltpu.VMEM((requests, 2, width), BF16),
            pltpu.VMEM(cache, BF16),
            pltpu.VMEM((requests, width), BF16),
        ),
        in_specs=[smem] * 4 + [vmem] * 4 + [hbm] * 2,
        out_specs=(vmem, vmem, vmem),
        scratch_shapes=[
            pltpu.VMEM(pool.shape, BF16),
            pltpu.VMEM(w_out.shape, BF16),
            pltpu.VMEM(cache, BF16),
            pltpu.VMEM(cache, BF16),
            pltpu.VMEM((requests, 2 * GROUPS, HEAD), F32),
            pltpu.VMEM((requests, GROUPS, HEAD), F32),
            pltpu.VMEM((GROUPS, 2 * requests, HEAD), F32),
            pltpu.VMEM((GROUPS, requests, HEAD), F32),
        ]
        + sums(2 * requests, [(2, cols // 2)] * 2 + [(2, cols)] * 2)
        + sums(requests, [(his, cols)] * 2)
        + [
            dma((2,)),
            dma((n,)),
            dma((n,)),
            dma((4,)),
            dma((4 * his,)),
            dma((4 * his,)),
            dma((4 * his,)),
        ],
        compiler_params=pltpu.CompilerParams(
            collective_id=0, has_side_effects=True, vmem_limit_bytes=28 * 1024 * 1024
        ),
        name="migrate",
    )(
        *map(
            in_hbm,
            (
                lengths,
                targets,
                migrating,
                page_table.T,
                queries_src,
                new_rows,
                queries_dst,
                rows_dst,
                pool,
                w_out,
            ),
        )
    )
    return pl.pallas_call(
        place,
        out_shape=tuple(pltpu.HBM(x.shape, x.dtype) for x in results),
        in_specs=[vmem] * 3,
        out_specs=(hbm,) * 3,
        scratch_shapes=[dma((PIECES + 2,))],
        compiler_params=pltpu.CompilerParams(vmem_limit_bytes=8 * 1024 * 1024),
        name="place",
    )(*(pltpu.with_memory_space_constraint(x, pltpu.VMEM) for x in results))


def solution(mesh):
    return jax.shard_map(
        shards,
        mesh=mesh,
        in_specs=(
            P("inst", None, None, "tp"),
            P("inst", None),
            P("inst"),
            P("inst"),
            P("inst"),
            P("inst", None, "tp"),
            P("inst", None, None, "tp"),
            P("inst", "tp"),
            P("inst", None, "tp"),
            P("tp", None),
        ),
        out_specs=(P("inst", None, None), P("inst", None, None, None, "tp"), P("inst", None)),
        check_vma=False,
    )
```

```python
import functools
import math

import jax
import jax.numpy as jnp
from jax import lax
from jax.experimental import pallas as pl
from jax.experimental.pallas import tpu as pltpu
from jax.sharding import PartitionSpec as P

MESH = pl.DeviceIdType.MESH
BF16 = jnp.bfloat16
F32 = jnp.float32
NEG = -1e30
HEAD = 128
PAGE = 128
GROUPS = 4
TILE = 16
PIECES = 8
MIX = 11


def xor(a, b, bits):
    total = 0
    for bit in range(bits):
        weight = 2**bit
        u, v = (a // weight) % 2, (b // weight) % 2
        total = total + (u + v - 2 * u * v) * weight
    return total


def order(k, n):
    if n != 32:
        return (k * MIX) % n
    late = k // 16
    spot = (k - 16 * late) % 8
    turn = (k - 16 * late) // 8
    hop0 = (k % 3 + 1) // 2
    hop1 = 1 - (spot % 3 + 1) // 2
    hop = (1 - late) * hop0 + late * hop1
    cross0 = k - k // 3 - 1
    cross1 = 10 + 3 * turn + spot // 3
    plane0 = k // 3
    plane1 = 6 + 5 * turn + spot - spot // 3 - 1
    count = hop * ((1 - late) * cross0 + late * cross1)
    count = count + (1 - hop) * ((1 - late) * plane0 + late * plane1)
    return ((count * MIX) % 16) * 2 + hop


def kernel(
    n,
    tp_size,
    lens,
    tgts,
    mig,
    table,
    qsrc,
    fresh,
    qdst,
    rdst,
    pool_hbm,
    w_hbm,
    s_full,
    cache_out,
    d_out,
    pool,
    w,
    send,
    arr,
    qs,
    qd,
    att_s,
    att_d,
    s_half,
    s_half_in,
    s_pair,
    s_cross,
    s_cross_in,
    s_rs,
    s_rs_in,
    e_half,
    e_half_in,
    e_pair,
    e_rs,
    e_rs_in,
    e_full,
    d_early,
    l_half,
    l_half_in,
    l_pair,
    l_parts,
    l_final,
    load_sem,
    send_sem,
    recv_sem,
    half_sem,
    rs_sem,
    ag_sem,
    fwd_sem,
    late_sem,
):
    me = lax.axis_index("inst")
    tp = lax.axis_index("tp")
    core = tp % 2
    hi = tp // 2
    his = tp_size // 2
    mate = tp + 1 - 2 * core
    bits = n.bit_length() - 1
    scale = 1.0 / math.sqrt(HEAD)
    early_rows = n * 3 // 4
    late_rows = n - early_rows
    cols = w.shape[1] // tp_size

    def peer_hi(step):
        return ((hi + step) % his) * 2 + core

    def partner(k):
        return xor(me, order(k, n), bits)

    load_pool = pltpu.make_async_copy(pool_hbm, pool, load_sem.at[0])
    load_w = pltpu.make_async_copy(w_hbm, w, load_sem.at[1])
    load_pool.start()
    barrier = pltpu.get_barrier_semaphore()

    def greet(k, _):
        pl.semaphore_signal(
            barrier, inc=1, device_id=(xor(me, k, bits), tp), device_id_type=MESH
        )
        return 0

    lax.fori_loop(1, n, greet, 0)
    pl.semaphore_signal(barrier, inc=1, device_id=(me, mate), device_id_type=MESH)
    for step in range(1, his):
        pl.semaphore_signal(barrier, inc=1, device_id=(me, peer_hi(step)), device_id_type=MESH)

    row = lax.broadcasted_iota(jnp.int32, (PAGE, HEAD), 0).astype(F32).astype(BF16)
    last = row == jnp.asarray(PAGE - 1, BF16)
    zero = jnp.zeros((PAGE, HEAD), BF16)
    tile_row = lax.broadcasted_iota(jnp.int32, (TILE, HEAD), 0).astype(F32)

    def move(k):
        peer = partner(k)
        return pltpu.make_async_remote_copy(
            src_ref=send.at[peer],
            dst_ref=arr.at[me],
            send_sem=send_sem.at[k],
            recv_sem=recv_sem.at[k],
            device_id=(peer, tp),
            device_id_type=MESH,
        )

    def arrive(k):
        peer = partner(k)
        return pltpu.make_async_remote_copy(
            src_ref=send.at[peer],
            dst_ref=arr.at[peer],
            send_sem=send_sem.at[k],
            recv_sem=recv_sem.at[k],
            device_id=(peer, tp),
            device_id_type=MESH,
        )

    def pack(k, ref):
        slot = partner(k)
        request = jnp.int32(0)
        for j in range(n):
            request = jnp.where(tgts[j] == slot, j, request)
        length = lens[request].astype(F32)
        flag = mig[request].astype(F32)
        rows_new = fresh[request].astype(F32)
        for c in range(2):
            ref[slot, 0, c] = pool[table[0, request], c]
            page = pool[table[1, request], c]
            ref[slot, 1, c, : PAGE - TILE] = page[: PAGE - TILE]
            end = jnp.where(tile_row == TILE - 3.0, rows_new[0, c : c + 1], page[PAGE - TILE :].astype(F32))
            end = jnp.where(tile_row == TILE - 2.0, rows_new[1, c : c + 1], end)
            end = jnp.where(tile_row == TILE - 1.0, length if c == 0 else flag, end)
            ref[slot, 1, c, PAGE - TILE :] = end.astype(BF16)

    q_wide = qsrc[...].astype(F32)
    for g in range(GROUPS):
        lanes = slice(g * HEAD, (g + 1) * HEAD)
        for t in range(2):
            qs[:, 2 * g + t, :] = q_wide[:, t, lanes]
        qd[:, g, :] = qdst[:, lanes].astype(F32)

    load_pool.wait()
    pl.semaphore_wait(barrier, n - 1 + his)
    load_w.start()

    def send_step(k, _):
        pack(k, send)
        move(k).start()
        return 0

    batch = min(4, n)
    ahead = min(4 * batch, n)
    lax.fori_loop(1, ahead, send_step, 0)
    pack(0, send)
    arr[me] = send[me]

    def pack_step(k, _):
        pack(k, send)
        return 0

    lax.fori_loop(ahead, n, pack_step, 0)

    def dot_t(a, b):
        return lax.dot_general(a, b, (((1,), (1,)), ((), ())), preferred_element_type=F32)

    def dot(a, b):
        return jnp.dot(a, b, preferred_element_type=F32)

    def soft(s0, s1):
        top = jnp.maximum(
            jnp.max(s0, axis=1, keepdims=True), jnp.max(s1, axis=1, keepdims=True)
        )
        e0, e1 = jnp.exp(s0 - top), jnp.exp(s1 - top)
        total = jnp.sum(e0, axis=1, keepdims=True) + jnp.sum(e1, axis=1, keepdims=True)
        return (e0 / total).astype(BF16), (e1 / total).astype(BF16)

    wide = min(8, n)
    lane8 = lax.broadcasted_iota(jnp.int32, (8, HEAD), 1)
    step8 = lax.broadcasted_iota(jnp.int32, (8, HEAD), 0) % 2
    fresh8 = (lane8 == PAGE - 3) | ((lane8 == PAGE - 2) & (step8 == 1))

    def src_step(b, _):
        parts0, parts1 = [], []
        for i in range(wide):
            request = b * wide + i
            slot = tgts[request]
            query = qs[request].astype(BF16)
            bound = lens[request]
            s0 = dot_t(query, send[slot, 0, 0]) * scale
            s1 = dot_t(query, send[slot, 1, 0]) * scale
            parts0.append(jnp.where(lane8 < bound, s0, NEG))
            parts1.append(jnp.where((lane8 + PAGE < bound) | fresh8, s1, NEG))
        w0, w1 = soft(jnp.concatenate(parts0, axis=0), jnp.concatenate(parts1, axis=0))
        for i in range(wide):
            request = b * wide + i
            slot = tgts[request]
            rows = slice(8 * i, 8 * i + 8)
            mixed = dot(w0[rows], send[slot, 0, 1]) + dot(w1[rows], send[slot, 1, 1])
            for g in range(GROUPS):
                att_s[g, pl.ds(2 * request, 2), :] = mixed[2 * g : 2 * g + 2]
        return 0

    lax.fori_loop(0, n // wide, src_step, 0)

    def remote(src, dst, sems, index, target):
        return pltpu.make_async_remote_copy(
            src_ref=src,
            dst_ref=dst,
            send_sem=sems.at[2 * index],
            recv_sem=sems.at[2 * index + 1],
            device_id=(me, target),
            device_id_type=MESH,
        )

    def block_cols(index):
        return pl.ds(pl.multiple_of(index * cols, cols), cols)

    def ring_tail(att, half, half_in, pair, cross, cross_in, rs, rs_in, full):
        a = jnp.concatenate([att[g].astype(BF16) for g in range(GROUPS)], axis=1)
        part = cols // 2
        up, down = peer_hi(1), peer_hi(his - 1)

        def spot(step, side=None):
            start = (((hi + step) % his) * 2 + core) * cols
            if side is None:
                return full.at[:, :, pl.ds(pl.multiple_of(start, cols), cols)]
            return full.at[:, :, pl.ds(pl.multiple_of(start + side * part, part), part)]

        def mates(step):
            start = (((hi + step) % his) * 2 + 1 - core) * cols
            return full.at[:, :, pl.ds(pl.multiple_of(start, cols), cols)]

        swap = remote(half, half_in, half_sem, 0, mate)
        over = [
            remote(cross.at[0], cross_in.at[0], rs_sem, 0, up),
            remote(cross.at[1], cross_in.at[1], rs_sem, 1, down),
        ]
        near = [
            remote(rs.at[0], rs_in.at[0], rs_sem, 2, up),
            remote(rs.at[1], rs_in.at[1], rs_sem, 3, down),
        ]
        give = [remote(spot(0), spot(0), ag_sem, i, to) for i, to in enumerate((up, down))]
        take = [
            remote(spot(0), spot(step), ag_sem, i, to)
            for i, (step, to) in enumerate(((his - 1, up), (1, down)))
        ]
        pass_on = [
            remote(spot(step, side), spot(step, side), ag_sem, 2 + side, to)
            for side, (step, to) in enumerate(((his - 1, up), (1, down)))
        ]
        last_in = [
            remote(spot(0, side), spot(2, side), ag_sem, 2 + side, to)
            for side, to in enumerate((up, down))
        ]
        forward = [remote(spot(step), spot(step), fwd_sem, step, mate) for step in range(his)]
        received = [remote(spot(step), mates(step), fwd_sem, step, mate) for step in range(his)]

        def project():
            for step in range(his):
                z = (hi + step) % his
                half[step] = dot(a, w[:, block_cols(z * 2 + 1 - core)]).astype(BF16)
            swap.start()
            for step in range(his):
                z = (hi + step) % his
                pair[step] = dot(a, w[:, block_cols(z * 2 + core)])

        def far():
            swap.wait()
            for step in range(his):
                pair[step] = pair[step] + half_in[step].astype(F32)
            cross[0] = pair[2, :, :part].astype(BF16)
            cross[1] = pair[2, :, part:].astype(BF16)
            for copy in over:
                copy.start()

        def close():
            for copy in over:
                copy.wait()
            rs[0, :, :part] = (pair[1, :, :part] + cross_in[0].astype(F32)).astype(BF16)
            rs[0, :, part:] = pair[1, :, part:].astype(BF16)
            rs[1, :, :part] = pair[his - 1, :, :part].astype(BF16)
            rs[1, :, part:] = (pair[his - 1, :, part:] + cross_in[1].astype(F32)).astype(BF16)
            for copy in near:
                copy.start()

        def total():
            for copy in near:
                copy.wait()
            sums = pair[0] + rs_in[0].astype(F32) + rs_in[1].astype(F32)
            spot(0)[...] = sums.reshape(full.shape[:2] + (cols,)).astype(BF16)
            for copy in give:
                copy.start()
            forward[0].start()

        def relay():
            for side, step in enumerate((his - 1, 1)):
                take[side].wait_recv()
                pass_on[side].start()
                forward[step].start()

        def end():
            for copy in last_in:
                copy.wait_recv()
            forward[2].start()
            for copy in received:
                copy.wait_recv()
            for copy in give + pass_on + forward:
                copy.wait_send()

        return project, far, close, total, relay, end

    def stack(x, parts):
        size = x.shape[1] // parts
        return jnp.concatenate([x[:, i * size : (i + 1) * size] for i in range(parts)], axis=0)

    def rows_of(att, rows):
        return jnp.concatenate([att[g, rows].astype(BF16) for g in range(GROUPS)], axis=1)

    def early_tail(att, half, half_in, pair, rs, rs_in, full):
        a = rows_of(att, slice(0, early_rows))
        swap = remote(half, half_in, half_sem, 1, mate)
        scatter = [
            remote(rs.at[step], rs_in.at[step], rs_sem, his + step, peer_hi(step))
            for step in range(1, his)
        ]
        mine = full.at[tp]
        owners = [((hi + his - step) % his) * 2 for step in range(his)]
        gather = [remote(mine, mine, ag_sem, his + step, peer_hi(step)) for step in range(1, his)]
        landed = [
            remote(mine, full.at[owners[step] + core], ag_sem, his + step, peer_hi(step))
            for step in range(1, his)
        ]
        forward, received = [], []
        for step in range(his):
            have, want = full.at[owners[step] + core], full.at[owners[step] + 1 - core]
            forward.append(remote(have, have, fwd_sem, his + step, mate))
            received.append(remote(have, want, fwd_sem, his + step, mate))

        def one():
            for step in range(his):
                z = (hi + step) % his
                half[step] = stack(dot(a, w[:, block_cols(z * 2 + 1 - core)]), 2).astype(BF16)
            swap.start()
            for step in range(his):
                z = (hi + step) % his
                pair[step] = stack(dot(a, w[:, block_cols(z * 2 + core)]), 2)

        def two():
            swap.wait()
            for step in range(1, his):
                rs[step] = (pair[step] + half_in[step].astype(F32)).astype(BF16)
                scatter[step - 1].start()
            pair[0] = pair[0] + half_in[0].astype(F32)

        def three():
            for copy in scatter:
                copy.wait()
            total = pair[0]
            for step in range(1, his):
                total = total + rs_in[step].astype(F32)
            mine[...] = total.astype(BF16)
            for copy in gather:
                copy.start()
            forward[0].start()

        def four():
            for step in range(1, his):
                landed[step - 1].wait_recv()
                forward[step].start()

        def five():
            for copy in received:
                copy.wait_recv()
            for copy in gather + forward:
                copy.wait_send()

        return one, two, three, four, five

    def late_tail(att, half, half_in, pair, parts, final):
        a = rows_of(att, slice(early_rows, n))
        swap = remote(half, half_in, late_sem, 0, mate)
        spread_out = [
            remote(parts.at[hi], parts.at[hi], late_sem, step, peer_hi(step))
            for step in range(1, his)
        ]
        spread_in = [
            remote(parts.at[hi], parts.at[(hi + his - step) % his], late_sem, step, peer_hi(step))
            for step in range(1, his)
        ]
        give = remote(final.at[core], final.at[core], late_sem, his, mate)
        take = remote(final.at[core], final.at[1 - core], late_sem, his, mate)

        def columns(side):
            blocks = [dot(a, w[:, block_cols(z * 2 + side)]) for z in range(his)]
            return stack(jnp.concatenate(blocks, axis=1), 2)

        def one():
            half[...] = columns(1 - core).astype(BF16)
            swap.start()
            pair[...] = columns(core)

        def two():
            swap.wait()
            parts[hi] = (pair[...] + half_in[...].astype(F32)).astype(BF16)
            for copy in spread_out:
                copy.start()

        def three():
            for copy in spread_in:
                copy.wait_recv()
            total = parts[0].astype(F32)
            for z in range(1, his):
                total = total + parts[z].astype(F32)
            final[core] = total.astype(BF16)
            give.start()

        def four():
            take.wait_recv()

        def five():
            for copy in spread_out:
                copy.wait_send()
            give.wait_send()

        return one, two, three, four, five

    def one_hot(first, count, skip):
        lane = lax.broadcasted_iota(jnp.int32, (n, HEAD), 1)
        owner = jnp.full((n, HEAD), -1, jnp.int32)
        for i in range(count):
            owner = jnp.where(lane == skip + i, partner(first + i), owner)
        hit = lax.broadcasted_iota(jnp.int32, (n, HEAD), 0) == owner
        return jnp.where(hit, 1.0, 0.0).astype(BF16)[:, : 2 * count]

    load_w.wait()
    project, far, close, total_up, relay, end = ring_tail(
        att_s, s_half, s_half_in, s_pair, s_cross, s_cross_in, s_rs, s_rs_in, s_full
    )
    project()

    lane4 = lax.broadcasted_iota(jnp.int32, (GROUPS, HEAD), 1).astype(F32)

    def state(slot):
        length = arr[slot, 1, 0, PAGE - TILE :].astype(F32)[TILE - 1 :]
        flag = arr[slot, 1, 1, PAGE - TILE :].astype(F32)[TILE - 1 :]
        return length, flag == 1.0

    def dst_step(b, _):
        parts0, parts1, values = [], [], []
        for i in range(batch):
            k = b * batch + i

            @pl.when(k > 0)
            def _():
                move(k).wait_send()

            @pl.when(k + ahead < n)
            def _():
                move(k + ahead).start()

        for i in range(batch):
            k = b * batch + i

            @pl.when(k > 0)
            def _():
                arrive(k).wait_recv()

        for i in range(batch):
            slot = partner(b * batch + i)
            length, moved = state(slot)
            own = rdst[slot].astype(F32)
            key1 = jnp.where(last, own[0:1].astype(BF16), arr[slot, 1, 0])
            value1 = jnp.where(last, own[1:2].astype(BF16), arr[slot, 1, 1])
            query = qd[slot].astype(BF16)
            s0 = dot_t(query, arr[slot, 0, 0]) * scale
            s1 = dot_t(query, key1) * scale
            parts0.append(jnp.where(lane4 < length, s0, NEG))
            keep1 = (lane4 + float(PAGE) < length) | (lane4 >= PAGE - 3.0)
            parts1.append(jnp.where(keep1, s1, NEG))
            values.append((arr[slot, 0, 1], value1, moved))
        for i in range(batch):
            w0, w1 = soft(parts0[i], parts1[i])
            mixed = dot(w0, values[i][0]) + dot(w1, values[i][1])
            mixed = jnp.where(values[i][2], mixed, 0.0)
            for g in range(GROUPS):
                att_d[g, pl.ds(b * batch + i, 1), :] = mixed[g : g + 1]
        return 0

    def fill_step(b, _):
        for i in range(batch):
            slot = partner(b * batch + i)
            length, moved = state(slot)
            length = jnp.where(moved, length, -512.0)
            own = rdst[slot].astype(F32)
            rows_in = [arr[slot, 1, c, PAGE - TILE :].astype(F32) for c in range(2)]
            for p in range(2):
                at = [(length + (j - p * PAGE)).astype(BF16) for j in range(3)]
                keep = row < at[0]
                hits = [row == spot for spot in at]
                for c in range(2):
                    rows_put = [
                        rows_in[c][TILE - 3 : TILE - 2],
                        rows_in[c][TILE - 2 : TILE - 1],
                        own[c : c + 1],
                    ]
                    block = jnp.where(keep, arr[slot, p, c], zero)
                    for hit, put in zip(hits, rows_put):
                        block = jnp.where(hit, put.astype(BF16), block)
                    cache_out[slot, p, c] = block
        return 0

    def both(b, _):
        dst_step(b, 0)
        return fill_step(b, 0)

    steps = n // batch
    marks = [steps * j // 8 for j in (0, 1, 3, 5, 6, 7, 8)]
    lax.fori_loop(marks[0], marks[1], both, 0)
    far()
    lax.fori_loop(marks[1], marks[2], both, 0)
    close()
    lax.fori_loop(marks[2], marks[3], both, 0)
    total_up()
    lax.fori_loop(marks[3], marks[4], dst_step, 0)
    early = early_tail(att_d, e_half, e_half_in, e_pair, e_rs, e_rs_in, e_full)
    early[0]()
    early[1]()
    lax.fori_loop(marks[4], marks[5], dst_step, 0)
    early[2]()
    relay()
    lax.fori_loop(marks[5], marks[6], dst_step, 0)
    late = late_tail(att_d, l_half, l_half_in, l_pair, l_parts, l_final)
    late[0]()
    early[3]()
    late[1]()
    lax.fori_loop(marks[3], marks[6], fill_step, 0)
    early[4]()
    size = cols // 2
    for side in range(2):
        spots = one_hot(0, early_rows, side * early_rows)
        for index in range(tp_size):
            start = index * cols + side * size
            d_early[:, start : start + size] = dot(spots, e_full[index])
    late_spots = [one_hot(early_rows, late_rows, side * late_rows) for side in range(2)]

    def set_out(side):
        for z in range(his):
            where = block_cols(z * 2 + side)
            have = l_final[side, :, (z % 2) * cols : (z % 2 + 1) * cols]
            rows_late = dot(late_spots[z // (his // 2)], have)
            d_out[:, where] = (d_early[:, where] + rows_late).astype(BF16)

    late[2]()
    set_out(core)
    late[3]()
    set_out(1 - core)
    end()
    late[4]()


def place(src_in, cache_in, dst_in, src_hbm, cache_hbm, dst_hbm, sem):
    size = cache_in.shape[0] // PIECES
    copies = [
        pltpu.make_async_copy(
            cache_in.at[i * size : (i + 1) * size],
            cache_hbm.at[i * size : (i + 1) * size],
            sem.at[i],
        )
        for i in range(PIECES)
    ]
    copies.append(pltpu.make_async_copy(src_in, src_hbm, sem.at[PIECES]))
    copies.append(pltpu.make_async_copy(dst_in, dst_hbm, sem.at[PIECES + 1]))
    for copy in copies:
        copy.start()
    for copy in copies:
        copy.wait()


def shards(
    pool,
    page_table,
    lengths,
    targets,
    migrating,
    queries_src,
    new_rows,
    queries_dst,
    rows_dst,
    w_out,
):
    n = lax.axis_size("inst")
    tp_size = lax.axis_size("tp")
    his = tp_size // 2
    requests = queries_src.shape[0]
    width = w_out.shape[1]
    cols = width // tp_size
    smem = pl.BlockSpec(memory_space=pltpu.SMEM)
    vmem = pl.BlockSpec(memory_space=pltpu.VMEM)
    hbm = pl.BlockSpec(memory_space=pl.ANY)
    cache = (requests, 2, 2, PAGE, HEAD)
    early = (requests // 4 * 6, cols // 2)
    late = (requests // 4 * 2, width // 4)

    def sums(rows, sent):
        return [
            pltpu.VMEM((his, rows, cols), BF16),
            pltpu.VMEM((his, rows, cols), BF16),
            pltpu.VMEM((his, rows, cols), F32),
        ] + [pltpu.VMEM((parts, rows, width), BF16) for parts, width in sent]

    dma = pltpu.SemaphoreType.DMA
    in_hbm = functools.partial(pltpu.with_memory_space_constraint, memory_space=pltpu.HBM)
    results = pl.pallas_call(
        functools.partial(kernel, n, tp_size),
        out_shape=(
            pltpu.VMEM((requests, 2, width), BF16),
            pltpu.VMEM(cache, BF16),
            pltpu.VMEM((requests, width), BF16),
        ),
        in_specs=[smem] * 4 + [vmem] * 4 + [hbm] * 2,
        out_specs=(vmem, vmem, vmem),
        scratch_shapes=[
            pltpu.VMEM(pool.shape, BF16),
            pltpu.VMEM(w_out.shape, BF16),
            pltpu.VMEM(cache, BF16),
            pltpu.VMEM(cache, BF16),
            pltpu.VMEM((requests, 2 * GROUPS, HEAD), F32),
            pltpu.VMEM((requests, GROUPS, HEAD), F32),
            pltpu.VMEM((GROUPS, 2 * requests, HEAD), F32),
            pltpu.VMEM((GROUPS, requests, HEAD), F32),
        ]
        + sums(2 * requests, [(2, cols // 2)] * 2 + [(2, cols)] * 2)
        + [
            pltpu.VMEM((his,) + early, BF16),
            pltpu.VMEM((his,) + early, BF16),
            pltpu.VMEM((his,) + early, F32),
            pltpu.VMEM((his,) + early, BF16),
            pltpu.VMEM((his,) + early, BF16),
            pltpu.VMEM((tp_size,) + early, BF16),
            pltpu.VMEM((requests, width), F32),
            pltpu.VMEM(late, BF16),
            pltpu.VMEM(late, BF16),
            pltpu.VMEM(late, F32),
            pltpu.VMEM((his,) + late, BF16),
            pltpu.VMEM((2,) + late, BF16),
        ]
        + [
            dma((2,)),
            dma((n,)),
            dma((n,)),
            dma((4,)),
            dma((4 * his,)),
            dma((4 * his,)),
            dma((4 * his,)),
            dma((2 * his + 2,)),
        ],
        compiler_params=pltpu.CompilerParams(
            collective_id=0, has_side_effects=True, vmem_limit_bytes=28 * 1024 * 1024
        ),
        name="migrate",
    )(
        *map(
            in_hbm,
            (
                lengths,
                targets,
                migrating,
                page_table.T,
                queries_src,
                new_rows,
                queries_dst,
                rows_dst,
                pool,
                w_out,
            ),
        )
    )
    return pl.pallas_call(
        place,
        out_shape=tuple(pltpu.HBM(x.shape, x.dtype) for x in results),
        in_specs=[vmem] * 3,
        out_specs=(hbm,) * 3,
        scratch_shapes=[dma((PIECES + 2,))],
        compiler_params=pltpu.CompilerParams(vmem_limit_bytes=8 * 1024 * 1024),
        name="place",
    )(*(pltpu.with_memory_space_constraint(x, pltpu.VMEM) for x in results))


def solution(mesh):
    return jax.shard_map(
        shards,
        mesh=mesh,
        in_specs=(
            P("inst", None, None, "tp"),
            P("inst", None),
            P("inst"),
            P("inst"),
            P("inst"),
            P("inst", None, "tp"),
            P("inst", None, None, "tp"),
            P("inst", "tp"),
            P("inst", None, "tp"),
            P("tp", None),
        ),
        out_specs=(P("inst", None, None), P("inst", None, None, None, "tp"), P("inst", None)),
        check_vma=False,
    )
```

```python
import functools
import math

import jax
import jax.numpy as jnp
from jax import lax
from jax.experimental import pallas as pl
from jax.experimental.pallas import tpu as pltpu
from jax.sharding import PartitionSpec as P

MESH = pl.DeviceIdType.MESH
BF16 = jnp.bfloat16
F32 = jnp.float32
NEG = -1e30
HEAD = 128
PAGE = 128
GROUPS = 4
TILE = 16
PIECES = 8
MIX = 11


def xor(a, b, bits):
    total = 0
    for bit in range(bits):
        weight = 2**bit
        u, v = (a // weight) % 2, (b // weight) % 2
        total = total + (u + v - 2 * u * v) * weight
    return total


def order(k, n):
    if n != 32:
        return (k * MIX) % n
    late = k // 16
    spot = (k - 16 * late) % 8
    turn = (k - 16 * late) // 8
    hop0 = (k % 3 + 1) // 2
    hop1 = 1 - (spot % 3 + 1) // 2
    hop = (1 - late) * hop0 + late * hop1
    cross0 = k - k // 3 - 1
    cross1 = 10 + 3 * turn + spot // 3
    plane0 = k // 3
    plane1 = 6 + 5 * turn + spot - spot // 3 - 1
    count = hop * ((1 - late) * cross0 + late * cross1)
    count = count + (1 - hop) * ((1 - late) * plane0 + late * plane1)
    return ((count * MIX) % 16) * 2 + hop


def kernel(
    n,
    tp_size,
    lens,
    tgts,
    mig,
    table,
    qsrc,
    fresh,
    qdst,
    rdst,
    pool_hbm,
    w_hbm,
    s_full,
    cache_out,
    d_full,
    pool,
    w,
    send,
    arr,
    qs,
    qd,
    att_s,
    att_d,
    s_half,
    s_half_in,
    s_pair,
    s_cross,
    s_cross_in,
    s_rs,
    s_rs_in,
    d_half,
    d_half_in,
    d_pair,
    d_rs,
    d_rs_in,
    load_sem,
    send_sem,
    recv_sem,
    half_sem,
    rs_sem,
    ag_sem,
    fwd_sem,
):
    me = lax.axis_index("inst")
    tp = lax.axis_index("tp")
    core = tp % 2
    hi = tp // 2
    his = tp_size // 2
    mate = tp + 1 - 2 * core
    bits = n.bit_length() - 1
    scale = 1.0 / math.sqrt(HEAD)
    cols = w.shape[1] // tp_size

    def peer_hi(step):
        return ((hi + step) % his) * 2 + core

    def partner(k):
        return xor(me, order(k, n), bits)

    load_pool = pltpu.make_async_copy(pool_hbm, pool, load_sem.at[0])
    load_w = pltpu.make_async_copy(w_hbm, w, load_sem.at[1])
    load_pool.start()
    barrier = pltpu.get_barrier_semaphore()

    def greet(k, _):
        pl.semaphore_signal(
            barrier, inc=1, device_id=(xor(me, k, bits), tp), device_id_type=MESH
        )
        return 0

    lax.fori_loop(1, n, greet, 0)
    pl.semaphore_signal(barrier, inc=1, device_id=(me, mate), device_id_type=MESH)
    for step in range(1, his):
        pl.semaphore_signal(barrier, inc=1, device_id=(me, peer_hi(step)), device_id_type=MESH)

    row = lax.broadcasted_iota(jnp.int32, (PAGE, HEAD), 0).astype(F32).astype(BF16)
    last = row == jnp.asarray(PAGE - 1, BF16)
    zero = jnp.zeros((PAGE, HEAD), BF16)
    tile_row = lax.broadcasted_iota(jnp.int32, (TILE, HEAD), 0).astype(F32)

    def move(k):
        peer = partner(k)
        return pltpu.make_async_remote_copy(
            src_ref=send.at[peer],
            dst_ref=arr.at[me],
            send_sem=send_sem.at[k],
            recv_sem=recv_sem.at[k],
            device_id=(peer, tp),
            device_id_type=MESH,
        )

    def launch(k):
        peer = partner(k)
        for p in range(2):
            for c in range(2):
                pltpu.make_async_remote_copy(
                    src_ref=send.at[peer, p, c],
                    dst_ref=arr.at[me, p, c],
                    send_sem=send_sem.at[k],
                    recv_sem=recv_sem.at[k],
                    device_id=(peer, tp),
                    device_id_type=MESH,
                ).start()

    def arrive(k):
        peer = partner(k)
        return pltpu.make_async_remote_copy(
            src_ref=send.at[peer],
            dst_ref=arr.at[peer],
            send_sem=send_sem.at[k],
            recv_sem=recv_sem.at[k],
            device_id=(peer, tp),
            device_id_type=MESH,
        )

    def pack(k, ref):
        slot = partner(k)
        request = jnp.int32(0)
        for j in range(n):
            request = jnp.where(tgts[j] == slot, j, request)
        length = lens[request].astype(F32)
        flag = mig[request].astype(F32)
        rows_new = fresh[request].astype(F32)
        for c in range(2):
            ref[slot, 0, c] = pool[table[0, request], c]
            page = pool[table[1, request], c]
            ref[slot, 1, c, : PAGE - TILE] = page[: PAGE - TILE]
            end = jnp.where(tile_row == TILE - 3.0, rows_new[0, c : c + 1], page[PAGE - TILE :].astype(F32))
            end = jnp.where(tile_row == TILE - 2.0, rows_new[1, c : c + 1], end)
            end = jnp.where(tile_row == TILE - 1.0, length if c == 0 else flag, end)
            ref[slot, 1, c, PAGE - TILE :] = end.astype(BF16)

    q_wide = qsrc[...].astype(F32)
    for g in range(GROUPS):
        lanes = slice(g * HEAD, (g + 1) * HEAD)
        for t in range(2):
            qs[:, 2 * g + t, :] = q_wide[:, t, lanes]
        qd[:, g, :] = qdst[:, lanes].astype(F32)

    load_pool.wait()
    load_w.start()

    def send_step(k, _):
        pack(k, send)
        launch(k)
        return 0

    def launch_step(k, _):
        launch(k)
        return 0

    def pack_step(k, _):
        pack(k, send)
        return 0

    batch = min(4, n)
    ahead = min(4 * batch, n)
    ready = min(9, n)
    lax.fori_loop(0, ready, pack_step, 0)
    pl.semaphore_wait(barrier, n - 1 + his)
    lax.fori_loop(1, ready, launch_step, 0)
    lax.fori_loop(ready, ahead, send_step, 0)
    lax.fori_loop(ahead, n, pack_step, 0)
    arr[me] = send[me]

    def dot_t(a, b):
        return lax.dot_general(a, b, (((1,), (1,)), ((), ())), preferred_element_type=F32)

    def dot(a, b):
        return jnp.dot(a, b, preferred_element_type=F32)

    def soft(s0, s1):
        top = jnp.maximum(
            jnp.max(s0, axis=1, keepdims=True), jnp.max(s1, axis=1, keepdims=True)
        )
        e0, e1 = jnp.exp(s0 - top), jnp.exp(s1 - top)
        total = jnp.sum(e0, axis=1, keepdims=True) + jnp.sum(e1, axis=1, keepdims=True)
        return (e0 / total).astype(BF16), (e1 / total).astype(BF16)

    wide = min(8, n)
    lane8 = lax.broadcasted_iota(jnp.int32, (8, HEAD), 1)
    step8 = lax.broadcasted_iota(jnp.int32, (8, HEAD), 0) % 2
    fresh8 = (lane8 == PAGE - 3) | ((lane8 == PAGE - 2) & (step8 == 1))

    def src_step(b, _):
        parts0, parts1 = [], []
        for i in range(wide):
            request = b * wide + i
            slot = tgts[request]
            query = qs[request].astype(BF16)
            bound = lens[request]
            s0 = dot_t(query, send[slot, 0, 0]) * scale
            s1 = dot_t(query, send[slot, 1, 0]) * scale
            parts0.append(jnp.where(lane8 < bound, s0, NEG))
            parts1.append(jnp.where((lane8 + PAGE < bound) | fresh8, s1, NEG))
        w0, w1 = soft(jnp.concatenate(parts0, axis=0), jnp.concatenate(parts1, axis=0))
        for i in range(wide):
            request = b * wide + i
            slot = tgts[request]
            rows = slice(8 * i, 8 * i + 8)
            mixed = dot(w0[rows], send[slot, 0, 1]) + dot(w1[rows], send[slot, 1, 1])
            for g in range(GROUPS):
                att_s[g, pl.ds(2 * request, 2), :] = mixed[2 * g : 2 * g + 2]
        return 0

    lax.fori_loop(0, n // wide, src_step, 0)

    def remote(src, dst, sems, index, target):
        return pltpu.make_async_remote_copy(
            src_ref=src,
            dst_ref=dst,
            send_sem=sems.at[2 * index],
            recv_sem=sems.at[2 * index + 1],
            device_id=(me, target),
            device_id_type=MESH,
        )

    def block_cols(index):
        return pl.ds(pl.multiple_of(index * cols, cols), cols)

    def ring_tail(att, half, half_in, pair, cross, cross_in, rs, rs_in, full):
        a = jnp.concatenate([att[g].astype(BF16) for g in range(GROUPS)], axis=1)
        part = cols // 2
        up, down = peer_hi(1), peer_hi(his - 1)

        def spot(step, side=None):
            start = (((hi + step) % his) * 2 + core) * cols
            if side is None:
                return full.at[:, :, pl.ds(pl.multiple_of(start, cols), cols)]
            return full.at[:, :, pl.ds(pl.multiple_of(start + side * part, part), part)]

        def mates(step):
            start = (((hi + step) % his) * 2 + 1 - core) * cols
            return full.at[:, :, pl.ds(pl.multiple_of(start, cols), cols)]

        swap = remote(half, half_in, half_sem, 0, mate)
        over = [
            remote(cross.at[0], cross_in.at[0], rs_sem, 0, up),
            remote(cross.at[1], cross_in.at[1], rs_sem, 1, down),
        ]
        near = [
            remote(rs.at[0], rs_in.at[0], rs_sem, 2, up),
            remote(rs.at[1], rs_in.at[1], rs_sem, 3, down),
        ]
        give = [remote(spot(0), spot(0), ag_sem, i, to) for i, to in enumerate((up, down))]
        take = [
            remote(spot(0), spot(step), ag_sem, i, to)
            for i, (step, to) in enumerate(((his - 1, up), (1, down)))
        ]
        pass_on = [
            remote(spot(step, side), spot(step, side), ag_sem, 2 + side, to)
            for side, (step, to) in enumerate(((his - 1, up), (1, down)))
        ]
        last_in = [
            remote(spot(0, side), spot(2, side), ag_sem, 2 + side, to)
            for side, to in enumerate((up, down))
        ]
        forward = [remote(spot(step), spot(step), fwd_sem, step, mate) for step in range(his)]
        received = [remote(spot(step), mates(step), fwd_sem, step, mate) for step in range(his)]

        def project():
            for step in range(his):
                z = (hi + step) % his
                half[step] = dot(a, w[:, block_cols(z * 2 + 1 - core)]).astype(BF16)
            swap.start()
            for step in range(his):
                z = (hi + step) % his
                pair[step] = dot(a, w[:, block_cols(z * 2 + core)])

        def far():
            swap.wait()
            for step in range(his):
                pair[step] = pair[step] + half_in[step].astype(F32)
            cross[0] = pair[2, :, :part].astype(BF16)
            cross[1] = pair[2, :, part:].astype(BF16)
            for copy in over:
                copy.start()

        def close():
            for copy in over:
                copy.wait()
            rs[0, :, :part] = (pair[1, :, :part] + cross_in[0].astype(F32)).astype(BF16)
            rs[0, :, part:] = pair[1, :, part:].astype(BF16)
            rs[1, :, :part] = pair[his - 1, :, :part].astype(BF16)
            rs[1, :, part:] = (pair[his - 1, :, part:] + cross_in[1].astype(F32)).astype(BF16)
            for copy in near:
                copy.start()

        def total():
            for copy in near:
                copy.wait()
            sums = pair[0] + rs_in[0].astype(F32) + rs_in[1].astype(F32)
            spot(0)[...] = sums.reshape(full.shape[:2] + (cols,)).astype(BF16)
            for copy in give:
                copy.start()
            forward[0].start()

        def relay():
            for side, step in enumerate((his - 1, 1)):
                take[side].wait_recv()
                pass_on[side].start()
                forward[step].start()

        def end():
            for copy in last_in:
                copy.wait_recv()
            forward[2].start()
            for copy in received:
                copy.wait_recv()
            for copy in give + pass_on + forward:
                copy.wait_send()

        return project, far, close, total, relay, end

    def tail(part, att, half, half_in, pair, rs, rs_in, full):
        a = jnp.concatenate([att[g].astype(BF16) for g in range(GROUPS)], axis=1)

        def part_full(index):
            where = block_cols(index)
            return full.at[:, where]

        swap = remote(half, half_in, half_sem, part, mate)
        scatter = [
            remote(rs.at[step], rs_in.at[step], rs_sem, part * his + step, peer_hi(step))
            for step in range(1, his)
        ]
        mine = part_full(tp)
        gather = [
            remote(mine, mine, ag_sem, part * his + step, peer_hi(step))
            for step in range(1, his)
        ]
        landed = [
            remote(
                mine,
                part_full(((hi + his - step) % his) * 2 + core),
                ag_sem,
                part * his + step,
                peer_hi(step),
            )
            for step in range(1, his)
        ]
        forward = []
        received = []
        for step in range(his):
            owner = ((hi + his - step) % his) * 2
            have, want = part_full(owner + core), part_full(owner + 1 - core)
            forward.append(remote(have, have, fwd_sem, part * his + step, mate))
            received.append(remote(have, want, fwd_sem, part * his + step, mate))

        def one():
            for step in range(his):
                z = (hi + step) % his
                half[step] = dot(a, w[:, block_cols(z * 2 + 1 - core)]).astype(BF16)
            swap.start()
            for step in range(his):
                z = (hi + step) % his
                pair[step] = dot(a, w[:, block_cols(z * 2 + core)])

        def two():
            swap.wait()
            for step in range(1, his):
                rs[step] = (pair[step] + half_in[step].astype(F32)).astype(BF16)
                scatter[step - 1].start()
            pair[0] = pair[0] + half_in[0].astype(F32)

        def three():
            for copy in scatter:
                copy.wait()
            total = pair[0]
            for step in range(1, his):
                total = total + rs_in[step].astype(F32)
            mine[...] = total.astype(BF16)
            for copy in gather:
                copy.start()
            forward[0].start()

        def four():
            for step in range(1, his):
                landed[step - 1].wait_recv()
                forward[step].start()
            for step in range(his):
                received[step].wait_recv()

        def five():
            for copy in gather:
                copy.wait_send()
            for copy in forward:
                copy.wait_send()

        return one, two, three, four, five

    load_w.wait()
    project, far, close, total_up, relay, end = ring_tail(
        att_s, s_half, s_half_in, s_pair, s_cross, s_cross_in, s_rs, s_rs_in, s_full
    )
    project()

    lane4 = lax.broadcasted_iota(jnp.int32, (GROUPS, HEAD), 1).astype(F32)

    def state(slot):
        length = arr[slot, 1, 0, PAGE - TILE :].astype(F32)[TILE - 1 :]
        flag = arr[slot, 1, 1, PAGE - TILE :].astype(F32)[TILE - 1 :]
        return length, flag == 1.0

    def dst_step(b, _):
        slots, parts0, parts1, values = [], [], [], []
        for i in range(batch):
            k = b * batch + i

            @pl.when(k > 0)
            def _():
                move(k).wait_send()

            @pl.when(k + ahead < n)
            def _():
                launch(k + ahead)

        for i in range(batch):
            k = b * batch + i

            @pl.when(k > 0)
            def _():
                arrive(k).wait_recv()

        for i in range(batch):
            slot = partner(b * batch + i)
            slots.append(slot)
            length, moved = state(slot)
            own = rdst[slot].astype(F32)
            key1 = jnp.where(last, own[0:1].astype(BF16), arr[slot, 1, 0])
            value1 = jnp.where(last, own[1:2].astype(BF16), arr[slot, 1, 1])
            query = qd[slot].astype(BF16)
            s0 = dot_t(query, arr[slot, 0, 0]) * scale
            s1 = dot_t(query, key1) * scale
            parts0.append(jnp.where(lane4 < length, s0, NEG))
            keep1 = (lane4 + float(PAGE) < length) | (lane4 >= PAGE - 3.0)
            parts1.append(jnp.where(keep1, s1, NEG))
            values.append((arr[slot, 0, 1], value1, moved))
        for i in range(batch):
            w0, w1 = soft(parts0[i], parts1[i])
            mixed = dot(w0, values[i][0]) + dot(w1, values[i][1])
            mixed = jnp.where(values[i][2], mixed, 0.0)
            for g in range(GROUPS):
                att_d[g, pl.ds(slots[i], 1), :] = mixed[g : g + 1]
        return 0

    def fill_step(b, _):
        for i in range(batch):
            slot = partner(b * batch + i)
            length, moved = state(slot)
            length = jnp.where(moved, length, -512.0)
            own = rdst[slot].astype(F32)
            rows_in = [arr[slot, 1, c, PAGE - TILE :].astype(F32) for c in range(2)]
            for p in range(2):
                at = [(length + (j - p * PAGE)).astype(BF16) for j in range(3)]
                keep = row < at[0]
                hits = [row == spot for spot in at]
                for c in range(2):
                    rows_put = [
                        rows_in[c][TILE - 3 : TILE - 2],
                        rows_in[c][TILE - 2 : TILE - 1],
                        own[c : c + 1],
                    ]
                    block = jnp.where(keep, arr[slot, p, c], zero)
                    for hit, put in zip(hits, rows_put):
                        block = jnp.where(hit, put.astype(BF16), block)
                    cache_out[slot, p, c] = block
        return 0

    def both(b, _):
        dst_step(b, 0)
        return fill_step(b, 0)

    steps = n // batch
    marks = [steps * j // 8 for j in (0, 1, 3, 5, 6, 7, 8)]
    lax.fori_loop(marks[0], marks[1], both, 0)
    far()
    lax.fori_loop(marks[1], marks[2], both, 0)
    close()
    lax.fori_loop(marks[2], marks[3], both, 0)
    total_up()
    lax.fori_loop(marks[3], marks[4], both, 0)
    lax.fori_loop(marks[4], marks[6], dst_step, 0)

    dst_tail = tail(1, att_d, d_half, d_half_in, d_pair, d_rs, d_rs_in, d_full)
    dst_tail[0]()
    relay()
    dst_tail[1]()
    lax.fori_loop(marks[4], marks[5], fill_step, 0)
    dst_tail[2]()
    lax.fori_loop(marks[5], marks[6], fill_step, 0)
    dst_tail[3]()
    end()
    dst_tail[4]()


def place(src_in, cache_in, dst_in, src_hbm, cache_hbm, dst_hbm, sem):
    size = cache_in.shape[0] // PIECES
    copies = [
        pltpu.make_async_copy(
            cache_in.at[i * size : (i + 1) * size],
            cache_hbm.at[i * size : (i + 1) * size],
            sem.at[i],
        )
        for i in range(PIECES)
    ]
    copies.append(pltpu.make_async_copy(src_in, src_hbm, sem.at[PIECES]))
    copies.append(pltpu.make_async_copy(dst_in, dst_hbm, sem.at[PIECES + 1]))
    for copy in copies:
        copy.start()
    for copy in copies:
        copy.wait()


def shards(
    pool,
    page_table,
    lengths,
    targets,
    migrating,
    queries_src,
    new_rows,
    queries_dst,
    rows_dst,
    w_out,
):
    n = lax.axis_size("inst")
    tp_size = lax.axis_size("tp")
    his = tp_size // 2
    requests = queries_src.shape[0]
    width = w_out.shape[1]
    cols = width // tp_size
    smem = pl.BlockSpec(memory_space=pltpu.SMEM)
    vmem = pl.BlockSpec(memory_space=pltpu.VMEM)
    hbm = pl.BlockSpec(memory_space=pl.ANY)
    cache = (requests, 2, 2, PAGE, HEAD)

    def sums(rows, sent):
        return [
            pltpu.VMEM((his, rows, cols), BF16),
            pltpu.VMEM((his, rows, cols), BF16),
            pltpu.VMEM((his, rows, cols), F32),
        ] + [pltpu.VMEM((parts, rows, width), BF16) for parts, width in sent]

    dma = pltpu.SemaphoreType.DMA
    in_hbm = functools.partial(pltpu.with_memory_space_constraint, memory_space=pltpu.HBM)
    results = pl.pallas_call(
        functools.partial(kernel, n, tp_size),
        out_shape=(
            pltpu.VMEM((requests, 2, width), BF16),
            pltpu.VMEM(cache, BF16),
            pltpu.VMEM((requests, width), BF16),
        ),
        in_specs=[smem] * 4 + [vmem] * 4 + [hbm] * 2,
        out_specs=(vmem, vmem, vmem),
        scratch_shapes=[
            pltpu.VMEM(pool.shape, BF16),
            pltpu.VMEM(w_out.shape, BF16),
            pltpu.VMEM(cache, BF16),
            pltpu.VMEM(cache, BF16),
            pltpu.VMEM((requests, 2 * GROUPS, HEAD), F32),
            pltpu.VMEM((requests, GROUPS, HEAD), F32),
            pltpu.VMEM((GROUPS, 2 * requests, HEAD), F32),
            pltpu.VMEM((GROUPS, requests, HEAD), F32),
        ]
        + sums(2 * requests, [(2, cols // 2)] * 2 + [(2, cols)] * 2)
        + sums(requests, [(his, cols)] * 2)
        + [
            dma((2,)),
            dma((n,)),
            dma((n,)),
            dma((4,)),
            dma((4 * his,)),
            dma((4 * his,)),
            dma((4 * his,)),
        ],
        compiler_params=pltpu.CompilerParams(
            collective_id=0, has_side_effects=True, vmem_limit_bytes=28 * 1024 * 1024
        ),
        name="migrate",
    )(
        *map(
            in_hbm,
            (
                lengths,
                targets,
                migrating,
                page_table.T,
                queries_src,
                new_rows,
                queries_dst,
                rows_dst,
                pool,
                w_out,
            ),
        )
    )
    return pl.pallas_call(
        place,
        out_shape=tuple(pltpu.HBM(x.shape, x.dtype) for x in results),
        in_specs=[vmem] * 3,
        out_specs=(hbm,) * 3,
        scratch_shapes=[dma((PIECES + 2,))],
        compiler_params=pltpu.CompilerParams(vmem_limit_bytes=8 * 1024 * 1024),
        name="place",
    )(*(pltpu.with_memory_space_constraint(x, pltpu.VMEM) for x in results))


def solution(mesh):
    return jax.shard_map(
        shards,
        mesh=mesh,
        in_specs=(
            P("inst", None, None, "tp"),
            P("inst", None),
            P("inst"),
            P("inst"),
            P("inst"),
            P("inst", None, "tp"),
            P("inst", None, None, "tp"),
            P("inst", "tp"),
            P("inst", None, "tp"),
            P("tp", None),
        ),
        out_specs=(P("inst", None, None), P("inst", None, None, None, "tp"), P("inst", None)),
        check_vma=False,
    )
```

```python
import functools
import math

import jax
import jax.numpy as jnp
from jax import lax
from jax.experimental import pallas as pl
from jax.experimental.pallas import tpu as pltpu
from jax.sharding import PartitionSpec as P

MESH = pl.DeviceIdType.MESH
BF16 = jnp.bfloat16
F32 = jnp.float32
NEG = -1e30
HEAD = 128
PAGE = 128
GROUPS = 4
TILE = 16
PIECES = 8
MIX = 11


def xor(a, b, bits):
    total = 0
    for bit in range(bits):
        weight = 2**bit
        u, v = (a // weight) % 2, (b // weight) % 2
        total = total + (u + v - 2 * u * v) * weight
    return total


def order(k, n):
    if n != 32:
        return (k * MIX) % n
    late = k // 16
    spot = (k - 16 * late) % 8
    turn = (k - 16 * late) // 8
    hop0 = (k % 3 + 1) // 2
    hop1 = 1 - (spot % 3 + 1) // 2
    hop = (1 - late) * hop0 + late * hop1
    cross0 = k - k // 3 - 1
    cross1 = 10 + 3 * turn + spot // 3
    plane0 = k // 3
    plane1 = 6 + 5 * turn + spot - spot // 3 - 1
    count = hop * ((1 - late) * cross0 + late * cross1)
    count = count + (1 - hop) * ((1 - late) * plane0 + late * plane1)
    return ((count * MIX) % 16) * 2 + hop


def kernel(
    n,
    tp_size,
    lens,
    tgts,
    mig,
    table,
    qsrc,
    fresh,
    qdst,
    rdst,
    pool_hbm,
    w_hbm,
    s_full,
    cache_out,
    d_full,
    pool,
    w,
    send,
    arr,
    qs,
    qd,
    att_s,
    att_d,
    s_half,
    s_half_in,
    s_pair,
    s_cross,
    s_cross_in,
    s_rs,
    s_rs_in,
    d_half,
    d_half_in,
    d_pair,
    d_rs,
    d_rs_in,
    load_sem,
    send_sem,
    recv_sem,
    half_sem,
    rs_sem,
    ag_sem,
    fwd_sem,
):
    me = lax.axis_index("inst")
    tp = lax.axis_index("tp")
    core = tp % 2
    hi = tp // 2
    his = tp_size // 2
    mate = tp + 1 - 2 * core
    bits = n.bit_length() - 1
    scale = 1.0 / math.sqrt(HEAD)
    cols = w.shape[1] // tp_size

    def peer_hi(step):
        return ((hi + step) % his) * 2 + core

    def partner(k):
        return xor(me, order(k, n), bits)

    load_pool = pltpu.make_async_copy(pool_hbm, pool, load_sem.at[0])
    load_w = pltpu.make_async_copy(w_hbm, w, load_sem.at[1])
    load_pool.start()
    barrier = pltpu.get_barrier_semaphore()

    def greet(k, _):
        pl.semaphore_signal(
            barrier, inc=1, device_id=(xor(me, k, bits), tp), device_id_type=MESH
        )
        return 0

    lax.fori_loop(1, n, greet, 0)
    pl.semaphore_signal(barrier, inc=1, device_id=(me, mate), device_id_type=MESH)
    for step in range(1, his):
        pl.semaphore_signal(barrier, inc=1, device_id=(me, peer_hi(step)), device_id_type=MESH)

    row = lax.broadcasted_iota(jnp.int32, (PAGE, HEAD), 0).astype(F32).astype(BF16)
    last = row == jnp.asarray(PAGE - 1, BF16)
    zero = jnp.zeros((PAGE, HEAD), BF16)
    tile_row = lax.broadcasted_iota(jnp.int32, (TILE, HEAD), 0).astype(F32)

    def move(k):
        peer = partner(k)
        return pltpu.make_async_remote_copy(
            src_ref=send.at[peer],
            dst_ref=arr.at[me],
            send_sem=send_sem.at[k],
            recv_sem=recv_sem.at[k],
            device_id=(peer, tp),
            device_id_type=MESH,
        )

    def launch(k):
        peer = partner(k)
        for p in range(2):
            for c in range(2):
                pltpu.make_async_remote_copy(
                    src_ref=send.at[peer, p, c],
                    dst_ref=arr.at[me, p, c],
                    send_sem=send_sem.at[k],
                    recv_sem=recv_sem.at[k],
                    device_id=(peer, tp),
                    device_id_type=MESH,
                ).start()

    def arrive(k):
        peer = partner(k)
        return pltpu.make_async_remote_copy(
            src_ref=send.at[peer],
            dst_ref=arr.at[peer],
            send_sem=send_sem.at[k],
            recv_sem=recv_sem.at[k],
            device_id=(peer, tp),
            device_id_type=MESH,
        )

    def pack(k, ref):
        slot = partner(k)
        request = jnp.int32(0)
        for j in range(n):
            request = jnp.where(tgts[j] == slot, j, request)
        length = lens[request].astype(F32)
        flag = mig[request].astype(F32)
        rows_new = fresh[request].astype(F32)
        for c in range(2):
            ref[slot, 0, c] = pool[table[0, request], c]
            page = pool[table[1, request], c]
            ref[slot, 1, c, : PAGE - TILE] = page[: PAGE - TILE]
            end = jnp.where(tile_row == TILE - 3.0, rows_new[0, c : c + 1], page[PAGE - TILE :].astype(F32))
            end = jnp.where(tile_row == TILE - 2.0, rows_new[1, c : c + 1], end)
            end = jnp.where(tile_row == TILE - 1.0, length if c == 0 else flag, end)
            ref[slot, 1, c, PAGE - TILE :] = end.astype(BF16)

    q_wide = qsrc[...].astype(F32)
    for g in range(GROUPS):
        lanes = slice(g * HEAD, (g + 1) * HEAD)
        for t in range(2):
            qs[:, 2 * g + t, :] = q_wide[:, t, lanes]
        qd[:, g, :] = qdst[:, lanes].astype(F32)

    load_pool.wait()
    load_w.start()

    def send_step(k, _):
        pack(k, send)
        launch(k)
        return 0

    def launch_step(k, _):
        launch(k)
        return 0

    def pack_step(k, _):
        pack(k, send)
        return 0

    batch = min(4, n)
    ahead = min(4 * batch, n)
    ready = min(9, n)
    lax.fori_loop(0, ready, pack_step, 0)
    pl.semaphore_wait(barrier, n - 1 + his)
    lax.fori_loop(1, ready, launch_step, 0)
    lax.fori_loop(ready, ahead, send_step, 0)
    lax.fori_loop(ahead, n, pack_step, 0)
    arr[me] = send[me]

    def dot_t(a, b):
        return lax.dot_general(a, b, (((1,), (1,)), ((), ())), preferred_element_type=F32)

    def dot(a, b):
        return jnp.dot(a, b, preferred_element_type=F32)

    def soft(s0, s1):
        top = jnp.maximum(
            jnp.max(s0, axis=1, keepdims=True), jnp.max(s1, axis=1, keepdims=True)
        )
        e0, e1 = jnp.exp(s0 - top), jnp.exp(s1 - top)
        total = jnp.sum(e0, axis=1, keepdims=True) + jnp.sum(e1, axis=1, keepdims=True)
        return (e0 / total).astype(BF16), (e1 / total).astype(BF16)

    wide = min(8, n)
    lane8 = lax.broadcasted_iota(jnp.int32, (8, HEAD), 1)
    step8 = lax.broadcasted_iota(jnp.int32, (8, HEAD), 0) % 2
    fresh8 = (lane8 == PAGE - 3) | ((lane8 == PAGE - 2) & (step8 == 1))

    def src_step(b, _):
        parts0, parts1 = [], []
        for i in range(wide):
            request = b * wide + i
            slot = tgts[request]
            query = qs[request].astype(BF16)
            bound = lens[request]
            s0 = dot_t(query, send[slot, 0, 0]) * scale
            s1 = dot_t(query, send[slot, 1, 0]) * scale
            parts0.append(jnp.where(lane8 < bound, s0, NEG))
            parts1.append(jnp.where((lane8 + PAGE < bound) | fresh8, s1, NEG))
        w0, w1 = soft(jnp.concatenate(parts0, axis=0), jnp.concatenate(parts1, axis=0))
        for i in range(wide):
            request = b * wide + i
            slot = tgts[request]
            rows = slice(8 * i, 8 * i + 8)
            mixed = dot(w0[rows], send[slot, 0, 1]) + dot(w1[rows], send[slot, 1, 1])
            for g in range(GROUPS):
                att_s[g, pl.ds(2 * request, 2), :] = mixed[2 * g : 2 * g + 2]
        return 0

    lax.fori_loop(0, n // wide, src_step, 0)

    def remote(src, dst, sems, index, target):
        return pltpu.make_async_remote_copy(
            src_ref=src,
            dst_ref=dst,
            send_sem=sems.at[2 * index],
            recv_sem=sems.at[2 * index + 1],
            device_id=(me, target),
            device_id_type=MESH,
        )

    def block_cols(index):
        return pl.ds(pl.multiple_of(index * cols, cols), cols)

    def ring_tail(att, half, half_in, pair, cross, cross_in, rs, rs_in, full):
        a = jnp.concatenate([att[g].astype(BF16) for g in range(GROUPS)], axis=1)
        part = cols // 2
        up, down = peer_hi(1), peer_hi(his - 1)

        def spot(step, side=None):
            start = (((hi + step) % his) * 2 + core) * cols
            if side is None:
                return full.at[:, :, pl.ds(pl.multiple_of(start, cols), cols)]
            return full.at[:, :, pl.ds(pl.multiple_of(start + side * part, part), part)]

        def mates(step):
            start = (((hi + step) % his) * 2 + 1 - core) * cols
            return full.at[:, :, pl.ds(pl.multiple_of(start, cols), cols)]

        swap = remote(half, half_in, half_sem, 0, mate)
        over = [
            remote(cross.at[0], cross_in.at[0], rs_sem, 0, up),
            remote(cross.at[1], cross_in.at[1], rs_sem, 1, down),
        ]
        near = [
            remote(rs.at[0], rs_in.at[0], rs_sem, 2, up),
            remote(rs.at[1], rs_in.at[1], rs_sem, 3, down),
        ]
        give = [remote(spot(0), spot(0), ag_sem, i, to) for i, to in enumerate((up, down))]
        take = [
            remote(spot(0), spot(step), ag_sem, i, to)
            for i, (step, to) in enumerate(((his - 1, up), (1, down)))
        ]
        pass_on = [
            remote(spot(step, side), spot(step, side), ag_sem, 2 + side, to)
            for side, (step, to) in enumerate(((his - 1, up), (1, down)))
        ]
        last_in = [
            remote(spot(0, side), spot(2, side), ag_sem, 2 + side, to)
            for side, to in enumerate((up, down))
        ]
        forward = [remote(spot(step), spot(step), fwd_sem, step, mate) for step in range(his)]
        received = [remote(spot(step), mates(step), fwd_sem, step, mate) for step in range(his)]

        def project():
            for step in range(his):
                z = (hi + step) % his
                half[step] = dot(a, w[:, block_cols(z * 2 + 1 - core)]).astype(BF16)
            swap.start()
            for step in range(his):
                z = (hi + step) % his
                pair[step] = dot(a, w[:, block_cols(z * 2 + core)])

        def far():
            swap.wait()
            for step in range(his):
                pair[step] = pair[step] + half_in[step].astype(F32)
            cross[0] = pair[2, :, :part].astype(BF16)
            cross[1] = pair[2, :, part:].astype(BF16)
            for copy in over:
                copy.start()

        def close():
            for copy in over:
                copy.wait()
            rs[0, :, :part] = (pair[1, :, :part] + cross_in[0].astype(F32)).astype(BF16)
            rs[0, :, part:] = pair[1, :, part:].astype(BF16)
            rs[1, :, :part] = pair[his - 1, :, :part].astype(BF16)
            rs[1, :, part:] = (pair[his - 1, :, part:] + cross_in[1].astype(F32)).astype(BF16)
            for copy in near:
                copy.start()

        def total():
            for copy in near:
                copy.wait()
            sums = pair[0] + rs_in[0].astype(F32) + rs_in[1].astype(F32)
            spot(0)[...] = sums.reshape(full.shape[:2] + (cols,)).astype(BF16)
            for copy in give:
                copy.start()
            forward[0].start()

        def relay():
            for side, step in enumerate((his - 1, 1)):
                take[side].wait_recv()
                pass_on[side].start()
                forward[step].start()

        def end():
            for copy in last_in:
                copy.wait_recv()
            forward[2].start()
            for copy in received:
                copy.wait_recv()
            for copy in give + pass_on + forward:
                copy.wait_send()

        return project, far, close, total, relay, end

    def tail(part, att, half, half_in, pair, rs, rs_in, full):
        a = jnp.concatenate([att[g].astype(BF16) for g in range(GROUPS)], axis=1)

        def part_full(index):
            where = block_cols(index)
            return full.at[:, where]

        swap = remote(half, half_in, half_sem, part, mate)
        scatter = [
            remote(rs.at[step], rs_in.at[step], rs_sem, part * his + step, peer_hi(step))
            for step in range(1, his)
        ]
        mine = part_full(tp)
        gather = [
            remote(mine, mine, ag_sem, part * his + step, peer_hi(step))
            for step in range(1, his)
        ]
        landed = [
            remote(
                mine,
                part_full(((hi + his - step) % his) * 2 + core),
                ag_sem,
                part * his + step,
                peer_hi(step),
            )
            for step in range(1, his)
        ]
        forward = []
        received = []
        for step in range(his):
            owner = ((hi + his - step) % his) * 2
            have, want = part_full(owner + core), part_full(owner + 1 - core)
            forward.append(remote(have, have, fwd_sem, part * his + step, mate))
            received.append(remote(have, want, fwd_sem, part * his + step, mate))

        def one():
            for step in range(his):
                z = (hi + step) % his
                half[step] = dot(a, w[:, block_cols(z * 2 + 1 - core)]).astype(BF16)
            swap.start()
            for step in range(his):
                z = (hi + step) % his
                pair[step] = dot(a, w[:, block_cols(z * 2 + core)])

        def two():
            swap.wait()
            for step in range(1, his):
                rs[step] = (pair[step] + half_in[step].astype(F32)).astype(BF16)
                scatter[step - 1].start()
            pair[0] = pair[0] + half_in[0].astype(F32)

        def three():
            for copy in scatter:
                copy.wait()
            total = pair[0]
            for step in range(1, his):
                total = total + rs_in[step].astype(F32)
            mine[...] = total.astype(BF16)
            for copy in gather:
                copy.start()
            forward[0].start()

        def four():
            for step in range(1, his):
                landed[step - 1].wait_recv()
                forward[step].start()
            for step in range(his):
                received[step].wait_recv()

        def five():
            for copy in gather:
                copy.wait_send()
            for copy in forward:
                copy.wait_send()

        return one, two, three, four, five

    load_w.wait()
    project, far, close, total_up, relay, end = ring_tail(
        att_s, s_half, s_half_in, s_pair, s_cross, s_cross_in, s_rs, s_rs_in, s_full
    )
    project()

    lane4 = lax.broadcasted_iota(jnp.int32, (GROUPS, HEAD), 1).astype(F32)

    def state(slot):
        length = arr[slot, 1, 0, PAGE - TILE :].astype(F32)[TILE - 1 :]
        flag = arr[slot, 1, 1, PAGE - TILE :].astype(F32)[TILE - 1 :]
        return length, flag == 1.0

    def dst_step(b, _):
        slots, parts0, parts1, values = [], [], [], []
        for i in range(batch):
            k = b * batch + i

            @pl.when(k > 0)
            def _():
                move(k).wait_send()

            @pl.when(k + ahead < n)
            def _():
                launch(k + ahead)

        for i in range(batch):
            k = b * batch + i

            @pl.when(k > 0)
            def _():
                arrive(k).wait_recv()

        for i in range(batch):
            slot = partner(b * batch + i)
            slots.append(slot)
            length, moved = state(slot)
            own = rdst[slot].astype(F32)
            key1 = jnp.where(last, own[0:1].astype(BF16), arr[slot, 1, 0])
            value1 = jnp.where(last, own[1:2].astype(BF16), arr[slot, 1, 1])
            query = qd[slot].astype(BF16)
            s0 = dot_t(query, arr[slot, 0, 0]) * scale
            s1 = dot_t(query, key1) * scale
            parts0.append(jnp.where(lane4 < length, s0, NEG))
            keep1 = (lane4 + float(PAGE) < length) | (lane4 >= PAGE - 3.0)
            parts1.append(jnp.where(keep1, s1, NEG))
            values.append((arr[slot, 0, 1], value1, moved))
        for i in range(batch):
            w0, w1 = soft(parts0[i], parts1[i])
            mixed = dot(w0, values[i][0]) + dot(w1, values[i][1])
            mixed = jnp.where(values[i][2], mixed, 0.0)
            for g in range(GROUPS):
                att_d[g, pl.ds(slots[i], 1), :] = mixed[g : g + 1]
        return 0

    def fill_step(b, _):
        for i in range(batch):
            slot = partner(b * batch + i)
            length, moved = state(slot)
            length = jnp.where(moved, length, -512.0)
            own = rdst[slot].astype(F32)
            rows_in = [arr[slot, 1, c, PAGE - TILE :].astype(F32) for c in range(2)]
            for p in range(2):
                at = [(length + (j - p * PAGE)).astype(BF16) for j in range(3)]
                keep = row < at[0]
                hits = [row == spot for spot in at]
                for c in range(2):
                    rows_put = [
                        rows_in[c][TILE - 3 : TILE - 2],
                        rows_in[c][TILE - 2 : TILE - 1],
                        own[c : c + 1],
                    ]
                    block = jnp.where(keep, arr[slot, p, c], zero)
                    for hit, put in zip(hits, rows_put):
                        block = jnp.where(hit, put.astype(BF16), block)
                    cache_out[slot, p, c] = block
        return 0

    def both(b, _):
        dst_step(b, 0)
        return fill_step(b, 0)

    steps = n // batch
    marks = [steps * j // 8 for j in (0, 2, 5, 6, 7, 8)]
    lax.fori_loop(marks[0], marks[1], both, 0)
    far()
    lax.fori_loop(marks[1], marks[2], both, 0)
    close()
    lax.fori_loop(marks[2], marks[5], dst_step, 0)

    dst_tail = tail(1, att_d, d_half, d_half_in, d_pair, d_rs, d_rs_in, d_full)
    dst_tail[0]()
    total_up()
    dst_tail[1]()
    lax.fori_loop(marks[2], marks[4], fill_step, 0)
    relay()
    dst_tail[2]()
    lax.fori_loop(marks[4], marks[5], fill_step, 0)
    end()
    dst_tail[3]()
    dst_tail[4]()


def place(src_in, cache_in, dst_in, src_hbm, cache_hbm, dst_hbm, sem):
    size = cache_in.shape[0] // PIECES
    copies = [
        pltpu.make_async_copy(
            cache_in.at[i * size : (i + 1) * size],
            cache_hbm.at[i * size : (i + 1) * size],
            sem.at[i],
        )
        for i in range(PIECES)
    ]
    copies.append(pltpu.make_async_copy(src_in, src_hbm, sem.at[PIECES]))
    copies.append(pltpu.make_async_copy(dst_in, dst_hbm, sem.at[PIECES + 1]))
    for copy in copies:
        copy.start()
    for copy in copies:
        copy.wait()


def shards(
    pool,
    page_table,
    lengths,
    targets,
    migrating,
    queries_src,
    new_rows,
    queries_dst,
    rows_dst,
    w_out,
):
    n = lax.axis_size("inst")
    tp_size = lax.axis_size("tp")
    his = tp_size // 2
    requests = queries_src.shape[0]
    width = w_out.shape[1]
    cols = width // tp_size
    smem = pl.BlockSpec(memory_space=pltpu.SMEM)
    vmem = pl.BlockSpec(memory_space=pltpu.VMEM)
    hbm = pl.BlockSpec(memory_space=pl.ANY)
    cache = (requests, 2, 2, PAGE, HEAD)

    def sums(rows, sent):
        return [
            pltpu.VMEM((his, rows, cols), BF16),
            pltpu.VMEM((his, rows, cols), BF16),
            pltpu.VMEM((his, rows, cols), F32),
        ] + [pltpu.VMEM((parts, rows, width), BF16) for parts, width in sent]

    dma = pltpu.SemaphoreType.DMA
    in_hbm = functools.partial(pltpu.with_memory_space_constraint, memory_space=pltpu.HBM)
    results = pl.pallas_call(
        functools.partial(kernel, n, tp_size),
        out_shape=(
            pltpu.VMEM((requests, 2, width), BF16),
            pltpu.VMEM(cache, BF16),
            pltpu.VMEM((requests, width), BF16),
        ),
        in_specs=[smem] * 4 + [vmem] * 4 + [hbm] * 2,
        out_specs=(vmem, vmem, vmem),
        scratch_shapes=[
            pltpu.VMEM(pool.shape, BF16),
            pltpu.VMEM(w_out.shape, BF16),
            pltpu.VMEM(cache, BF16),
            pltpu.VMEM(cache, BF16),
            pltpu.VMEM((requests, 2 * GROUPS, HEAD), F32),
            pltpu.VMEM((requests, GROUPS, HEAD), F32),
            pltpu.VMEM((GROUPS, 2 * requests, HEAD), F32),
            pltpu.VMEM((GROUPS, requests, HEAD), F32),
        ]
        + sums(2 * requests, [(2, cols // 2)] * 2 + [(2, cols)] * 2)
        + sums(requests, [(his, cols)] * 2)
        + [
            dma((2,)),
            dma((n,)),
            dma((n,)),
            dma((4,)),
            dma((4 * his,)),
            dma((4 * his,)),
            dma((4 * his,)),
        ],
        compiler_params=pltpu.CompilerParams(
            collective_id=0, has_side_effects=True, vmem_limit_bytes=28 * 1024 * 1024
        ),
        name="migrate",
    )(
        *map(
            in_hbm,
            (
                lengths,
                targets,
                migrating,
                page_table.T,
                queries_src,
                new_rows,
                queries_dst,
                rows_dst,
                pool,
                w_out,
            ),
        )
    )
    return pl.pallas_call(
        place,
        out_shape=tuple(pltpu.HBM(x.shape, x.dtype) for x in results),
        in_specs=[vmem] * 3,
        out_specs=(hbm,) * 3,
        scratch_shapes=[dma((PIECES + 2,))],
        compiler_params=pltpu.CompilerParams(vmem_limit_bytes=8 * 1024 * 1024),
        name="place",
    )(*(pltpu.with_memory_space_constraint(x, pltpu.VMEM) for x in results))


def solution(mesh):
    return jax.shard_map(
        shards,
        mesh=mesh,
        in_specs=(
            P("inst", None, None, "tp"),
            P("inst", None),
            P("inst"),
            P("inst"),
            P("inst"),
            P("inst", None, "tp"),
            P("inst", None, None, "tp"),
            P("inst", "tp"),
            P("inst", None, "tp"),
            P("tp", None),
        ),
        out_specs=(P("inst", None, None), P("inst", None, None, None, "tp"), P("inst", None)),
        check_vma=False,
    )
```

```python
import functools
import math

import jax
import jax.numpy as jnp
from jax import lax
from jax.experimental import pallas as pl
from jax.experimental.pallas import tpu as pltpu
from jax.sharding import PartitionSpec as P

MESH = pl.DeviceIdType.MESH
BF16 = jnp.bfloat16
F32 = jnp.float32
NEG = -1e30
HEAD = 128
PAGE = 128
GROUPS = 4
TILE = 16
PIECES = 8
MIX = 11


def xor(a, b, bits):
    total = 0
    for bit in range(bits):
        weight = 2**bit
        u, v = (a // weight) % 2, (b // weight) % 2
        total = total + (u + v - 2 * u * v) * weight
    return total


def order(k, n):
    if n != 32:
        return (k * MIX) % n
    late = k // 16
    spot = (k - 16 * late) % 8
    turn = (k - 16 * late) // 8
    hop0 = (k % 3 + 1) // 2
    hop1 = 1 - (spot % 3 + 1) // 2
    hop = (1 - late) * hop0 + late * hop1
    cross0 = k - k // 3 - 1
    cross1 = 10 + 3 * turn + spot // 3
    plane0 = k // 3
    plane1 = 6 + 5 * turn + spot - spot // 3 - 1
    count = hop * ((1 - late) * cross0 + late * cross1)
    count = count + (1 - hop) * ((1 - late) * plane0 + late * plane1)
    return ((count * MIX) % 16) * 2 + hop


def kernel(
    n,
    tp_size,
    lens,
    tgts,
    mig,
    table,
    qsrc,
    fresh,
    qdst,
    rdst,
    pool_hbm,
    w_hbm,
    s_full,
    cache_out,
    d_full,
    pool,
    w,
    send,
    arr,
    qs,
    qd,
    att_s,
    att_d,
    s_half,
    s_half_in,
    s_pair,
    s_cross,
    s_cross_in,
    s_rs,
    s_rs_in,
    d_half,
    d_half_in,
    d_pair,
    d_rs,
    d_rs_in,
    load_sem,
    send_sem,
    recv_sem,
    half_sem,
    rs_sem,
    ag_sem,
    fwd_sem,
):
    me = lax.axis_index("inst")
    tp = lax.axis_index("tp")
    core = tp % 2
    hi = tp // 2
    his = tp_size // 2
    mate = tp + 1 - 2 * core
    bits = n.bit_length() - 1
    scale = 1.0 / math.sqrt(HEAD)
    cols = w.shape[1] // tp_size

    def peer_hi(step):
        return ((hi + step) % his) * 2 + core

    def partner(k):
        return xor(me, order(k, n), bits)

    load_pool = pltpu.make_async_copy(pool_hbm, pool, load_sem.at[0])
    load_w = pltpu.make_async_copy(w_hbm, w, load_sem.at[1])
    load_pool.start()
    barrier = pltpu.get_barrier_semaphore()

    def greet(k, _):
        pl.semaphore_signal(
            barrier, inc=1, device_id=(xor(me, k, bits), tp), device_id_type=MESH
        )
        return 0

    lax.fori_loop(1, n, greet, 0)
    pl.semaphore_signal(barrier, inc=1, device_id=(me, mate), device_id_type=MESH)
    for step in range(1, his):
        pl.semaphore_signal(barrier, inc=1, device_id=(me, peer_hi(step)), device_id_type=MESH)

    row = lax.broadcasted_iota(jnp.int32, (PAGE, HEAD), 0).astype(F32).astype(BF16)
    last = row == jnp.asarray(PAGE - 1, BF16)
    zero = jnp.zeros((PAGE, HEAD), BF16)
    tile_row = lax.broadcasted_iota(jnp.int32, (TILE, HEAD), 0).astype(F32)

    def move(k):
        peer = partner(k)
        return pltpu.make_async_remote_copy(
            src_ref=send.at[peer],
            dst_ref=arr.at[me],
            send_sem=send_sem.at[k],
            recv_sem=recv_sem.at[k],
            device_id=(peer, tp),
            device_id_type=MESH,
        )

    def launch(k):
        peer = partner(k)
        for p in range(2):
            for c in range(2):
                pltpu.make_async_remote_copy(
                    src_ref=send.at[peer, p, c],
                    dst_ref=arr.at[me, p, c],
                    send_sem=send_sem.at[k],
                    recv_sem=recv_sem.at[k],
                    device_id=(peer, tp),
                    device_id_type=MESH,
                ).start()

    def arrive(k):
        peer = partner(k)
        return pltpu.make_async_remote_copy(
            src_ref=send.at[peer],
            dst_ref=arr.at[peer],
            send_sem=send_sem.at[k],
            recv_sem=recv_sem.at[k],
            device_id=(peer, tp),
            device_id_type=MESH,
        )

    def pack(k, ref):
        slot = partner(k)
        request = jnp.int32(0)
        for j in range(n):
            request = jnp.where(tgts[j] == slot, j, request)
        length = lens[request].astype(F32)
        flag = mig[request].astype(F32)
        rows_new = fresh[request].astype(F32)
        for c in range(2):
            ref[slot, 0, c] = pool[table[0, request], c]
            page = pool[table[1, request], c]
            ref[slot, 1, c, : PAGE - TILE] = page[: PAGE - TILE]
            end = jnp.where(tile_row == TILE - 3.0, rows_new[0, c : c + 1], page[PAGE - TILE :].astype(F32))
            end = jnp.where(tile_row == TILE - 2.0, rows_new[1, c : c + 1], end)
            end = jnp.where(tile_row == TILE - 1.0, length if c == 0 else flag, end)
            ref[slot, 1, c, PAGE - TILE :] = end.astype(BF16)

    q_wide = qsrc[...].astype(F32)
    for g in range(GROUPS):
        lanes = slice(g * HEAD, (g + 1) * HEAD)
        for t in range(2):
            qs[:, 2 * g + t, :] = q_wide[:, t, lanes]
        qd[:, g, :] = qdst[:, lanes].astype(F32)

    load_pool.wait()
    load_w.start()

    def send_step(k, _):
        pack(k, send)
        launch(k)
        return 0

    def launch_step(k, _):
        launch(k)
        return 0

    def pack_step(k, _):
        pack(k, send)
        return 0

    batch = min(4, n)
    ahead = min(4 * batch, n)
    ready = min(9, n)
    lax.fori_loop(0, ready, pack_step, 0)
    pl.semaphore_wait(barrier, n - 1 + his)
    lax.fori_loop(1, ready, launch_step, 0)
    lax.fori_loop(ready, n, pack_step, 0)
    arr[me] = send[me]

    def dot_t(a, b):
        return lax.dot_general(a, b, (((1,), (1,)), ((), ())), preferred_element_type=F32)

    def dot(a, b):
        return jnp.dot(a, b, preferred_element_type=F32)

    def soft(s0, s1):
        top = jnp.maximum(
            jnp.max(s0, axis=1, keepdims=True), jnp.max(s1, axis=1, keepdims=True)
        )
        e0, e1 = jnp.exp(s0 - top), jnp.exp(s1 - top)
        total = jnp.sum(e0, axis=1, keepdims=True) + jnp.sum(e1, axis=1, keepdims=True)
        return (e0 / total).astype(BF16), (e1 / total).astype(BF16)

    wide = min(8, n)
    lane8 = lax.broadcasted_iota(jnp.int32, (8, HEAD), 1)
    step8 = lax.broadcasted_iota(jnp.int32, (8, HEAD), 0) % 2
    fresh8 = (lane8 == PAGE - 3) | ((lane8 == PAGE - 2) & (step8 == 1))

    def src_step(b, _):
        parts0, parts1 = [], []
        for i in range(wide):
            request = b * wide + i
            slot = tgts[request]
            query = qs[request].astype(BF16)
            bound = lens[request]
            s0 = dot_t(query, send[slot, 0, 0]) * scale
            s1 = dot_t(query, send[slot, 1, 0]) * scale
            parts0.append(jnp.where(lane8 < bound, s0, NEG))
            parts1.append(jnp.where((lane8 + PAGE < bound) | fresh8, s1, NEG))
        w0, w1 = soft(jnp.concatenate(parts0, axis=0), jnp.concatenate(parts1, axis=0))
        for i in range(wide):
            request = b * wide + i
            slot = tgts[request]
            rows = slice(8 * i, 8 * i + 8)
            mixed = dot(w0[rows], send[slot, 0, 1]) + dot(w1[rows], send[slot, 1, 1])
            for g in range(GROUPS):
                att_s[g, pl.ds(2 * request, 2), :] = mixed[2 * g : 2 * g + 2]
        return 0

    lax.fori_loop(0, n // wide, src_step, 0)

    def remote(src, dst, sems, index, target):
        return pltpu.make_async_remote_copy(
            src_ref=src,
            dst_ref=dst,
            send_sem=sems.at[2 * index],
            recv_sem=sems.at[2 * index + 1],
            device_id=(me, target),
            device_id_type=MESH,
        )

    def block_cols(index):
        return pl.ds(pl.multiple_of(index * cols, cols), cols)

    def ring_tail(att, half, half_in, pair, cross, cross_in, rs, rs_in, full):
        a = jnp.concatenate([att[g].astype(BF16) for g in range(GROUPS)], axis=1)
        part = cols // 2
        up, down = peer_hi(1), peer_hi(his - 1)

        def spot(step, side=None):
            start = (((hi + step) % his) * 2 + core) * cols
            if side is None:
                return full.at[:, :, pl.ds(pl.multiple_of(start, cols), cols)]
            return full.at[:, :, pl.ds(pl.multiple_of(start + side * part, part), part)]

        def mates(step):
            start = (((hi + step) % his) * 2 + 1 - core) * cols
            return full.at[:, :, pl.ds(pl.multiple_of(start, cols), cols)]

        swap = remote(half, half_in, half_sem, 0, mate)
        over = [
            remote(cross.at[0], cross_in.at[0], rs_sem, 0, up),
            remote(cross.at[1], cross_in.at[1], rs_sem, 1, down),
        ]
        near = [
            remote(rs.at[0], rs_in.at[0], rs_sem, 2, up),
            remote(rs.at[1], rs_in.at[1], rs_sem, 3, down),
        ]
        give = [remote(spot(0), spot(0), ag_sem, i, to) for i, to in enumerate((up, down))]
        take = [
            remote(spot(0), spot(step), ag_sem, i, to)
            for i, (step, to) in enumerate(((his - 1, up), (1, down)))
        ]
        pass_on = [
            remote(spot(step, side), spot(step, side), ag_sem, 2 + side, to)
            for side, (step, to) in enumerate(((his - 1, up), (1, down)))
        ]
        last_in = [
            remote(spot(0, side), spot(2, side), ag_sem, 2 + side, to)
            for side, to in enumerate((up, down))
        ]
        forward = [remote(spot(step), spot(step), fwd_sem, step, mate) for step in range(his)]
        received = [remote(spot(step), mates(step), fwd_sem, step, mate) for step in range(his)]

        def project():
            for step in range(his):
                z = (hi + step) % his
                half[step] = dot(a, w[:, block_cols(z * 2 + 1 - core)]).astype(BF16)
            swap.start()
            for step in range(his):
                z = (hi + step) % his
                pair[step] = dot(a, w[:, block_cols(z * 2 + core)])

        def far():
            swap.wait()
            for step in range(his):
                pair[step] = pair[step] + half_in[step].astype(F32)
            cross[0] = pair[2, :, :part].astype(BF16)
            cross[1] = pair[2, :, part:].astype(BF16)
            for copy in over:
                copy.start()

        def close():
            for copy in over:
                copy.wait()
            rs[0, :, :part] = (pair[1, :, :part] + cross_in[0].astype(F32)).astype(BF16)
            rs[0, :, part:] = pair[1, :, part:].astype(BF16)
            rs[1, :, :part] = pair[his - 1, :, :part].astype(BF16)
            rs[1, :, part:] = (pair[his - 1, :, part:] + cross_in[1].astype(F32)).astype(BF16)
            for copy in near:
                copy.start()

        def total():
            for copy in near:
                copy.wait()
            sums = pair[0] + rs_in[0].astype(F32) + rs_in[1].astype(F32)
            spot(0)[...] = sums.reshape(full.shape[:2] + (cols,)).astype(BF16)
            for copy in give:
                copy.start()
            forward[0].start()

        def relay():
            for side, step in enumerate((his - 1, 1)):
                take[side].wait_recv()
                pass_on[side].start()
                forward[step].start()

        def end():
            for copy in last_in:
                copy.wait_recv()
            forward[2].start()
            for copy in received:
                copy.wait_recv()
            for copy in give + pass_on + forward:
                copy.wait_send()

        return project, far, close, total, relay, end

    def tail(part, att, half, half_in, pair, rs, rs_in, full):
        a = jnp.concatenate([att[g].astype(BF16) for g in range(GROUPS)], axis=1)

        def part_full(index):
            where = block_cols(index)
            return full.at[:, where]

        swap = remote(half, half_in, half_sem, part, mate)
        scatter = [
            remote(rs.at[step], rs_in.at[step], rs_sem, part * his + step, peer_hi(step))
            for step in range(1, his)
        ]
        mine = part_full(tp)
        gather = [
            remote(mine, mine, ag_sem, part * his + step, peer_hi(step))
            for step in range(1, his)
        ]
        landed = [
            remote(
                mine,
                part_full(((hi + his - step) % his) * 2 + core),
                ag_sem,
                part * his + step,
                peer_hi(step),
            )
            for step in range(1, his)
        ]
        forward = []
        received = []
        for step in range(his):
            owner = ((hi + his - step) % his) * 2
            have, want = part_full(owner + core), part_full(owner + 1 - core)
            forward.append(remote(have, have, fwd_sem, part * his + step, mate))
            received.append(remote(have, want, fwd_sem, part * his + step, mate))

        def one():
            for step in range(his):
                z = (hi + step) % his
                half[step] = dot(a, w[:, block_cols(z * 2 + 1 - core)]).astype(BF16)
            swap.start()
            for step in range(his):
                z = (hi + step) % his
                pair[step] = dot(a, w[:, block_cols(z * 2 + core)])

        def two():
            swap.wait()
            for step in range(1, his):
                rs[step] = (pair[step] + half_in[step].astype(F32)).astype(BF16)
                scatter[step - 1].start()
            pair[0] = pair[0] + half_in[0].astype(F32)

        def three():
            for copy in scatter:
                copy.wait()
            total = pair[0]
            for step in range(1, his):
                total = total + rs_in[step].astype(F32)
            mine[...] = total.astype(BF16)
            for copy in gather:
                copy.start()
            forward[0].start()

        def four():
            for step in range(1, his):
                landed[step - 1].wait_recv()
                forward[step].start()
            for step in range(his):
                received[step].wait_recv()

        def five():
            for copy in gather:
                copy.wait_send()
            for copy in forward:
                copy.wait_send()

        return one, two, three, four, five

    load_w.wait()
    project, far, close, total_up, relay, end = ring_tail(
        att_s, s_half, s_half_in, s_pair, s_cross, s_cross_in, s_rs, s_rs_in, s_full
    )
    lax.fori_loop(ready, ready + 2, launch_step, 0)
    project()
    far()
    lax.fori_loop(ready + 2, ahead, launch_step, 0)

    lane4 = lax.broadcasted_iota(jnp.int32, (GROUPS, HEAD), 1).astype(F32)

    def state(slot):
        length = arr[slot, 1, 0, PAGE - TILE :].astype(F32)[TILE - 1 :]
        flag = arr[slot, 1, 1, PAGE - TILE :].astype(F32)[TILE - 1 :]
        return length, flag == 1.0

    def dst_step(b, _):
        slots, parts0, parts1, values = [], [], [], []
        for i in range(batch):
            k = b * batch + i

            @pl.when(k > 0)
            def _():
                move(k).wait_send()

            @pl.when(k + ahead < n)
            def _():
                launch(k + ahead)

        for i in range(batch):
            k = b * batch + i

            @pl.when(k > 0)
            def _():
                arrive(k).wait_recv()

        for i in range(batch):
            slot = partner(b * batch + i)
            slots.append(slot)
            length, moved = state(slot)
            own = rdst[slot].astype(F32)
            key1 = jnp.where(last, own[0:1].astype(BF16), arr[slot, 1, 0])
            value1 = jnp.where(last, own[1:2].astype(BF16), arr[slot, 1, 1])
            query = qd[slot].astype(BF16)
            s0 = dot_t(query, arr[slot, 0, 0]) * scale
            s1 = dot_t(query, key1) * scale
            parts0.append(jnp.where(lane4 < length, s0, NEG))
            keep1 = (lane4 + float(PAGE) < length) | (lane4 >= PAGE - 3.0)
            parts1.append(jnp.where(keep1, s1, NEG))
            values.append((arr[slot, 0, 1], value1, moved))
        for i in range(batch):
            w0, w1 = soft(parts0[i], parts1[i])
            mixed = dot(w0, values[i][0]) + dot(w1, values[i][1])
            mixed = jnp.where(values[i][2], mixed, 0.0)
            for g in range(GROUPS):
                att_d[g, pl.ds(slots[i], 1), :] = mixed[g : g + 1]
        return 0

    def fill_step(b, _):
        for i in range(batch):
            slot = partner(b * batch + i)
            length, moved = state(slot)
            length = jnp.where(moved, length, -512.0)
            own = rdst[slot].astype(F32)
            rows_in = [arr[slot, 1, c, PAGE - TILE :].astype(F32) for c in range(2)]
            for p in range(2):
                at = [(length + (j - p * PAGE)).astype(BF16) for j in range(3)]
                keep = row < at[0]
                hits = [row == spot for spot in at]
                for c in range(2):
                    rows_put = [
                        rows_in[c][TILE - 3 : TILE - 2],
                        rows_in[c][TILE - 2 : TILE - 1],
                        own[c : c + 1],
                    ]
                    block = jnp.where(keep, arr[slot, p, c], zero)
                    for hit, put in zip(hits, rows_put):
                        block = jnp.where(hit, put.astype(BF16), block)
                    cache_out[slot, p, c] = block
        return 0

    def both(b, _):
        dst_step(b, 0)
        return fill_step(b, 0)

    steps = n // batch
    marks = [steps * j // 8 for j in (0, 2, 4, 6, 7, 8)]
    lax.fori_loop(marks[0], marks[1], both, 0)
    close()
    lax.fori_loop(marks[1], marks[2], both, 0)
    total_up()
    lax.fori_loop(marks[2], marks[3], both, 0)
    relay()
    lax.fori_loop(marks[3], marks[5], dst_step, 0)

    dst_tail = tail(1, att_d, d_half, d_half_in, d_pair, d_rs, d_rs_in, d_full)
    dst_tail[0]()
    lax.fori_loop(marks[3], marks[4], fill_step, 0)
    dst_tail[1]()
    lax.fori_loop(marks[4], marks[5], fill_step, 0)
    end()
    for stage in dst_tail[2:]:
        stage()


def place(src_in, cache_in, dst_in, src_hbm, cache_hbm, dst_hbm, sem):
    size = cache_in.shape[0] // PIECES
    copies = [
        pltpu.make_async_copy(
            cache_in.at[i * size : (i + 1) * size],
            cache_hbm.at[i * size : (i + 1) * size],
            sem.at[i],
        )
        for i in range(PIECES)
    ]
    copies.append(pltpu.make_async_copy(src_in, src_hbm, sem.at[PIECES]))
    copies.append(pltpu.make_async_copy(dst_in, dst_hbm, sem.at[PIECES + 1]))
    for copy in copies:
        copy.start()
    for copy in copies:
        copy.wait()


def shards(
    pool,
    page_table,
    lengths,
    targets,
    migrating,
    queries_src,
    new_rows,
    queries_dst,
    rows_dst,
    w_out,
):
    n = lax.axis_size("inst")
    tp_size = lax.axis_size("tp")
    his = tp_size // 2
    requests = queries_src.shape[0]
    width = w_out.shape[1]
    cols = width // tp_size
    smem = pl.BlockSpec(memory_space=pltpu.SMEM)
    vmem = pl.BlockSpec(memory_space=pltpu.VMEM)
    hbm = pl.BlockSpec(memory_space=pl.ANY)
    cache = (requests, 2, 2, PAGE, HEAD)

    def sums(rows, sent):
        return [
            pltpu.VMEM((his, rows, cols), BF16),
            pltpu.VMEM((his, rows, cols), BF16),
            pltpu.VMEM((his, rows, cols), F32),
        ] + [pltpu.VMEM((parts, rows, width), BF16) for parts, width in sent]

    dma = pltpu.SemaphoreType.DMA
    in_hbm = functools.partial(pltpu.with_memory_space_constraint, memory_space=pltpu.HBM)
    results = pl.pallas_call(
        functools.partial(kernel, n, tp_size),
        out_shape=(
            pltpu.VMEM((requests, 2, width), BF16),
            pltpu.VMEM(cache, BF16),
            pltpu.VMEM((requests, width), BF16),
        ),
        in_specs=[smem] * 4 + [vmem] * 4 + [hbm] * 2,
        out_specs=(vmem, vmem, vmem),
        scratch_shapes=[
            pltpu.VMEM(pool.shape, BF16),
            pltpu.VMEM(w_out.shape, BF16),
            pltpu.VMEM(cache, BF16),
            pltpu.VMEM(cache, BF16),
            pltpu.VMEM((requests, 2 * GROUPS, HEAD), F32),
            pltpu.VMEM((requests, GROUPS, HEAD), F32),
            pltpu.VMEM((GROUPS, 2 * requests, HEAD), F32),
            pltpu.VMEM((GROUPS, requests, HEAD), F32),
        ]
        + sums(2 * requests, [(2, cols // 2)] * 2 + [(2, cols)] * 2)
        + sums(requests, [(his, cols)] * 2)
        + [
            dma((2,)),
            dma((n,)),
            dma((n,)),
            dma((4,)),
            dma((4 * his,)),
            dma((4 * his,)),
            dma((4 * his,)),
        ],
        compiler_params=pltpu.CompilerParams(
            collective_id=0, has_side_effects=True, vmem_limit_bytes=28 * 1024 * 1024
        ),
        name="migrate",
    )(
        *map(
            in_hbm,
            (
                lengths,
                targets,
                migrating,
                page_table.T,
                queries_src,
                new_rows,
                queries_dst,
                rows_dst,
                pool,
                w_out,
            ),
        )
    )
    return pl.pallas_call(
        place,
        out_shape=tuple(pltpu.HBM(x.shape, x.dtype) for x in results),
        in_specs=[vmem] * 3,
        out_specs=(hbm,) * 3,
        scratch_shapes=[dma((PIECES + 2,))],
        compiler_params=pltpu.CompilerParams(vmem_limit_bytes=8 * 1024 * 1024),
        name="place",
    )(*(pltpu.with_memory_space_constraint(x, pltpu.VMEM) for x in results))


def solution(mesh):
    return jax.shard_map(
        shards,
        mesh=mesh,
        in_specs=(
            P("inst", None, None, "tp"),
            P("inst", None),
            P("inst"),
            P("inst"),
            P("inst"),
            P("inst", None, "tp"),
            P("inst", None, None, "tp"),
            P("inst", "tp"),
            P("inst", None, "tp"),
            P("tp", None),
        ),
        out_specs=(P("inst", None, None), P("inst", None, None, None, "tp"), P("inst", None)),
        check_vma=False,
    )
```

```python
import functools
import math

import jax
import jax.numpy as jnp
from jax import lax
from jax.experimental import pallas as pl
from jax.experimental.pallas import tpu as pltpu
from jax.sharding import PartitionSpec as P

MESH = pl.DeviceIdType.MESH
BF16 = jnp.bfloat16
F32 = jnp.float32
NEG = -1e30
HEAD = 128
PAGE = 128
GROUPS = 4
TILE = 16
PIECES = 8
MIX = 11


def xor(a, b, bits):
    total = 0
    for bit in range(bits):
        weight = 2**bit
        u, v = (a // weight) % 2, (b // weight) % 2
        total = total + (u + v - 2 * u * v) * weight
    return total


def order(k, n):
    if n != 32:
        return (k * MIX) % n
    late = k // 16
    spot = (k - 16 * late) % 8
    turn = (k - 16 * late) // 8
    hop0 = (k % 3 + 1) // 2
    hop1 = 1 - (spot % 3 + 1) // 2
    hop = (1 - late) * hop0 + late * hop1
    cross0 = k - k // 3 - 1
    cross1 = 10 + 3 * turn + spot // 3
    plane0 = k // 3
    plane1 = 6 + 5 * turn + spot - spot // 3 - 1
    count = hop * ((1 - late) * cross0 + late * cross1)
    count = count + (1 - hop) * ((1 - late) * plane0 + late * plane1)
    return ((count * MIX) % 16) * 2 + hop


def kernel(
    n,
    tp_size,
    lens,
    tgts,
    mig,
    table,
    qsrc_hbm,
    fresh_hbm,
    qdst_hbm,
    rdst_hbm,
    pool_hbm,
    w_hbm,
    s_full,
    cache_out,
    d_full,
    qsrc,
    fresh,
    qdst,
    rdst,
    pool,
    w,
    send,
    arr,
    qs,
    qd,
    att_s,
    att_d,
    s_half,
    s_half_in,
    s_pair,
    s_cross,
    s_cross_in,
    s_rs,
    s_rs_in,
    d_half,
    d_half_in,
    d_pair,
    d_rs,
    d_rs_in,
    load_sem,
    send_sem,
    recv_sem,
    half_sem,
    rs_sem,
    ag_sem,
    fwd_sem,
):
    me = lax.axis_index("inst")
    tp = lax.axis_index("tp")
    core = tp % 2
    hi = tp // 2
    his = tp_size // 2
    mate = tp + 1 - 2 * core
    bits = n.bit_length() - 1
    scale = 1.0 / math.sqrt(HEAD)
    cols = w.shape[1] // tp_size

    def peer_hi(step):
        return ((hi + step) % his) * 2 + core

    def partner(k):
        return xor(me, order(k, n), bits)

    load_pool = pltpu.make_async_copy(pool_hbm, pool, load_sem.at[0])
    load_w = pltpu.make_async_copy(w_hbm, w, load_sem.at[1])
    small = [
        pltpu.make_async_copy(src, dst, load_sem.at[2 + i])
        for i, (src, dst) in enumerate(
            ((fresh_hbm, fresh), (qsrc_hbm, qsrc), (qdst_hbm, qdst), (rdst_hbm, rdst))
        )
    ]
    load_pool.start()
    for copy in small:
        copy.start()
    barrier = pltpu.get_barrier_semaphore()

    def greet(k, _):
        pl.semaphore_signal(
            barrier, inc=1, device_id=(xor(me, k, bits), tp), device_id_type=MESH
        )
        return 0

    lax.fori_loop(1, n, greet, 0)
    pl.semaphore_signal(barrier, inc=1, device_id=(me, mate), device_id_type=MESH)
    for step in range(1, his):
        pl.semaphore_signal(barrier, inc=1, device_id=(me, peer_hi(step)), device_id_type=MESH)

    row = lax.broadcasted_iota(jnp.int32, (PAGE, HEAD), 0).astype(F32).astype(BF16)
    last = row == jnp.asarray(PAGE - 1, BF16)
    zero = jnp.zeros((PAGE, HEAD), BF16)
    tile_row = lax.broadcasted_iota(jnp.int32, (TILE, HEAD), 0).astype(F32)

    def move(k):
        peer = partner(k)
        return pltpu.make_async_remote_copy(
            src_ref=send.at[peer],
            dst_ref=arr.at[me],
            send_sem=send_sem.at[k],
            recv_sem=recv_sem.at[k],
            device_id=(peer, tp),
            device_id_type=MESH,
        )

    def launch(k):
        peer = partner(k)
        for p in range(2):
            for c in range(2):
                pltpu.make_async_remote_copy(
                    src_ref=send.at[peer, p, c],
                    dst_ref=arr.at[me, p, c],
                    send_sem=send_sem.at[k],
                    recv_sem=recv_sem.at[k],
                    device_id=(peer, tp),
                    device_id_type=MESH,
                ).start()

    def arrive(k):
        peer = partner(k)
        return pltpu.make_async_remote_copy(
            src_ref=send.at[peer],
            dst_ref=arr.at[peer],
            send_sem=send_sem.at[k],
            recv_sem=recv_sem.at[k],
            device_id=(peer, tp),
            device_id_type=MESH,
        )

    def pack(k, ref):
        slot = partner(k)
        request = jnp.int32(0)
        for j in range(n):
            request = jnp.where(tgts[j] == slot, j, request)
        length = lens[request].astype(F32)
        flag = mig[request].astype(F32)
        rows_new = fresh[request].astype(F32)
        for c in range(2):
            ref[slot, 0, c] = pool[table[0, request], c]
            page = pool[table[1, request], c]
            ref[slot, 1, c, : PAGE - TILE] = page[: PAGE - TILE]
            end = jnp.where(tile_row == TILE - 3.0, rows_new[0, c : c + 1], page[PAGE - TILE :].astype(F32))
            end = jnp.where(tile_row == TILE - 2.0, rows_new[1, c : c + 1], end)
            end = jnp.where(tile_row == TILE - 1.0, length if c == 0 else flag, end)
            ref[slot, 1, c, PAGE - TILE :] = end.astype(BF16)

    for copy in small:
        copy.wait()
    q_wide = qsrc[...].astype(F32)
    for g in range(GROUPS):
        lanes = slice(g * HEAD, (g + 1) * HEAD)
        for t in range(2):
            qs[:, 2 * g + t, :] = q_wide[:, t, lanes]
        qd[:, g, :] = qdst[:, lanes].astype(F32)

    load_pool.wait()
    load_w.start()

    def send_step(k, _):
        pack(k, send)
        launch(k)
        return 0

    def launch_step(k, _):
        launch(k)
        return 0

    def pack_step(k, _):
        pack(k, send)
        return 0

    batch = min(4, n)
    ahead = min(4 * batch, n)
    ready = min(9, n)
    lax.fori_loop(0, ready, pack_step, 0)
    pl.semaphore_wait(barrier, n - 1 + his)
    lax.fori_loop(1, ready, launch_step, 0)
    lax.fori_loop(ready, ahead, send_step, 0)
    lax.fori_loop(ahead, n, pack_step, 0)
    arr[me] = send[me]

    def dot_t(a, b):
        return lax.dot_general(a, b, (((1,), (1,)), ((), ())), preferred_element_type=F32)

    def dot(a, b):
        return jnp.dot(a, b, preferred_element_type=F32)

    def soft(s0, s1):
        top = jnp.maximum(
            jnp.max(s0, axis=1, keepdims=True), jnp.max(s1, axis=1, keepdims=True)
        )
        e0, e1 = jnp.exp(s0 - top), jnp.exp(s1 - top)
        total = jnp.sum(e0, axis=1, keepdims=True) + jnp.sum(e1, axis=1, keepdims=True)
        return (e0 / total).astype(BF16), (e1 / total).astype(BF16)

    wide = min(8, n)
    lane8 = lax.broadcasted_iota(jnp.int32, (8, HEAD), 1)
    step8 = lax.broadcasted_iota(jnp.int32, (8, HEAD), 0) % 2
    fresh8 = (lane8 == PAGE - 3) | ((lane8 == PAGE - 2) & (step8 == 1))

    def src_step(b, _):
        parts0, parts1 = [], []
        for i in range(wide):
            request = b * wide + i
            slot = tgts[request]
            query = qs[request].astype(BF16)
            bound = lens[request]
            s0 = dot_t(query, send[slot, 0, 0]) * scale
            s1 = dot_t(query, send[slot, 1, 0]) * scale
            parts0.append(jnp.where(lane8 < bound, s0, NEG))
            parts1.append(jnp.where((lane8 + PAGE < bound) | fresh8, s1, NEG))
        w0, w1 = soft(jnp.concatenate(parts0, axis=0), jnp.concatenate(parts1, axis=0))
        for i in range(wide):
            request = b * wide + i
            slot = tgts[request]
            rows = slice(8 * i, 8 * i + 8)
            mixed = dot(w0[rows], send[slot, 0, 1]) + dot(w1[rows], send[slot, 1, 1])
            for g in range(GROUPS):
                att_s[g, pl.ds(2 * request, 2), :] = mixed[2 * g : 2 * g + 2]
        return 0

    lax.fori_loop(0, n // wide, src_step, 0)

    def remote(src, dst, sems, index, target):
        return pltpu.make_async_remote_copy(
            src_ref=src,
            dst_ref=dst,
            send_sem=sems.at[2 * index],
            recv_sem=sems.at[2 * index + 1],
            device_id=(me, target),
            device_id_type=MESH,
        )

    def block_cols(index):
        return pl.ds(pl.multiple_of(index * cols, cols), cols)

    def ring_tail(att, half, half_in, pair, cross, cross_in, rs, rs_in, full):
        a = jnp.concatenate([att[g].astype(BF16) for g in range(GROUPS)], axis=1)
        part = cols // 2
        up, down = peer_hi(1), peer_hi(his - 1)

        def spot(step, side=None):
            start = (((hi + step) % his) * 2 + core) * cols
            if side is None:
                return full.at[:, :, pl.ds(pl.multiple_of(start, cols), cols)]
            return full.at[:, :, pl.ds(pl.multiple_of(start + side * part, part), part)]

        def mates(step):
            start = (((hi + step) % his) * 2 + 1 - core) * cols
            return full.at[:, :, pl.ds(pl.multiple_of(start, cols), cols)]

        swap = remote(half, half_in, half_sem, 0, mate)
        over = [
            remote(cross.at[0], cross_in.at[0], rs_sem, 0, up),
            remote(cross.at[1], cross_in.at[1], rs_sem, 1, down),
        ]
        near = [
            remote(rs.at[0], rs_in.at[0], rs_sem, 2, up),
            remote(rs.at[1], rs_in.at[1], rs_sem, 3, down),
        ]
        give = [remote(spot(0), spot(0), ag_sem, i, to) for i, to in enumerate((up, down))]
        take = [
            remote(spot(0), spot(step), ag_sem, i, to)
            for i, (step, to) in enumerate(((his - 1, up), (1, down)))
        ]
        pass_on = [
            remote(spot(step, side), spot(step, side), ag_sem, 2 + side, to)
            for side, (step, to) in enumerate(((his - 1, up), (1, down)))
        ]
        last_in = [
            remote(spot(0, side), spot(2, side), ag_sem, 2 + side, to)
            for side, to in enumerate((up, down))
        ]
        forward = [remote(spot(step), spot(step), fwd_sem, step, mate) for step in range(his)]
        received = [remote(spot(step), mates(step), fwd_sem, step, mate) for step in range(his)]

        def project():
            for step in range(his):
                z = (hi + step) % his
                half[step] = dot(a, w[:, block_cols(z * 2 + 1 - core)]).astype(BF16)
            swap.start()
            for step in range(his):
                z = (hi + step) % his
                pair[step] = dot(a, w[:, block_cols(z * 2 + core)])

        def far():
            swap.wait()
            for step in range(his):
                pair[step] = pair[step] + half_in[step].astype(F32)
            cross[0] = pair[2, :, :part].astype(BF16)
            cross[1] = pair[2, :, part:].astype(BF16)
            for copy in over:
                copy.start()

        def close():
            for copy in over:
                copy.wait()
            rs[0, :, :part] = (pair[1, :, :part] + cross_in[0].astype(F32)).astype(BF16)
            rs[0, :, part:] = pair[1, :, part:].astype(BF16)
            rs[1, :, :part] = pair[his - 1, :, :part].astype(BF16)
            rs[1, :, part:] = (pair[his - 1, :, part:] + cross_in[1].astype(F32)).astype(BF16)
            for copy in near:
                copy.start()

        def total():
            for copy in near:
                copy.wait()
            sums = pair[0] + rs_in[0].astype(F32) + rs_in[1].astype(F32)
            spot(0)[...] = sums.reshape(full.shape[:2] + (cols,)).astype(BF16)
            for copy in give:
                copy.start()
            forward[0].start()

        def relay():
            for side, step in enumerate((his - 1, 1)):
                take[side].wait_recv()
                pass_on[side].start()
                forward[step].start()

        def end():
            for copy in last_in:
                copy.wait_recv()
            forward[2].start()
            for copy in received:
                copy.wait_recv()
            for copy in give + pass_on + forward:
                copy.wait_send()

        return project, far, close, total, relay, end

    def tail(part, att, half, half_in, pair, rs, rs_in, full):
        a = jnp.concatenate([att[g].astype(BF16) for g in range(GROUPS)], axis=1)

        def part_full(index):
            where = block_cols(index)
            return full.at[:, where]

        swap = remote(half, half_in, half_sem, part, mate)
        scatter = [
            remote(rs.at[step], rs_in.at[step], rs_sem, part * his + step, peer_hi(step))
            for step in range(1, his)
        ]
        mine = part_full(tp)
        gather = [
            remote(mine, mine, ag_sem, part * his + step, peer_hi(step))
            for step in range(1, his)
        ]
        landed = [
            remote(
                mine,
                part_full(((hi + his - step) % his) * 2 + core),
                ag_sem,
                part * his + step,
                peer_hi(step),
            )
            for step in range(1, his)
        ]
        forward = []
        received = []
        for step in range(his):
            owner = ((hi + his - step) % his) * 2
            have, want = part_full(owner + core), part_full(owner + 1 - core)
            forward.append(remote(have, have, fwd_sem, part * his + step, mate))
            received.append(remote(have, want, fwd_sem, part * his + step, mate))

        def one():
            for step in range(his):
                z = (hi + step) % his
                half[step] = dot(a, w[:, block_cols(z * 2 + 1 - core)]).astype(BF16)
            swap.start()
            for step in range(his):
                z = (hi + step) % his
                pair[step] = dot(a, w[:, block_cols(z * 2 + core)])

        def two():
            swap.wait()
            for step in range(1, his):
                rs[step] = (pair[step] + half_in[step].astype(F32)).astype(BF16)
                scatter[step - 1].start()
            pair[0] = pair[0] + half_in[0].astype(F32)

        def three():
            for copy in scatter:
                copy.wait()
            total = pair[0]
            for step in range(1, his):
                total = total + rs_in[step].astype(F32)
            mine[...] = total.astype(BF16)
            for copy in gather:
                copy.start()
            forward[0].start()

        def four():
            for step in range(1, his):
                landed[step - 1].wait_recv()
                forward[step].start()
            for step in range(his):
                received[step].wait_recv()

        def five():
            for copy in gather:
                copy.wait_send()
            for copy in forward:
                copy.wait_send()

        return one, two, three, four, five

    load_w.wait()
    project, far, close, total_up, relay, end = ring_tail(
        att_s, s_half, s_half_in, s_pair, s_cross, s_cross_in, s_rs, s_rs_in, s_full
    )
    project()

    lane4 = lax.broadcasted_iota(jnp.int32, (GROUPS, HEAD), 1).astype(F32)

    def state(slot):
        length = arr[slot, 1, 0, PAGE - TILE :].astype(F32)[TILE - 1 :]
        flag = arr[slot, 1, 1, PAGE - TILE :].astype(F32)[TILE - 1 :]
        return length, flag == 1.0

    def attend_items(start, count):
        slots, parts0, parts1, values = [], [], [], []
        for i in range(count):
            k = start + i

            @pl.when(k > 0)
            def _():
                move(k).wait_send()

            @pl.when(k + ahead < n)
            def _():
                launch(k + ahead)

        for i in range(count):
            k = start + i

            @pl.when(k > 0)
            def _():
                arrive(k).wait_recv()

        for i in range(count):
            slot = partner(start + i)
            slots.append(slot)
            length, moved = state(slot)
            own = rdst[slot].astype(F32)
            key1 = jnp.where(last, own[0:1].astype(BF16), arr[slot, 1, 0])
            value1 = jnp.where(last, own[1:2].astype(BF16), arr[slot, 1, 1])
            query = qd[slot].astype(BF16)
            s0 = dot_t(query, arr[slot, 0, 0]) * scale
            s1 = dot_t(query, key1) * scale
            parts0.append(jnp.where(lane4 < length, s0, NEG))
            keep1 = (lane4 + float(PAGE) < length) | (lane4 >= PAGE - 3.0)
            parts1.append(jnp.where(keep1, s1, NEG))
            values.append((arr[slot, 0, 1], value1, moved))
        for i in range(count):
            w0, w1 = soft(parts0[i], parts1[i])
            mixed = dot(w0, values[i][0]) + dot(w1, values[i][1])
            mixed = jnp.where(values[i][2], mixed, 0.0)
            for g in range(GROUPS):
                att_d[g, pl.ds(slots[i], 1), :] = mixed[g : g + 1]

    def dst_step(b, _):
        attend_items(b * batch, batch)
        return 0

    def last_step(b, _):
        attend_items(b * 2 * batch, 2 * batch)
        return 0

    def fill_step(b, _):
        for i in range(batch):
            slot = partner(b * batch + i)
            length, moved = state(slot)
            length = jnp.where(moved, length, -512.0)
            own = rdst[slot].astype(F32)
            rows_in = [arr[slot, 1, c, PAGE - TILE :].astype(F32) for c in range(2)]
            for p in range(2):
                at = [(length + (j - p * PAGE)).astype(BF16) for j in range(3)]
                keep = row < at[0]
                hits = [row == spot for spot in at]
                for c in range(2):
                    rows_put = [
                        rows_in[c][TILE - 3 : TILE - 2],
                        rows_in[c][TILE - 2 : TILE - 1],
                        own[c : c + 1],
                    ]
                    block = jnp.where(keep, arr[slot, p, c], zero)
                    for hit, put in zip(hits, rows_put):
                        block = jnp.where(hit, put.astype(BF16), block)
                    cache_out[slot, p, c] = block
        return 0

    def both(b, _):
        dst_step(b, 0)
        return fill_step(b, 0)

    steps = n // batch
    marks = [steps * j // 8 for j in (0, 1, 3, 5, 6, 7, 8)]
    lax.fori_loop(marks[0], marks[1], both, 0)
    far()
    lax.fori_loop(marks[1], marks[2], both, 0)
    close()
    lax.fori_loop(marks[2], marks[3], both, 0)
    total_up()
    lax.fori_loop(marks[3], marks[4], both, 0)
    lax.fori_loop(marks[4] // 2, marks[6] // 2, last_step, 0)

    dst_tail = tail(1, att_d, d_half, d_half_in, d_pair, d_rs, d_rs_in, d_full)
    dst_tail[0]()
    relay()
    dst_tail[1]()
    lax.fori_loop(marks[4], marks[5], fill_step, 0)
    dst_tail[2]()
    lax.fori_loop(marks[5], marks[6], fill_step, 0)
    dst_tail[3]()
    end()
    dst_tail[4]()


def place(src_in, cache_in, dst_in, src_hbm, cache_hbm, dst_hbm, sem):
    size = cache_in.shape[0] // PIECES
    copies = [
        pltpu.make_async_copy(
            cache_in.at[i * size : (i + 1) * size],
            cache_hbm.at[i * size : (i + 1) * size],
            sem.at[i],
        )
        for i in range(PIECES)
    ]
    copies.append(pltpu.make_async_copy(src_in, src_hbm, sem.at[PIECES]))
    copies.append(pltpu.make_async_copy(dst_in, dst_hbm, sem.at[PIECES + 1]))
    for copy in copies:
        copy.start()
    for copy in copies:
        copy.wait()


def shards(
    pool,
    page_table,
    lengths,
    targets,
    migrating,
    queries_src,
    new_rows,
    queries_dst,
    rows_dst,
    w_out,
):
    n = lax.axis_size("inst")
    tp_size = lax.axis_size("tp")
    his = tp_size // 2
    requests = queries_src.shape[0]
    width = w_out.shape[1]
    cols = width // tp_size
    smem = pl.BlockSpec(memory_space=pltpu.SMEM)
    vmem = pl.BlockSpec(memory_space=pltpu.VMEM)
    hbm = pl.BlockSpec(memory_space=pl.ANY)
    cache = (requests, 2, 2, PAGE, HEAD)

    def sums(rows, sent):
        return [
            pltpu.VMEM((his, rows, cols), BF16),
            pltpu.VMEM((his, rows, cols), BF16),
            pltpu.VMEM((his, rows, cols), F32),
        ] + [pltpu.VMEM((parts, rows, width), BF16) for parts, width in sent]

    dma = pltpu.SemaphoreType.DMA
    in_hbm = functools.partial(pltpu.with_memory_space_constraint, memory_space=pltpu.HBM)
    results = pl.pallas_call(
        functools.partial(kernel, n, tp_size),
        out_shape=(
            pltpu.VMEM((requests, 2, width), BF16),
            pltpu.VMEM(cache, BF16),
            pltpu.VMEM((requests, width), BF16),
        ),
        in_specs=[smem] * 4 + [hbm] * 6,
        out_specs=(vmem, vmem, vmem),
        scratch_shapes=[
            pltpu.VMEM(queries_src.shape, BF16),
            pltpu.VMEM(new_rows.shape, BF16),
            pltpu.VMEM(queries_dst.shape, BF16),
            pltpu.VMEM(rows_dst.shape, BF16),
            pltpu.VMEM(pool.shape, BF16),
            pltpu.VMEM(w_out.shape, BF16),
            pltpu.VMEM(cache, BF16),
            pltpu.VMEM(cache, BF16),
            pltpu.VMEM((requests, 2 * GROUPS, HEAD), F32),
            pltpu.VMEM((requests, GROUPS, HEAD), F32),
            pltpu.VMEM((GROUPS, 2 * requests, HEAD), F32),
            pltpu.VMEM((GROUPS, requests, HEAD), F32),
        ]
        + sums(2 * requests, [(2, cols // 2)] * 2 + [(2, cols)] * 2)
        + sums(requests, [(his, cols)] * 2)
        + [
            dma((6,)),
            dma((n,)),
            dma((n,)),
            dma((4,)),
            dma((4 * his,)),
            dma((4 * his,)),
            dma((4 * his,)),
        ],
        compiler_params=pltpu.CompilerParams(
            collective_id=0, has_side_effects=True, vmem_limit_bytes=28 * 1024 * 1024
        ),
        name="migrate",
    )(
        *map(
            in_hbm,
            (
                lengths,
                targets,
                migrating,
                page_table.T,
                queries_src,
                new_rows,
                queries_dst,
                rows_dst,
                pool,
                w_out,
            ),
        )
    )
    return pl.pallas_call(
        place,
        out_shape=tuple(pltpu.HBM(x.shape, x.dtype) for x in results),
        in_specs=[vmem] * 3,
        out_specs=(hbm,) * 3,
        scratch_shapes=[dma((PIECES + 2,))],
        compiler_params=pltpu.CompilerParams(vmem_limit_bytes=8 * 1024 * 1024),
        name="place",
    )(*(pltpu.with_memory_space_constraint(x, pltpu.VMEM) for x in results))


def solution(mesh):
    return jax.shard_map(
        shards,
        mesh=mesh,
        in_specs=(
            P("inst", None, None, "tp"),
            P("inst", None),
            P("inst"),
            P("inst"),
            P("inst"),
            P("inst", None, "tp"),
            P("inst", None, None, "tp"),
            P("inst", "tp"),
            P("inst", None, "tp"),
            P("tp", None),
        ),
        out_specs=(P("inst", None, None), P("inst", None, None, None, "tp"), P("inst", None)),
        check_vma=False,
    )
```

```python
import functools
import math

import jax
import jax.numpy as jnp
from jax import lax
from jax.experimental import pallas as pl
from jax.experimental.pallas import tpu as pltpu
from jax.sharding import PartitionSpec as P

MESH = pl.DeviceIdType.MESH
BF16 = jnp.bfloat16
F32 = jnp.float32
NEG = -1e30
HEAD = 128
PAGE = 128
GROUPS = 4
TILE = 16
PIECES = 8
SWAPS = ((1, 21), (2, 20), (24, 18))
MIX = 11


def xor(a, b, bits):
    total = 0
    for bit in range(bits):
        weight = 2**bit
        u, v = (a // weight) % 2, (b // weight) % 2
        total = total + (u + v - 2 * u * v) * weight
    return total


def same(a, b):
    return 1 - ((a - b) * (a - b) + 1023) // 1024


def order(k, n):
    if n != 32:
        return (k * MIX) % n
    late = k // 16
    spot = (k - 16 * late) % 8
    turn = (k - 16 * late) // 8
    hop0 = (k % 3 + 1) // 2
    hop1 = 1 - (spot % 3 + 1) // 2
    hop = (1 - late) * hop0 + late * hop1
    cross0 = k - k // 3 - 1
    cross1 = 10 + 3 * turn + spot // 3
    plane0 = k // 3
    plane1 = 6 + 5 * turn + spot - spot // 3 - 1
    count = hop * ((1 - late) * cross0 + late * cross1)
    count = count + (1 - hop) * ((1 - late) * plane0 + late * plane1)
    peer = ((count * MIX) % 16) * 2 + hop
    for one, other in SWAPS:
        peer = peer + (same(peer, one) - same(peer, other)) * (other - one)
    return peer


def kernel(
    n,
    tp_size,
    lens,
    tgts,
    mig,
    table,
    qsrc_hbm,
    fresh_hbm,
    qdst_hbm,
    rdst_hbm,
    pool_hbm,
    w_hbm,
    s_full,
    cache_out,
    d_full,
    qsrc,
    fresh,
    qdst,
    rdst,
    pool,
    w,
    send,
    arr,
    qs,
    qd,
    att_s,
    att_d,
    s_half,
    s_half_in,
    s_pair,
    s_cross,
    s_cross_in,
    s_rs,
    s_rs_in,
    d_half,
    d_half_in,
    d_pair,
    d_rs,
    d_rs_in,
    load_sem,
    send_sem,
    recv_sem,
    half_sem,
    rs_sem,
    ag_sem,
    fwd_sem,
):
    me = lax.axis_index("inst")
    tp = lax.axis_index("tp")
    core = tp % 2
    hi = tp // 2
    his = tp_size // 2
    mate = tp + 1 - 2 * core
    bits = n.bit_length() - 1
    scale = 1.0 / math.sqrt(HEAD)
    cols = w.shape[1] // tp_size

    def peer_hi(step):
        return ((hi + step) % his) * 2 + core

    def partner(k):
        return xor(me, order(k, n), bits)

    load_pool = pltpu.make_async_copy(pool_hbm, pool, load_sem.at[0])
    load_w = pltpu.make_async_copy(w_hbm, w, load_sem.at[1])
    small = [
        pltpu.make_async_copy(src, dst, load_sem.at[2 + i])
        for i, (src, dst) in enumerate(
            ((fresh_hbm, fresh), (qsrc_hbm, qsrc), (qdst_hbm, qdst), (rdst_hbm, rdst))
        )
    ]
    load_pool.start()
    for copy in small:
        copy.start()
    barrier = pltpu.get_barrier_semaphore()

    def greet(k, _):
        pl.semaphore_signal(
            barrier, inc=1, device_id=(xor(me, k, bits), tp), device_id_type=MESH
        )
        return 0

    lax.fori_loop(1, n, greet, 0)
    pl.semaphore_signal(barrier, inc=1, device_id=(me, mate), device_id_type=MESH)
    for step in range(1, his):
        pl.semaphore_signal(barrier, inc=1, device_id=(me, peer_hi(step)), device_id_type=MESH)

    row = lax.broadcasted_iota(jnp.int32, (PAGE, HEAD), 0).astype(F32).astype(BF16)
    last = row == jnp.asarray(PAGE - 1, BF16)
    zero = jnp.zeros((PAGE, HEAD), BF16)
    tile_row = lax.broadcasted_iota(jnp.int32, (TILE, HEAD), 0).astype(F32)

    def move(k):
        peer = partner(k)
        return pltpu.make_async_remote_copy(
            src_ref=send.at[peer],
            dst_ref=arr.at[me],
            send_sem=send_sem.at[k],
            recv_sem=recv_sem.at[k],
            device_id=(peer, tp),
            device_id_type=MESH,
        )

    def launch(k):
        peer = partner(k)
        for p in range(2):
            for c in range(2):
                pltpu.make_async_remote_copy(
                    src_ref=send.at[peer, p, c],
                    dst_ref=arr.at[me, p, c],
                    send_sem=send_sem.at[k],
                    recv_sem=recv_sem.at[k],
                    device_id=(peer, tp),
                    device_id_type=MESH,
                ).start()

    def arrive(k):
        peer = partner(k)
        return pltpu.make_async_remote_copy(
            src_ref=send.at[peer],
            dst_ref=arr.at[peer],
            send_sem=send_sem.at[k],
            recv_sem=recv_sem.at[k],
            device_id=(peer, tp),
            device_id_type=MESH,
        )

    def pack(k, ref):
        slot = partner(k)
        request = jnp.int32(0)
        for j in range(n):
            request = jnp.where(tgts[j] == slot, j, request)
        length = lens[request].astype(F32)
        flag = mig[request].astype(F32)
        rows_new = fresh[request].astype(F32)
        for c in range(2):
            ref[slot, 0, c] = pool[table[0, request], c]
            page = pool[table[1, request], c]
            ref[slot, 1, c, : PAGE - TILE] = page[: PAGE - TILE]
            end = jnp.where(tile_row == TILE - 3.0, rows_new[0, c : c + 1], page[PAGE - TILE :].astype(F32))
            end = jnp.where(tile_row == TILE - 2.0, rows_new[1, c : c + 1], end)
            end = jnp.where(tile_row == TILE - 1.0, length if c == 0 else flag, end)
            ref[slot, 1, c, PAGE - TILE :] = end.astype(BF16)

    for copy in small:
        copy.wait()
    q_wide = qsrc[...].astype(F32)
    for g in range(GROUPS):
        lanes = slice(g * HEAD, (g + 1) * HEAD)
        for t in range(2):
            qs[:, 2 * g + t, :] = q_wide[:, t, lanes]
        qd[:, g, :] = qdst[:, lanes].astype(F32)

    load_pool.wait()
    load_w.start()

    def send_step(k, _):
        pack(k, send)
        launch(k)
        return 0

    def launch_step(k, _):
        launch(k)
        return 0

    def pack_step(k, _):
        pack(k, send)
        return 0

    batch = min(4, n)
    ahead = min(4 * batch, n)
    ready = min(9, n)
    lax.fori_loop(0, ready, pack_step, 0)
    pl.semaphore_wait(barrier, n - 1 + his)
    lax.fori_loop(1, ready, launch_step, 0)
    lax.fori_loop(ready, ahead, send_step, 0)
    lax.fori_loop(ahead, n, pack_step, 0)
    arr[me] = send[me]

    def dot_t(a, b):
        return lax.dot_general(a, b, (((1,), (1,)), ((), ())), preferred_element_type=F32)

    def dot(a, b):
        return jnp.dot(a, b, preferred_element_type=F32)

    def soft(s0, s1):
        top = jnp.maximum(
            jnp.max(s0, axis=1, keepdims=True), jnp.max(s1, axis=1, keepdims=True)
        )
        e0, e1 = jnp.exp(s0 - top), jnp.exp(s1 - top)
        total = jnp.sum(e0, axis=1, keepdims=True) + jnp.sum(e1, axis=1, keepdims=True)
        return (e0 / total).astype(BF16), (e1 / total).astype(BF16)

    wide = min(8, n)
    lane8 = lax.broadcasted_iota(jnp.int32, (8, HEAD), 1)
    step8 = lax.broadcasted_iota(jnp.int32, (8, HEAD), 0) % 2
    fresh8 = (lane8 == PAGE - 3) | ((lane8 == PAGE - 2) & (step8 == 1))

    def src_step(b, _):
        parts0, parts1 = [], []
        for i in range(wide):
            request = b * wide + i
            slot = tgts[request]
            query = qs[request].astype(BF16)
            bound = lens[request]
            s0 = dot_t(query, send[slot, 0, 0]) * scale
            s1 = dot_t(query, send[slot, 1, 0]) * scale
            parts0.append(jnp.where(lane8 < bound, s0, NEG))
            parts1.append(jnp.where((lane8 + PAGE < bound) | fresh8, s1, NEG))
        w0, w1 = soft(jnp.concatenate(parts0, axis=0), jnp.concatenate(parts1, axis=0))
        for i in range(wide):
            request = b * wide + i
            slot = tgts[request]
            rows = slice(8 * i, 8 * i + 8)
            mixed = dot(w0[rows], send[slot, 0, 1]) + dot(w1[rows], send[slot, 1, 1])
            for g in range(GROUPS):
                att_s[g, pl.ds(2 * request, 2), :] = mixed[2 * g : 2 * g + 2]
        return 0

    lax.fori_loop(0, n // wide, src_step, 0)

    def remote(src, dst, sems, index, target):
        return pltpu.make_async_remote_copy(
            src_ref=src,
            dst_ref=dst,
            send_sem=sems.at[2 * index],
            recv_sem=sems.at[2 * index + 1],
            device_id=(me, target),
            device_id_type=MESH,
        )

    def block_cols(index):
        return pl.ds(pl.multiple_of(index * cols, cols), cols)

    def ring_tail(att, half, half_in, pair, cross, cross_in, rs, rs_in, full):
        a = jnp.concatenate([att[g].astype(BF16) for g in range(GROUPS)], axis=1)
        part = cols // 2
        up, down = peer_hi(1), peer_hi(his - 1)

        def spot(step, side=None):
            start = (((hi + step) % his) * 2 + core) * cols
            if side is None:
                return full.at[:, :, pl.ds(pl.multiple_of(start, cols), cols)]
            return full.at[:, :, pl.ds(pl.multiple_of(start + side * part, part), part)]

        def mates(step):
            start = (((hi + step) % his) * 2 + 1 - core) * cols
            return full.at[:, :, pl.ds(pl.multiple_of(start, cols), cols)]

        swap = remote(half, half_in, half_sem, 0, mate)
        over = [
            remote(cross.at[0], cross_in.at[0], rs_sem, 0, up),
            remote(cross.at[1], cross_in.at[1], rs_sem, 1, down),
        ]
        near = [
            remote(rs.at[0], rs_in.at[0], rs_sem, 2, up),
            remote(rs.at[1], rs_in.at[1], rs_sem, 3, down),
        ]
        give = [remote(spot(0), spot(0), ag_sem, i, to) for i, to in enumerate((up, down))]
        take = [
            remote(spot(0), spot(step), ag_sem, i, to)
            for i, (step, to) in enumerate(((his - 1, up), (1, down)))
        ]
        pass_on = [
            remote(spot(step, side), spot(step, side), ag_sem, 2 + side, to)
            for side, (step, to) in enumerate(((his - 1, up), (1, down)))
        ]
        last_in = [
            remote(spot(0, side), spot(2, side), ag_sem, 2 + side, to)
            for side, to in enumerate((up, down))
        ]
        forward = [remote(spot(step), spot(step), fwd_sem, step, mate) for step in range(his)]
        received = [remote(spot(step), mates(step), fwd_sem, step, mate) for step in range(his)]

        def project():
            for step in range(his):
                z = (hi + step) % his
                half[step] = dot(a, w[:, block_cols(z * 2 + 1 - core)]).astype(BF16)
            swap.start()
            for step in range(his):
                z = (hi + step) % his
                pair[step] = dot(a, w[:, block_cols(z * 2 + core)])

        def far():
            swap.wait()
            for step in range(his):
                pair[step] = pair[step] + half_in[step].astype(F32)
            cross[0] = pair[2, :, :part].astype(BF16)
            cross[1] = pair[2, :, part:].astype(BF16)
            for copy in over:
                copy.start()

        def close():
            for copy in over:
                copy.wait()
            rs[0, :, :part] = (pair[1, :, :part] + cross_in[0].astype(F32)).astype(BF16)
            rs[0, :, part:] = pair[1, :, part:].astype(BF16)
            rs[1, :, :part] = pair[his - 1, :, :part].astype(BF16)
            rs[1, :, part:] = (pair[his - 1, :, part:] + cross_in[1].astype(F32)).astype(BF16)
            for copy in near:
                copy.start()

        def total():
            for copy in near:
                copy.wait()
            sums = pair[0] + rs_in[0].astype(F32) + rs_in[1].astype(F32)
            spot(0)[...] = sums.reshape(full.shape[:2] + (cols,)).astype(BF16)
            for copy in give:
                copy.start()
            forward[0].start()

        def relay():
            for side, step in enumerate((his - 1, 1)):
                take[side].wait_recv()
                pass_on[side].start()
                forward[step].start()

        def end():
            for copy in last_in:
                copy.wait_recv()
            forward[2].start()
            for copy in received:
                copy.wait_recv()
            for copy in give + pass_on + forward:
                copy.wait_send()

        return project, far, close, total, relay, end

    def tail(part, att, half, half_in, pair, rs, rs_in, full):
        a = jnp.concatenate([att[g].astype(BF16) for g in range(GROUPS)], axis=1)

        def part_full(index):
            where = block_cols(index)
            return full.at[:, where]

        swap = remote(half, half_in, half_sem, part, mate)
        scatter = [
            remote(rs.at[step], rs_in.at[step], rs_sem, part * his + step, peer_hi(step))
            for step in range(1, his)
        ]
        mine = part_full(tp)
        gather = [
            remote(mine, mine, ag_sem, part * his + step, peer_hi(step))
            for step in range(1, his)
        ]
        landed = [
            remote(
                mine,
                part_full(((hi + his - step) % his) * 2 + core),
                ag_sem,
                part * his + step,
                peer_hi(step),
            )
            for step in range(1, his)
        ]
        forward = []
        received = []
        for step in range(his):
            owner = ((hi + his - step) % his) * 2
            have, want = part_full(owner + core), part_full(owner + 1 - core)
            forward.append(remote(have, have, fwd_sem, part * his + step, mate))
            received.append(remote(have, want, fwd_sem, part * his + step, mate))

        def one():
            for step in range(his):
                z = (hi + step) % his
                half[step] = dot(a, w[:, block_cols(z * 2 + 1 - core)]).astype(BF16)
            swap.start()
            for step in range(his):
                z = (hi + step) % his
                pair[step] = dot(a, w[:, block_cols(z * 2 + core)])

        def two():
            swap.wait()
            for step in range(1, his):
                rs[step] = (pair[step] + half_in[step].astype(F32)).astype(BF16)
                scatter[step - 1].start()
            pair[0] = pair[0] + half_in[0].astype(F32)

        def three():
            for copy in scatter:
                copy.wait()
            total = pair[0]
            for step in range(1, his):
                total = total + rs_in[step].astype(F32)
            mine[...] = total.astype(BF16)
            for copy in gather:
                copy.start()
            forward[0].start()

        def four():
            for step in range(1, his):
                landed[step - 1].wait_recv()
                forward[step].start()
            for step in range(his):
                received[step].wait_recv()

        def five():
            for copy in gather:
                copy.wait_send()
            for copy in forward:
                copy.wait_send()

        return one, two, three, four, five

    load_w.wait()
    project, far, close, total_up, relay, end = ring_tail(
        att_s, s_half, s_half_in, s_pair, s_cross, s_cross_in, s_rs, s_rs_in, s_full
    )
    project()

    lane4 = lax.broadcasted_iota(jnp.int32, (GROUPS, HEAD), 1).astype(F32)

    def state(slot):
        length = arr[slot, 1, 0, PAGE - TILE :].astype(F32)[TILE - 1 :]
        flag = arr[slot, 1, 1, PAGE - TILE :].astype(F32)[TILE - 1 :]
        return length, flag == 1.0

    def attend_items(start, count):
        slots, parts0, parts1, values = [], [], [], []
        for i in range(count):
            k = start + i

            @pl.when(k > 0)
            def _():
                move(k).wait_send()

            @pl.when(k + ahead < n)
            def _():
                launch(k + ahead)

        for i in range(count):
            k = start + i

            @pl.when(k > 0)
            def _():
                arrive(k).wait_recv()

        for i in range(count):
            slot = partner(start + i)
            slots.append(slot)
            length, moved = state(slot)
            own = rdst[slot].astype(F32)
            key1 = jnp.where(last, own[0:1].astype(BF16), arr[slot, 1, 0])
            value1 = jnp.where(last, own[1:2].astype(BF16), arr[slot, 1, 1])
            query = qd[slot].astype(BF16)
            s0 = dot_t(query, arr[slot, 0, 0]) * scale
            s1 = dot_t(query, key1) * scale
            parts0.append(jnp.where(lane4 < length, s0, NEG))
            keep1 = (lane4 + float(PAGE) < length) | (lane4 >= PAGE - 3.0)
            parts1.append(jnp.where(keep1, s1, NEG))
            values.append((arr[slot, 0, 1], value1, moved))
        for i in range(count):
            w0, w1 = soft(parts0[i], parts1[i])
            mixed = dot(w0, values[i][0]) + dot(w1, values[i][1])
            mixed = jnp.where(values[i][2], mixed, 0.0)
            for g in range(GROUPS):
                att_d[g, pl.ds(slots[i], 1), :] = mixed[g : g + 1]

    def dst_step(b, _):
        attend_items(b * batch, batch)
        return 0

    def last_step(b, _):
        attend_items(b * 2 * batch, 2 * batch)
        return 0

    def fill_step(b, _):
        for i in range(batch):
            slot = partner(b * batch + i)
            length, moved = state(slot)
            length = jnp.where(moved, length, -512.0)
            own = rdst[slot].astype(F32)
            rows_in = [arr[slot, 1, c, PAGE - TILE :].astype(F32) for c in range(2)]
            for p in range(2):
                at = [(length + (j - p * PAGE)).astype(BF16) for j in range(3)]
                keep = row < at[0]
                hits = [row == spot for spot in at]
                for c in range(2):
                    rows_put = [
                        rows_in[c][TILE - 3 : TILE - 2],
                        rows_in[c][TILE - 2 : TILE - 1],
                        own[c : c + 1],
                    ]
                    block = jnp.where(keep, arr[slot, p, c], zero)
                    for hit, put in zip(hits, rows_put):
                        block = jnp.where(hit, put.astype(BF16), block)
                    cache_out[slot, p, c] = block
        return 0

    def both(b, _):
        dst_step(b, 0)
        return fill_step(b, 0)

    steps = n // batch
    marks = [steps * j // 8 for j in (0, 1, 3, 5, 6, 7, 8)]
    lax.fori_loop(marks[0], marks[1], both, 0)
    far()
    lax.fori_loop(marks[1], marks[2], both, 0)
    close()
    lax.fori_loop(marks[2], marks[3], both, 0)
    total_up()
    lax.fori_loop(marks[3], marks[4], both, 0)
    lax.fori_loop(marks[4] // 2, marks[6] // 2, last_step, 0)

    dst_tail = tail(1, att_d, d_half, d_half_in, d_pair, d_rs, d_rs_in, d_full)
    dst_tail[0]()
    relay()
    dst_tail[1]()
    lax.fori_loop(marks[4], marks[5], fill_step, 0)
    dst_tail[2]()
    lax.fori_loop(marks[5], marks[6], fill_step, 0)
    dst_tail[3]()
    end()
    dst_tail[4]()


def place(src_in, cache_in, dst_in, src_hbm, cache_hbm, dst_hbm, sem):
    size = cache_in.shape[0] // PIECES
    copies = [
        pltpu.make_async_copy(
            cache_in.at[i * size : (i + 1) * size],
            cache_hbm.at[i * size : (i + 1) * size],
            sem.at[i],
        )
        for i in range(PIECES)
    ]
    copies.append(pltpu.make_async_copy(src_in, src_hbm, sem.at[PIECES]))
    copies.append(pltpu.make_async_copy(dst_in, dst_hbm, sem.at[PIECES + 1]))
    for copy in copies:
        copy.start()
    for copy in copies:
        copy.wait()


def shards(
    pool,
    page_table,
    lengths,
    targets,
    migrating,
    queries_src,
    new_rows,
    queries_dst,
    rows_dst,
    w_out,
):
    n = lax.axis_size("inst")
    tp_size = lax.axis_size("tp")
    his = tp_size // 2
    requests = queries_src.shape[0]
    width = w_out.shape[1]
    cols = width // tp_size
    smem = pl.BlockSpec(memory_space=pltpu.SMEM)
    vmem = pl.BlockSpec(memory_space=pltpu.VMEM)
    hbm = pl.BlockSpec(memory_space=pl.ANY)
    cache = (requests, 2, 2, PAGE, HEAD)

    def sums(rows, sent):
        return [
            pltpu.VMEM((his, rows, cols), BF16),
            pltpu.VMEM((his, rows, cols), BF16),
            pltpu.VMEM((his, rows, cols), F32),
        ] + [pltpu.VMEM((parts, rows, width), BF16) for parts, width in sent]

    dma = pltpu.SemaphoreType.DMA
    in_hbm = functools.partial(pltpu.with_memory_space_constraint, memory_space=pltpu.HBM)
    results = pl.pallas_call(
        functools.partial(kernel, n, tp_size),
        out_shape=(
            pltpu.VMEM((requests, 2, width), BF16),
            pltpu.VMEM(cache, BF16),
            pltpu.VMEM((requests, width), BF16),
        ),
        in_specs=[smem] * 4 + [hbm] * 6,
        out_specs=(vmem, vmem, vmem),
        scratch_shapes=[
            pltpu.VMEM(queries_src.shape, BF16),
            pltpu.VMEM(new_rows.shape, BF16),
            pltpu.VMEM(queries_dst.shape, BF16),
            pltpu.VMEM(rows_dst.shape, BF16),
            pltpu.VMEM(pool.shape, BF16),
            pltpu.VMEM(w_out.shape, BF16),
            pltpu.VMEM(cache, BF16),
            pltpu.VMEM(cache, BF16),
            pltpu.VMEM((requests, 2 * GROUPS, HEAD), F32),
            pltpu.VMEM((requests, GROUPS, HEAD), F32),
            pltpu.VMEM((GROUPS, 2 * requests, HEAD), F32),
            pltpu.VMEM((GROUPS, requests, HEAD), F32),
        ]
        + sums(2 * requests, [(2, cols // 2)] * 2 + [(2, cols)] * 2)
        + sums(requests, [(his, cols)] * 2)
        + [
            dma((6,)),
            dma((n,)),
            dma((n,)),
            dma((4,)),
            dma((4 * his,)),
            dma((4 * his,)),
            dma((4 * his,)),
        ],
        compiler_params=pltpu.CompilerParams(
            collective_id=0, has_side_effects=True, vmem_limit_bytes=28 * 1024 * 1024
        ),
        name="migrate",
    )(
        *map(
            in_hbm,
            (
                lengths,
                targets,
                migrating,
                page_table.T,
                queries_src,
                new_rows,
                queries_dst,
                rows_dst,
                pool,
                w_out,
            ),
        )
    )
    return pl.pallas_call(
        place,
        out_shape=tuple(pltpu.HBM(x.shape, x.dtype) for x in results),
        in_specs=[vmem] * 3,
        out_specs=(hbm,) * 3,
        scratch_shapes=[dma((PIECES + 2,))],
        compiler_params=pltpu.CompilerParams(vmem_limit_bytes=8 * 1024 * 1024),
        name="place",
    )(*(pltpu.with_memory_space_constraint(x, pltpu.VMEM) for x in results))


def solution(mesh):
    return jax.shard_map(
        shards,
        mesh=mesh,
        in_specs=(
            P("inst", None, None, "tp"),
            P("inst", None),
            P("inst"),
            P("inst"),
            P("inst"),
            P("inst", None, "tp"),
            P("inst", None, None, "tp"),
            P("inst", "tp"),
            P("inst", None, "tp"),
            P("tp", None),
        ),
        out_specs=(P("inst", None, None), P("inst", None, None, None, "tp"), P("inst", None)),
        check_vma=False,
    )
```
